32 devices in a mesh: dp: 8 (over y, x, core), tensor: 4 (over z).
Axes of the slice: x: 2, y: 2, z: 4, core: 2. Of those that a mesh axis runs over, the one named last changes fastest.
Arguments:
- tokens: bfloat16 [16384, 1024], P(('dp', 'tensor')), may hold values from -6 to 6
- encoded: bfloat16 [8192, 1024], P(('dp', 'tensor')), may hold values from -6 to 6
- parents: int32 [8, 16], P('dp'), may hold values from 0 to 14, as said below
- source_lengths: int32 [8], P('dp'), may hold values from 769 to 1024, as said below
- cotangent: bfloat16 [16384, 1024], P(('dp', 'tensor')), may hold values from -6 to 6
- first_gain: float32 [1024], replicated, may hold values from 0.5 to 1.5
- first_shift: float32 [1024], replicated, may hold values from -1.25 to 1.25
- self_query: bfloat16 [1024, 1024], P('dp', 'tensor'), may hold values from -0.1875 to 0.1875
- self_query_bias: float32 [1024], P('tensor'), may hold values from -1.75 to 1.75
- self_key: bfloat16 [1024, 1024], P('dp', 'tensor'), may hold values from -0.1875 to 0.1875
- self_value: bfloat16 [1024, 1024], P('dp', 'tensor'), may hold values from -0.1875 to 0.1875
- self_value_bias: float32 [1024], P('tensor'), may hold values from -1.75 to 1.75
- self_out: bfloat16 [1024, 1024], P('tensor', 'dp'), may hold values from -0.5 to 0.5
- self_out_bias: float32 [1024], replicated, may hold values from -1.75 to 1.75
- second_gain: float32 [1024], replicated, may hold values from 0.5 to 1.5
- second_shift: float32 [1024], replicated, may hold values from -1.25 to 1.25
- cross_query: bfloat16 [1024, 1024], P('dp', 'tensor'), may hold values from -0.1875 to 0.1875
- cross_query_bias: float32 [1024], P('tensor'), may hold values from -1.75 to 1.75
- cross_key: bfloat16 [1024, 1024], P('dp', 'tensor'), may hold values from -0.1875 to 0.1875
- cross_value: bfloat16 [1024, 1024], P('dp', 'tensor'), may hold values from -0.1875 to 0.1875
- cross_value_bias: float32 [1024], P('tensor'), may hold values from -1.75 to 1.75
- cross_out: bfloat16 [1024, 1024], P('tensor', 'dp'), may hold values from -0.5 to 0.5
- cross_out_bias: float32 [1024], replicated, may hold values from -1.75 to 1.75
- third_gain: float32 [1024], replicated, may hold values from 0.5 to 1.5
- third_shift: float32 [1024], replicated, may hold values from -1.25 to 1.25
- up_weight: bfloat16 [1024, 8192], P('dp', 'tensor'), may hold values from -0.1875 to 0.1875
- up_bias: float32 [8192], P('tensor'), may hold values from -3 to 3
- down_weight: bfloat16 [8192, 1024], P('tensor', 'dp'), may hold values from -0.0625 to 0.0625
- down_bias: float32 [1024], replicated, may hold values from -1.75 to 1.75
Outputs:
- block_out: bfloat16 [16384, 1024], P(('dp', 'tensor'))
- tokens_grad: float32 [16384, 1024], P(('dp', 'tensor'))
- encoded_grad: float32 [8192, 1024], P(('dp', 'tensor'))
- first_gain_grad: float32 [1024], replicated
- first_shift_grad: float32 [1024], replicated
- self_query_grad: float32 [1024, 1024], P('dp', 'tensor')
- self_query_bias_grad: float32 [1024], P('tensor')
- self_key_grad: float32 [1024, 1024], P('dp', 'tensor')
- self_value_grad: float32 [1024, 1024], P('dp', 'tensor')
- self_value_bias_grad: float32 [1024], P('tensor')
- self_out_grad: float32 [1024, 1024], P('tensor', 'dp')
- self_out_bias_grad: float32 [1024], replicated
- second_gain_grad: float32 [1024], replicated
- second_shift_grad: float32 [1024], replicated
- cross_query_grad: float32 [1024, 1024], P('dp', 'tensor')
- cross_query_bias_grad: float32 [1024], P('tensor')
- cross_key_grad: float32 [1024, 1024], P('dp', 'tensor')
- cross_value_grad: float32 [1024, 1024], P('dp', 'tensor')
- cross_value_bias_grad: float32 [1024], P('tensor')
- cross_out_grad: float32 [1024, 1024], P('tensor', 'dp')
- cross_out_bias_grad: float32 [1024], replicated
- third_gain_grad: float32 [1024], replicated
- third_shift_grad: float32 [1024], replicated
- up_weight_grad: float32 [1024, 8192], P('dp', 'tensor')
- up_bias_grad: float32 [8192], P('tensor')
- down_weight_grad: float32 [8192, 1024], P('tensor', 'dp')
- down_bias_grad: float32 [1024], replicated
The draws below stay inside these ranges and needn't reach their ends.
Inputs may be any that keep to these rules, and one draw needn't show every extreme that they name: `parents`: for segment s of a tree, the parent segment on its path to the root: 0 for segments 0 and 1, else s - 1 or s - 2. `source_lengths`: some tree has all 1024 encoder states.
All inputs are finite; a program needn't handle non-finite values.
Results may differ from the reference program's by a relative error of at most 0.025.
Values may be sent and summed in bfloat16 or wider, within the bound.
No kernel may reach another device: no remote copies, remote signals or barrier semaphores. Data moves between devices by JAX's collectives and lax.ppermute only.
A program may use at most 192 MiB of HBM per device.

```python
import jax
import jax.numpy as jnp
from jax import lax

D = 1024
HEAD_DIM = 64
FF = 8192
SEG = 128
SOURCE = 1024
TREE_LEN = 2048
SEGMENTS = 16
TREES = 8
TOKENS = 16384
SOURCES = 8192


def draw_parents(key, part):
    key = jax.random.fold_in(key, 11)
    backward = jax.random.randint(key, (TREES, SEGMENTS), 1, 3)
    places = jnp.arange(SEGMENTS)
    chosen = jnp.maximum(places[None, :] - backward, 0)
    chosen = chosen.at[0, SEGMENTS - 1].set(SEGMENTS - 2)
    return chosen.astype(jnp.int32)


def draw_source_lengths(key, part):
    key = jax.random.fold_in(key, 23)
    lengths = jax.random.randint(key, (TREES,), SOURCE - SOURCE // 4 + 1, SOURCE + 1)
    chosen = jax.random.randint(jax.random.fold_in(key, 1), (), 0, TREES)
    return jnp.where(jnp.arange(TREES) == chosen, SOURCE, lengths).astype(jnp.int32)


def shard_levels(key, extent, pieces, low, high):
    gain, own = 1.0, jax.random.fold_in(key, 6)
    for position, parts in pieces:
        steps = jnp.exp(jax.random.uniform(jax.random.fold_in(own, position), (parts,), jnp.float32, low / len(pieces), high / len(pieces)))
        gain = gain * jnp.repeat(steps, extent[position] // parts).reshape([-1 if axis == position else 1 for axis in range(len(extent))])
    return gain


def normal_values(key, extent, deviation, most, shards=(), held_as=jnp.bfloat16):
    loudness = shard_levels(key, extent, shards, -0.22, 0.18) if shards else 1.0
    array = jax.random.normal(key, extent, jnp.float32) * deviation * loudness
    return jnp.minimum(jnp.maximum(array, -most), most).astype(held_as)


def setup_inputs(seed: int = 0) -> dict:
    key_list = jax.random.split(jax.random.key(seed), 30)
    tokens = normal_values(key_list[0], (TOKENS, D), 1.0, 6.0, ((0, 32),))
    encoded = normal_values(key_list[1], (SOURCES, D), 1.0, 6.0, ((0, 32),))
    parents = draw_parents(jax.random.fold_in(key_list[29], 71), 0)
    source_lengths = draw_source_lengths(jax.random.fold_in(key_list[29], 71), 0)
    cotangent = normal_values(key_list[4], (TOKENS, D), 1.0, 6.0, ((0, 32),))
    first_gain = jnp.clip(1.0 + 0.1 * jax.random.normal(key_list[5], (D,), jnp.float32), 0.5, 1.5)
    first_shift = normal_values(key_list[6], (D,), 0.2, 1.25, (), jnp.float32)
    self_query = normal_values(key_list[7], (D, D), D ** -0.5, 0.1875, ((0, 8), (1, 4)))
    self_query_bias = normal_values(key_list[8], (D,), 0.3, 1.75, ((0, 4),), jnp.float32)
    self_key = normal_values(key_list[9], (D, D), D ** -0.5, 0.1875, ((0, 8), (1, 4)))
    self_value = normal_values(key_list[10], (D, D), D ** -0.5, 0.1875, ((0, 8), (1, 4)))
    self_value_bias = normal_values(key_list[11], (D,), 0.3, 1.75, ((0, 4),), jnp.float32)
    self_out = normal_values(key_list[12], (D, D), (D // 8) ** -0.5, 0.5, ((0, 4), (1, 8)))
    self_out_bias = normal_values(key_list[13], (D,), 0.3, 1.75, (), jnp.float32)
    second_gain = jnp.clip(1.0 + 0.1 * jax.random.normal(key_list[14], (D,), jnp.float32), 0.5, 1.5)
    second_shift = normal_values(key_list[15], (D,), 0.2, 1.25, (), jnp.float32)
    cross_query = normal_values(key_list[16], (D, D), D ** -0.5, 0.1875, ((0, 8), (1, 4)))
    cross_query_bias = normal_values(key_list[17], (D,), 0.3, 1.75, ((0, 4),), jnp.float32)
    cross_key = normal_values(key_list[18], (D, D), D ** -0.5, 0.1875, ((0, 8), (1, 4)))
    cross_value = normal_values(key_list[19], (D, D), D ** -0.5, 0.1875, ((0, 8), (1, 4)))
    cross_value_bias = normal_values(key_list[20], (D,), 0.3, 1.75, ((0, 4),), jnp.float32)
    cross_out = normal_values(key_list[21], (D, D), (D // 8) ** -0.5, 0.5, ((0, 4), (1, 8)))
    cross_out_bias = normal_values(key_list[22], (D,), 0.3, 1.75, (), jnp.float32)
    third_gain = jnp.clip(1.0 + 0.1 * jax.random.normal(key_list[23], (D,), jnp.float32), 0.5, 1.5)
    third_shift = normal_values(key_list[24], (D,), 0.2, 1.25, (), jnp.float32)
    up_weight = normal_values(key_list[25], (D, FF), D ** -0.5, 0.1875, ((0, 8), (1, 4)))
    up_bias = normal_values(key_list[26], (FF,), 0.5, 3.0, ((0, 4),), jnp.float32)
    down_weight = normal_values(key_list[27], (FF, D), FF ** -0.5, 0.0625, ((0, 4), (1, 8)))
    down_bias = normal_values(key_list[28], (D,), 0.3, 1.75, (), jnp.float32)
    return {"tokens": tokens, "encoded": encoded, "parents": parents, "source_lengths": source_lengths, "cotangent": cotangent, "first_gain": first_gain, "first_shift": first_shift, "self_query": self_query, "self_query_bias": self_query_bias, "self_key": self_key, "self_value": self_value, "self_value_bias": self_value_bias, "self_out": self_out, "self_out_bias": self_out_bias, "second_gain": second_gain, "second_shift": second_shift, "cross_query": cross_query, "cross_query_bias": cross_query_bias, "cross_key": cross_key, "cross_value": cross_value, "cross_value_bias": cross_value_bias, "cross_out": cross_out, "cross_out_bias": cross_out_bias, "third_gain": third_gain, "third_shift": third_shift, "up_weight": up_weight, "up_bias": up_bias, "down_weight": down_weight, "down_bias": down_bias}


@jax.custom_vjp
def low(v):
    return lax.optimization_barrier(v.astype(jnp.bfloat16)).astype(jnp.float32)

@jax.custom_vjp
def low_back(v):
    return v

def low_keep(v):
    return (low(v), None)

def low_pass(kept, grad):
    return (grad,)

def back_keep(v):
    return (v, None)

def back_low(kept, grad):
    return (low(grad),)
low.defvjp(low_keep, low_pass)
low_back.defvjp(back_keep, back_low)

def matmul(left, right):
    return jnp.dot(left, right, precision=lax.Precision.HIGHEST)

def layer_norm(rows, scale_gain, shift):
    average = lax.optimization_barrier(jnp.mean(rows, axis=-1, keepdims=True))
    centered = rows - average
    variance = lax.optimization_barrier(jnp.mean(centered * centered, axis=-1, keepdims=True))
    return centered * lax.rsqrt(variance + 1e-05) * scale_gain + shift

def ancestors(parent_row):
    count = parent_row.shape[0]

    def extend(segment_index, table):
        fresh = jnp.where(jnp.arange(count) == segment_index, 1.0, 0.0) + table[parent_row[segment_index]]
        return table.at[segment_index].set(fresh)
    return lax.fori_loop(1, count, extend, jnp.eye(count, dtype=jnp.float32))

def split_heads(matrix):
    return matrix.reshape(matrix.shape[0], -1, HEAD_DIM)

def attend(query, keys, values, allowed):
    total = query.shape[0]
    block = min(512, total)

    def one_block(items):
        query_block, allowed_block = items
        scores = jnp.einsum('qhd,khd->hqk', query_block, keys, precision=lax.Precision.HIGHEST) * HEAD_DIM ** (-0.5)
        scores = low_back(scores)
        scores = jnp.where(allowed_block[None], scores, -1e+30)
        probs = low(jax.nn.softmax(scores, axis=-1))
        return jnp.einsum('hqk,khd->qhd', probs, values, precision=lax.Precision.HIGHEST)
    outputs = lax.map(jax.checkpoint(one_block), (query.reshape(total // block, block, query.shape[1], HEAD_DIM), allowed.reshape(total // block, block, allowed.shape[1])))
    return outputs.reshape(total, -1)

def tree_layer(rows, source, parent_row, source_len, params):
    first_gain, first_shift, self_query, self_query_bias, self_key, self_value, self_value_bias, self_out, self_out_bias, second_gain, second_shift, cross_query, cross_query_bias, cross_key, cross_value, cross_value_bias, cross_out, cross_out_bias, third_gain, third_shift, up_weight, up_bias, down_weight, down_bias = params
    table = ancestors(parent_row)
    places = jnp.arange(TREE_LEN)
    segment_of = places // SEG
    allowed_self = (table[segment_of][:, segment_of] > 0.5) & (places[None, :] <= places[:, None])
    allowed_cross = jnp.broadcast_to(jnp.arange(SOURCE)[None, :] < source_len, (TREE_LEN, SOURCE))
    normed = low(layer_norm(rows, first_gain, first_shift))
    query = low(low_back(matmul(normed, self_query) + self_query_bias))
    keys = low(low_back(matmul(normed, self_key)))
    values = low(low_back(matmul(normed, self_value) + self_value_bias))
    mixed = low(low_back(attend(split_heads(query), split_heads(keys), split_heads(values), allowed_self)))
    hidden_one = rows + low_back(matmul(mixed, self_out) + self_out_bias)
    normed = low(layer_norm(hidden_one, second_gain, second_shift))
    query = low(low_back(matmul(normed, cross_query) + cross_query_bias))
    keys = low(low_back(matmul(source, cross_key)))
    values = low(low_back(matmul(source, cross_value) + cross_value_bias))
    mixed = low(low_back(attend(split_heads(query), split_heads(keys), split_heads(values), allowed_cross)))
    hidden_two = hidden_one + low_back(matmul(mixed, cross_out) + cross_out_bias)
    normed = low(layer_norm(hidden_two, third_gain, third_shift))
    inner = low(jax.nn.gelu(low_back(matmul(normed, up_weight) + up_bias), approximate=False))
    return hidden_two + low_back(matmul(inner, down_weight) + down_bias)

def reference(tokens, encoded, parents, source_lengths, cotangent, first_gain, first_shift, self_query, self_query_bias, self_key, self_value, self_value_bias, self_out, self_out_bias, second_gain, second_shift, cross_query, cross_query_bias, cross_key, cross_value, cross_value_bias, cross_out, cross_out_bias, third_gain, third_shift, up_weight, up_bias, down_weight, down_bias):
    params = tuple((item.astype(jnp.float32) for item in (first_gain, first_shift, self_query, self_query_bias, self_key, self_value, self_value_bias, self_out, self_out_bias, second_gain, second_shift, cross_query, cross_query_bias, cross_key, cross_value, cross_value_bias, cross_out, cross_out_bias, third_gain, third_shift, up_weight, up_bias, down_weight, down_bias)))
    rows = tokens.astype(jnp.float32).reshape(TREES, TREE_LEN, D)
    source = encoded.astype(jnp.float32).reshape(TREES, SOURCE, D)

    def forward(rows, source, params):

        def one_tree(items):
            return tree_layer(items[0], items[1], items[2], items[3], params)
        return lax.map(jax.checkpoint(one_tree), (rows, source, parents, source_lengths))
    outputs, pullback = jax.vjp(forward, rows, source, params)
    rows_grad, source_grad, grads = pullback(cotangent.astype(jnp.float32).reshape(TREES, TREE_LEN, D))
    return (outputs.reshape(TOKENS, D).astype(jnp.bfloat16), rows_grad.reshape(TOKENS, D), source_grad.reshape(SOURCES, D), grads[0], grads[1], grads[2], grads[3], grads[4], grads[5], grads[6], grads[7], grads[8], grads[9], grads[10], grads[11], grads[12], grads[13], grads[14], grads[15], grads[16], grads[17], grads[18], grads[19], grads[20], grads[21], grads[22], grads[23])
```

```python
import functools
import jax
import jax.numpy as jnp
from jax import lax
from jax.experimental import pallas as pl
from jax.experimental.pallas import tpu as pltpu
from jax.sharding import Mesh, PartitionSpec as P

HEAD_DIM = 64
SEG = 128
PAIR = 2 * HEAD_DIM
LOG2E = 1.4426950408889634
SCALE = HEAD_DIM ** -0.5
NEG = -1e30
f32, bf16 = jnp.float32, jnp.bfloat16
VMEM_LIMIT = 56 * 1024 * 1024


def dot(a, b, ca=1, cb=0):
    return lax.dot_general(a, b, (((ca,), (cb,)), ((), ())), preferred_element_type=f32)


def stack_heads(x):
    lane = lax.broadcasted_iota(jnp.int32, x.shape, 1)
    zero = jnp.zeros_like(x)
    return jnp.concatenate(
        [jnp.where(lane < HEAD_DIM, x, zero), jnp.where(lane >= HEAD_DIM, x, zero)], axis=0
    )


def unstack_heads(xt):
    n = xt.shape[1] // 2
    return jnp.concatenate([xt[:HEAD_DIM, :n], xt[HEAD_DIM:, n:]], axis=0).T


def forward_chunk(k, v, qT, bias, m, l, acc):
    s = dot(k, qT) * (SCALE * LOG2E)
    if bias is not None:
        s = bias(s)
    if m is None:
        m_new = jnp.max(s, axis=0, keepdims=True)
        p = jnp.exp2(s - m_new)
        l = jnp.sum(p, axis=0, keepdims=True)
        acc[...] = dot(v, p.astype(bf16), 0, 0)
    else:
        m_new = jnp.maximum(m, jnp.max(s, axis=0, keepdims=True))
        p = jnp.exp2(s - m_new)
        fade = jnp.exp2(m - m_new)
        l = l * fade + jnp.sum(p, axis=0, keepdims=True)
        acc[...] = acc[...] * fade + dot(v, p.astype(bf16), 0, 0)
    return m_new, l


def self_forward_kernel(plan, q_ref, k_ref, v_ref, bias_ref, o_ref, lse_ref, acc, *, rows, chunk):
    segs = chunk // SEG
    qT = stack_heads(q_ref[...]).T
    wide = 2 * rows

    def own_bias(a):
        def apply(s):
            key = lax.broadcasted_iota(jnp.int32, (chunk, wide), 0) + a * chunk
            query = lax.broadcasted_iota(jnp.int32, (chunk, wide), 1) & (rows - 1)
            b = jnp.concatenate(
                [jnp.broadcast_to(bias_ref[a * segs + j : a * segs + j + 1, :], (SEG, wide)) for j in range(segs)], 0)
            return jnp.where(key <= query, s + b, NEG)
        return apply

    m = l = None
    for a in range(rows // chunk):
        m, l = forward_chunk(
            k_ref[a * chunk : (a + 1) * chunk, :], v_ref[a * chunk : (a + 1) * chunk, :], qT, own_bias(a), m, l, acc)

    def step(i, carry):
        m, l = carry
        places = [plan[1 + i * segs + j] for j in range(segs)]
        brows = [plan[1 + plan.shape[0] // 2 + i * segs + j] for j in range(segs)]
        k = jnp.concatenate([k_ref[pl.ds(pl.multiple_of(p * SEG, SEG), SEG), :] for p in places], 0)
        v = jnp.concatenate([v_ref[pl.ds(pl.multiple_of(p * SEG, SEG), SEG), :] for p in places], 0)

        def apply(s):
            b = jnp.concatenate([jnp.broadcast_to(bias_ref[pl.ds(p, 1), :], (SEG, wide)) for p in brows], 0)
            return s + b
        return forward_chunk(k, v, qT, apply, m, l, acc)

    m, l = lax.fori_loop(0, plan[0], step, (m, l))
    o_ref[...] = unstack_heads(acc[...] * (1.0 / l)).astype(bf16)
    lse_ref[0] = m + jnp.log2(l)


def self_forward(plan, q, k, v, bias, chunk=256):
    rows, total = q.shape[0], k.shape[0]
    pairs = q.shape[1] // PAIR
    return pl.pallas_call(
        functools.partial(self_forward_kernel, rows=rows, chunk=chunk),
        grid_spec=pltpu.PrefetchScalarGridSpec(
            num_scalar_prefetch=1,
            grid=(pairs,),
            in_specs=[
                pl.BlockSpec((rows, PAIR), lambda h, p: (0, h)),
                pl.BlockSpec((total, PAIR), lambda h, p: (0, h)),
                pl.BlockSpec((total, PAIR), lambda h, p: (0, h)),
                pl.BlockSpec(bias.shape, lambda h, p: (0, 0)),
            ],
            out_specs=[
                pl.BlockSpec((rows, PAIR), lambda h, p: (0, h)),
                pl.BlockSpec((1, 1, 2 * rows), lambda h, p: (h, 0, 0)),
            ],
            scratch_shapes=[pltpu.VMEM((PAIR, 2 * rows), f32)],
        ),
        out_shape=[
            jax.ShapeDtypeStruct(q.shape, bf16),
            jax.ShapeDtypeStruct((pairs, 1, 2 * rows), f32),
        ],
        compiler_params=pltpu.CompilerParams(vmem_limit_bytes=VMEM_LIMIT),
        cost_estimate=pl.CostEstimate(flops=8 * rows * total * q.shape[1], bytes_accessed=4 * q.size + 4 * k.size, transcendentals=0),
        name="self_forward",
    )(plan, q, k, v, bias)


def cross_forward_kernel(length, q_ref, k_ref, v_ref, o_ref, lse_ref, acc, *, rows, chunk, sure):
    qT = stack_heads(q_ref[...]).T
    total = k_ref.shape[0]
    m = l = None
    for a in range(total // chunk):
        def apply(s, a=a):
            key = lax.broadcasted_iota(jnp.int32, s.shape, 0) + a * chunk
            return jnp.where(key < length[0], s, NEG)
        m, l = forward_chunk(
            k_ref[a * chunk : (a + 1) * chunk, :], v_ref[a * chunk : (a + 1) * chunk, :], qT,
            apply if (a + 1) * chunk > sure else None, m, l, acc)
    o_ref[...] = unstack_heads(acc[...] * (1.0 / l)).astype(bf16)
    lse_ref[0] = m + jnp.log2(l)


def cross_forward(length, q, k, v, sure, chunk=256):
    rows, total = q.shape[0], k.shape[0]
    pairs = q.shape[1] // PAIR
    return pl.pallas_call(
        functools.partial(cross_forward_kernel, rows=rows, chunk=chunk, sure=sure),
        grid_spec=pltpu.PrefetchScalarGridSpec(
            num_scalar_prefetch=1,
            grid=(pairs,),
            in_specs=[
                pl.BlockSpec((rows, PAIR), lambda h, p: (0, h)),
                pl.BlockSpec((total, PAIR), lambda h, p: (0, h)),
                pl.BlockSpec((total, PAIR), lambda h, p: (0, h)),
            ],
            out_specs=[
                pl.BlockSpec((rows, PAIR), lambda h, p: (0, h)),
                pl.BlockSpec((1, 1, 2 * rows), lambda h, p: (h, 0, 0)),
            ],
            scratch_shapes=[pltpu.VMEM((PAIR, 2 * rows), f32)],
        ),
        out_shape=[
            jax.ShapeDtypeStruct(q.shape, bf16),
            jax.ShapeDtypeStruct((pairs, 1, 2 * rows), f32),
        ],
        compiler_params=pltpu.CompilerParams(vmem_limit_bytes=VMEM_LIMIT),
        cost_estimate=pl.CostEstimate(flops=16 * rows * total * q.shape[1], bytes_accessed=4 * q.size + 4 * k.size, transcendentals=0),
        name="cross_forward",
    )(length, q, k, v)


def backward_chunk(k, v, qst, qT, dost, doT, lse, delta, bias, dqT, first):
    s = dot(k, qT) * (SCALE * LOG2E)
    if bias is not None:
        s = bias(s)
    p = jnp.exp2(s - lse)
    ds = (p * (dot(v, doT) - delta)).astype(bf16)
    dv = dot(p.astype(bf16), dost)
    dk = dot(ds, qst) * SCALE
    part = dot(k, ds, 0, 0)
    if first:
        dqT[...] = part
    else:
        dqT[...] += part
    return dk.astype(bf16), dv.astype(bf16)


def backward_setup(q_ref, o_ref, do_ref):
    qst = stack_heads(q_ref[...])
    dost = stack_heads(do_ref[...])
    qT, doT = qst.T, dost.T
    oT = o_ref[...].T.astype(f32)
    oT2 = jnp.concatenate([oT, oT], axis=1)
    delta = jnp.sum(doT.astype(f32) * oT2, axis=0, keepdims=True)
    return qst, qT, dost, doT, delta


def self_backward_kernel(plan, q_ref, k_ref, v_ref, o_ref, do_ref, lse_ref, bias_ref, dq_ref, dk_ref, dv_ref, dqT, *, rows, chunk):
    segs = chunk // SEG
    wide = 2 * rows
    qst, qT, dost, doT, delta = backward_setup(q_ref, o_ref, do_ref)
    lse = lse_ref[0]
    dqT[...] = jnp.zeros_like(dqT)
    dk_ref[rows:, :] = jnp.zeros((dk_ref.shape[0] - rows, PAIR), bf16)
    dv_ref[rows:, :] = jnp.zeros((dv_ref.shape[0] - rows, PAIR), bf16)

    def step(i, carry):
        places = [pl.multiple_of(plan[1 + i * segs + j] * SEG, SEG) for j in range(segs)]
        brows = [plan[1 + plan.shape[0] // 2 + i * segs + j] for j in range(segs)]
        k = jnp.concatenate([k_ref[pl.ds(p, SEG), :] for p in places], 0)
        v = jnp.concatenate([v_ref[pl.ds(p, SEG), :] for p in places], 0)

        def apply(s):
            b = jnp.concatenate([jnp.broadcast_to(bias_ref[pl.ds(p, 1), :], (SEG, wide)) for p in brows], 0)
            return s + b
        dk, dv = backward_chunk(k, v, qst, qT, dost, doT, lse, delta, apply, dqT, False)
        for j in range(segs):
            dk_ref[pl.ds(places[j], SEG), :] = dk[j * SEG : (j + 1) * SEG]
            dv_ref[pl.ds(places[j], SEG), :] = dv[j * SEG : (j + 1) * SEG]
        return carry

    lax.fori_loop(0, plan[0], step, 0)

    for a in range(rows // chunk):
        def apply(s, a=a):
            key = lax.broadcasted_iota(jnp.int32, (chunk, wide), 0) + a * chunk
            query = lax.broadcasted_iota(jnp.int32, (chunk, wide), 1) & (rows - 1)
            b = jnp.concatenate(
                [jnp.broadcast_to(bias_ref[a * segs + j : a * segs + j + 1, :], (SEG, wide)) for j in range(segs)], 0)
            return jnp.where(key <= query, s + b, NEG)
        sl = slice(a * chunk, (a + 1) * chunk)
        dk, dv = backward_chunk(k_ref[sl, :], v_ref[sl, :], qst, qT, dost, doT, lse, delta, apply, dqT, False)
        dk_ref[sl, :] = dk
        dv_ref[sl, :] = dv
    dq_ref[...] = (unstack_heads(dqT[...]) * SCALE).astype(bf16)


def self_backward(plan, q, k, v, o, do, lse, bias, chunk=256):
    rows, total = q.shape[0], k.shape[0]
    pairs = q.shape[1] // PAIR
    qs = pl.BlockSpec((rows, PAIR), lambda h, p: (0, h))
    ks = pl.BlockSpec((total, PAIR), lambda h, p: (0, h))
    return pl.pallas_call(
        functools.partial(self_backward_kernel, rows=rows, chunk=chunk),
        grid_spec=pltpu.PrefetchScalarGridSpec(
            num_scalar_prefetch=1,
            grid=(pairs,),
            in_specs=[qs, ks, ks, qs, qs,
                pl.BlockSpec((1, 1, 2 * rows), lambda h, p: (h, 0, 0)),
                pl.BlockSpec(bias.shape, lambda h, p: (0, 0)),
            ],
            out_specs=[qs, ks, ks],
            scratch_shapes=[pltpu.VMEM((PAIR, 2 * rows), f32)],
        ),
        out_shape=[jax.ShapeDtypeStruct(q.shape, bf16), jax.ShapeDtypeStruct(k.shape, bf16), jax.ShapeDtypeStruct(k.shape, bf16)],
        compiler_params=pltpu.CompilerParams(vmem_limit_bytes=VMEM_LIMIT),
        cost_estimate=pl.CostEstimate(flops=20 * rows * total * q.shape[1], bytes_accessed=8 * q.size + 8 * k.size, transcendentals=0),
        name="self_backward",
    )(plan, q, k, v, o, do, lse, bias)


def cross_backward_kernel(length, q_ref, k_ref, v_ref, o_ref, do_ref, lse_ref, dq_ref, dk_ref, dv_ref, dqT, *, rows, chunk, sure):
    qst, qT, dost, doT, delta = backward_setup(q_ref, o_ref, do_ref)
    lse = lse_ref[0]
    for a in range(k_ref.shape[0] // chunk):
        def apply(s, a=a):
            key = lax.broadcasted_iota(jnp.int32, s.shape, 0) + a * chunk
            return jnp.where(key < length[0], s, NEG)
        sl = slice(a * chunk, (a + 1) * chunk)
        dk, dv = backward_chunk(k_ref[sl, :], v_ref[sl, :], qst, qT, dost, doT, lse, delta,
                                apply if (a + 1) * chunk > sure else None, dqT, a == 0)
        dk_ref[sl, :] = dk
        dv_ref[sl, :] = dv
    dq_ref[...] = (unstack_heads(dqT[...]) * SCALE).astype(bf16)


def cross_backward(length, q, k, v, o, do, lse, sure, chunk=256):
    rows, total = q.shape[0], k.shape[0]
    pairs = q.shape[1] // PAIR
    qs = pl.BlockSpec((rows, PAIR), lambda h, p: (0, h))
    ks = pl.BlockSpec((total, PAIR), lambda h, p: (0, h))
    return pl.pallas_call(
        functools.partial(cross_backward_kernel, rows=rows, chunk=chunk, sure=sure),
        grid_spec=pltpu.PrefetchScalarGridSpec(
            num_scalar_prefetch=1,
            grid=(pairs,),
            in_specs=[qs, ks, ks, qs, qs, pl.BlockSpec((1, 1, 2 * rows), lambda h, p: (h, 0, 0))],
            out_specs=[qs, ks, ks],
            scratch_shapes=[pltpu.VMEM((PAIR, 2 * rows), f32)],
        ),
        out_shape=[jax.ShapeDtypeStruct(q.shape, bf16), jax.ShapeDtypeStruct(k.shape, bf16), jax.ShapeDtypeStruct(k.shape, bf16)],
        compiler_params=pltpu.CompilerParams(vmem_limit_bytes=VMEM_LIMIT),
        cost_estimate=pl.CostEstimate(flops=40 * rows * total * q.shape[1], bytes_accessed=8 * q.size + 8 * k.size, transcendentals=0),
        name="cross_backward",
    )(length, q, k, v, o, do, lse)


ERFC = (0.254829592, -0.284496736, 1.421413741, -1.453152027, 1.061405429)


def gelu_pair(v):
    e = jnp.exp2(v * v * (-0.5 * LOG2E))
    t = 1.0 / (1.0 + jnp.abs(v) * (0.3275911 * 0.7071067811865476))
    a1, a2, a3, a4, a5 = (0.5 * a for a in ERFC)
    tail = ((((a5 * t + a4) * t + a3) * t + a2) * t + a1) * t * e
    cdf = jnp.where(v >= 0.0, 1.0 - tail, tail)
    return v * cdf, cdf + v * e * 0.3989422804014327


def feed_forward_kernel(r_ref, g_ref, w_ref, ub_ref, out_ref, back_ref, inner_ref, grad_ref):
    hidden, width = w_ref.shape[0] * w_ref.shape[2], w_ref.shape[3]
    up = w_ref[:, 0].reshape(hidden, width)
    down = w_ref[:, 1].reshape(hidden, width)
    lifted = dot(r_ref[...], up, 1, 1) + ub_ref[...]
    grad_inner = dot(g_ref[...], down, 1, 1)
    value, slope = gelu_pair(lifted)
    inner = value.astype(bf16)
    grad = (grad_inner * slope).astype(bf16)
    inner_ref[...] = inner
    grad_ref[...] = grad
    back_ref[...] = dot(grad, up).astype(bf16)
    out_ref[...] = dot(inner, down).astype(bf16)


def feed_forward(r, g, weights, ub, tile=512):
    rows, width = r.shape
    hidden = weights.shape[0] * weights.shape[2]
    row = pl.BlockSpec((tile, width), lambda i: (i, 0))
    tall = pl.BlockSpec((tile, hidden), lambda i: (i, 0))
    return pl.pallas_call(
        feed_forward_kernel,
        grid=(rows // tile,),
        in_specs=[
            row,
            row,
            pl.BlockSpec(weights.shape, lambda i: (0, 0, 0, 0)),
            pl.BlockSpec(ub.shape, lambda i: (0, 0)),
        ],
        out_specs=[row, row, tall, tall],
        out_shape=[
            jax.ShapeDtypeStruct((rows, width), bf16),
            jax.ShapeDtypeStruct((rows, width), bf16),
            jax.ShapeDtypeStruct((rows, hidden), bf16),
            jax.ShapeDtypeStruct((rows, hidden), bf16),
        ],
        compiler_params=pltpu.CompilerParams(vmem_limit_bytes=VMEM_LIMIT),
        cost_estimate=pl.CostEstimate(
            flops=8 * rows * width * hidden,
            bytes_accessed=12 * rows * width + 2 * weights.size,
            transcendentals=0,
        ),
        name="feed_forward",
    )(r, g, weights, ub)


EPSILON = 1e-05


def normed(rows, gain, shift):
    average = jnp.mean(rows, axis=-1, keepdims=True)
    centered = rows - average
    variance = jnp.mean(centered * centered, axis=-1, keepdims=True)
    return (centered * lax.rsqrt(variance + EPSILON) * gain + shift).astype(bf16)


def norm_back(rows, gain, grad):
    average = jnp.mean(rows, axis=-1, keepdims=True)
    centered = rows - average
    scale = lax.rsqrt(jnp.mean(centered * centered, axis=-1, keepdims=True) + EPSILON)
    xhat = centered * scale
    scaled = grad * gain
    back = scale * (
        scaled
        - jnp.mean(scaled, axis=-1, keepdims=True)
        - xhat * jnp.mean(scaled * xhat, axis=-1, keepdims=True)
    )
    return back, jnp.sum(grad * xhat, axis=0), jnp.sum(grad, axis=0)


def column_sums(matrix):
    return jnp.sum(matrix.astype(f32), axis=0)


def flip(x, k, size):
    return lax.ppermute(x, "low", [(i, i ^ k) for i in range(size)])


def gather_low(x, size):
    if size != 8:
        return [x if k == 0 else flip(x, k, size) for k in range(size)]
    half = x.shape[0] // 2
    first, second = x[:half], x[half:]
    x0, y1 = flip(first, 2, size), flip(second, 4, size)
    x1, y0 = flip(second, 2, size), flip(first, 4, size)
    xy0, xy1 = flip(x0, 4, size), flip(y1, 2, size)
    even = [
        x,
        jnp.concatenate([x0, x1], 0),
        jnp.concatenate([y0, y1], 0),
        jnp.concatenate([xy0, xy1], 0),
    ]
    odd = [flip(e, 1, size) for e in even]
    return [p for pair in zip(even, odd) for p in pair]


def scatter_low(pieces, size):
    if size != 8:
        total = pieces[0].astype(f32)
        for k in range(1, size):
            total = total + flip(pieces[k], k, size).astype(f32)
        return total
    even = [
        (pieces[k].astype(f32) + flip(pieces[k + 1], 1, size).astype(f32)) for k in (6, 4, 2, 0)
    ]
    back = [flip(e.astype(bf16), k, size).astype(f32) for e, k in zip(even[:3], (6, 4, 2))]
    return even[3] + back[0] + back[1] + back[2]


def arrange(pieces, low, axis):
    count, extent = len(pieces), pieces[0].shape[axis]
    shape = list(pieces[0].shape)
    shape[axis] = count * extent
    whole = jnp.zeros(shape, pieces[0].dtype)
    for k, piece in enumerate(pieces):
        whole = lax.dynamic_update_slice_in_dim(whole, piece, (low ^ k) * extent, axis)
    return whole


def gather_tensor(x, size, place, axis):
    shape = list(x.shape)
    extent = shape[axis]
    shape[axis] = extent * size
    whole = lax.dynamic_update_slice_in_dim(jnp.zeros(shape, x.dtype), x, place * extent, axis)
    for k in range(1, size):
        got = lax.ppermute(x, "tensor", [(i, (i + k) % size) for i in range(size)])
        whole = lax.dynamic_update_slice_in_dim(
            whole, got, lax.rem(place + size - k, size) * extent, axis
        )
    return whole


def gather_weights(shards, sizes, low, place):
    wide = gather_tensor(jnp.stack(shards), sizes[2], place, 2)
    rows = wide.shape[1]
    pieces = gather_low(wide.transpose(1, 0, 2).reshape(rows, -1), sizes[1])
    matrices = arrange(pieces, low, 0)
    if sizes[0] > 1:
        matrices = lax.all_gather(matrices, "high", axis=0, tiled=True)
    width = wide.shape[2]
    return [matrices[:, i * width : (i + 1) * width] for i in range(len(shards))]


def scatter_weights(grads, sizes, low, place):
    count, width = len(grads), grads[0].shape[1]
    stacked = jnp.concatenate([g.astype(bf16) for g in grads], axis=1)
    if sizes[0] > 1:
        stacked = lax.psum_scatter(stacked, "high", scatter_dimension=0, tiled=True)
    extent = stacked.shape[0] // sizes[1]
    pieces = [
        lax.dynamic_slice_in_dim(stacked, (low ^ k) * extent, extent, 0) for k in range(sizes[1])
    ]
    mine = scatter_low(pieces, sizes[1]).astype(bf16)
    mine = mine.reshape(extent, count, sizes[2], width // sizes[2]).transpose(2, 1, 0, 3)
    parts = lax.all_to_all(mine, "tensor", split_axis=0, concat_axis=0, tiled=True)
    total = jnp.sum(parts.astype(f32), axis=0)
    return [total[i] for i in range(count)]


def path_plan(parents, place, own, blocks):
    count = parents.shape[0]
    labels = jnp.arange(count)
    table = (
        (labels[:, None] == labels[None, :])
        | ((parents[:, None] == labels[None, :]) & (labels[:, None] > 0))
    ).astype(f32)
    reach = 1
    while reach < count:
        table = jnp.minimum(jnp.dot(table, table), 1.0)
        reach *= 2
    slots = jnp.arange(blocks * own)
    back, inside = slots // own, slots % own
    segment = (place - back) * own + inside
    pick = (labels[:, None] == segment[None, :]).astype(f32)
    mine = (labels[None, :] == (place * own + jnp.arange(own))[:, None]).astype(f32)
    seen = jnp.dot(jnp.dot(mine, table), pick)
    needed = jnp.any(seen > 0.5, axis=0) & (back > 0)
    rank = jnp.cumsum(needed.astype(jnp.int32)) - 1
    total = jnp.sum(needed.astype(jnp.int32))
    steps = jnp.arange(slots.shape[0])
    chosen = needed[None, :] & (rank[None, :] == steps[:, None])
    order = jnp.sum(jnp.where(chosen, slots[None, :], 0), axis=1)
    rows = jnp.where(steps < total, order, slots.shape[0])
    lanes = jnp.arange(2 * own * SEG)
    spread = (((lanes // SEG) % own)[None, :] == jnp.arange(own)[:, None]).astype(f32)
    bias = jnp.where(jnp.dot(seen.T, spread) > 0.5, 0.0, NEG)
    bias = jnp.concatenate([bias, jnp.full((8, bias.shape[1]), NEG, f32)], axis=0)
    per_step = CHUNK // SEG
    plan = jnp.concatenate([((total + per_step - 1) // per_step)[None], order, jnp.zeros((1,), jnp.int32), rows])
    return plan.astype(jnp.int32), bias


CHUNK = 512


def on_device(sizes, sure):
    high, low_size, size = sizes

    def run(
        tokens,
        encoded,
        parents,
        source_lengths,
        cotangent,
        first_gain,
        first_shift,
        self_query,
        self_query_bias,
        self_key,
        self_value,
        self_value_bias,
        self_out,
        self_out_bias,
        second_gain,
        second_shift,
        cross_query,
        cross_query_bias,
        cross_key,
        cross_value,
        cross_value_bias,
        cross_out,
        cross_out_bias,
        third_gain,
        third_shift,
        up_weight,
        up_bias,
        down_weight,
        down_bias,
    ):
        low = lax.axis_index("low")
        place = lax.axis_index("tensor")
        rows, width = tokens.shape
        up_chain = [(i, i + 1) for i in range(size - 1)]
        down_chain = [(i + 1, i) for i in range(size - 1)]

        blocks = [tokens]
        for _ in range(size - 1):
            blocks.append(lax.ppermute(blocks[-1], "tensor", up_chain))
        wq, wk, wv = gather_weights([self_query, self_key, self_value], sizes, low, place)
        wo, xq, xk, xv, xo = gather_weights(
            [self_out.T, cross_query, cross_key, cross_value, cross_out.T], sizes, low, place
        )
        source = lax.all_gather(encoded, "tensor", axis=0, tiled=True)
        both = jnp.stack([up_weight.T, down_weight])
        both = lax.all_to_all(both, "low", split_axis=1, concat_axis=2, tiled=True)
        if high > 1:
            both = lax.all_gather(both, "high", axis=2, tiled=True)
        hidden = both.shape[1]
        lifts = lax.all_gather(both[None], "tensor", axis=0, tiled=True)
        ub = lax.all_gather(
            lax.dynamic_slice_in_dim(up_bias, low * hidden, hidden, 0), "tensor", axis=0, tiled=True
        )
        biases = lax.all_gather(
            jnp.stack([self_query_bias, self_value_bias, cross_query_bias, cross_value_bias]),
            "tensor", axis=1, tiled=True,
        )
        q_bias, v_bias, xq_bias, xv_bias = [biases[i] for i in range(4)]
        cots = gather_low(cotangent, low_size)
        plan, bias = path_plan(parents[0], place, rows // SEG, size)

        tokens_f = tokens.astype(f32)
        one = normed(jnp.concatenate(blocks, 0).astype(f32), first_gain, first_shift)
        own = one[:rows]
        q1 = (dot(own, wq) + q_bias).astype(bf16)
        k1 = dot(one, wk).astype(bf16)
        v1 = (dot(one, wv) + v_bias).astype(bf16)
        mixed_one, lse_one = self_forward(plan, q1, k1, v1, bias, CHUNK)
        hidden_one = tokens_f + dot(mixed_one, wo, 1, 1) + self_out_bias
        two = normed(hidden_one, second_gain, second_shift)
        q2 = (dot(two, xq) + xq_bias).astype(bf16)
        k2 = dot(source, xk).astype(bf16)
        v2 = (dot(source, xv) + xv_bias).astype(bf16)
        mixed_two, lse_two = cross_forward(source_lengths, q2, k2, v2, sure, CHUNK)
        hidden_two = hidden_one + dot(mixed_two, xo, 1, 1) + cross_out_bias
        three = normed(hidden_two, third_gain, third_shift)

        threes = gather_low(three, low_size)
        outs, backs, inners, lifted_grads = [], [], [], []
        for k in range(0, low_size, 2):
            r = jnp.concatenate(threes[k : k + 2], 0)
            g = jnp.concatenate(cots[k : k + 2], 0)
            out, back, inner, grad = feed_forward(r, g, lifts, ub[None])
            outs += [out[:rows], out[rows:]]
            backs += [back[:rows], back[rows:]]
            inners.append((inner, g))
            lifted_grads.append((grad, r))
        grad_three = scatter_low(backs, low_size)
        block_out = hidden_two + scatter_low(outs, low_size) + down_bias
        up_bias_part = sum(column_sums(grad) for grad, _ in lifted_grads)
        up_grad = sum(dot(grad, r, 0, 0) for grad, r in lifted_grads)
        down_grad = sum(dot(inner, g, 0, 0) for inner, g in inners)
        lift_grads = jnp.stack(
            [up_grad.reshape(size, hidden, width), down_grad.reshape(size, hidden, width)], 1
        ).astype(bf16)
        lift_grads = lax.psum_scatter(lift_grads, "tensor", scatter_dimension=0, tiled=True)[0]
        if high > 1:
            lift_grads = lax.psum_scatter(lift_grads, "high", scatter_dimension=2, tiled=True)
        lift_grads = lax.all_to_all(lift_grads, "low", split_axis=2, concat_axis=1, tiled=True)
        up_weight_grad = lift_grads[0].T.astype(f32)
        down_weight_grad = lift_grads[1].astype(f32)

        down_bias_grad = column_sums(cotangent)
        back, third_gain_grad, third_shift_grad = norm_back(hidden_two, third_gain, grad_three)
        grad_hidden_two = cotangent.astype(f32) + back
        grad_two = grad_hidden_two.astype(bf16)
        cross_out_bias_grad = column_sums(grad_two)
        xo_grad = dot(grad_two, mixed_two, 0, 0)
        do2 = dot(grad_two, xo).astype(bf16)
        dq2, dk2, dv2 = cross_backward(
            source_lengths, q2, k2, v2, mixed_two, do2, lse_two, sure, CHUNK
        )
        xq_grad = dot(two, dq2, 0, 0)
        xk_grad = dot(source, dk2, 0, 0)
        xv_grad = dot(source, dv2, 0, 0)
        encoded_grad = lax.psum_scatter(
            (dot(dk2, xk, 1, 1) + dot(dv2, xv, 1, 1)).astype(bf16),
            "tensor", scatter_dimension=0, tiled=True,
        ).astype(f32)
        back, second_gain_grad, second_shift_grad = norm_back(
            hidden_one, second_gain, dot(dq2, xq, 1, 1)
        )
        grad_hidden_one = grad_hidden_two + back
        grad_one = grad_hidden_one.astype(bf16)
        self_out_bias_grad = column_sums(grad_one)
        wo_grad = dot(grad_one, mixed_one, 0, 0)
        do1 = dot(grad_one, wo).astype(bf16)
        dq1, dk1, dv1 = self_backward(plan, q1, k1, v1, mixed_one, do1, lse_one, bias, CHUNK)
        wq_grad = dot(own, dq1, 0, 0)
        wk_grad = dot(one, dk1, 0, 0)
        wv_grad = dot(one, dv1, 0, 0)
        shares = dot(dk1, wk, 1, 1) + dot(dv1, wv, 1, 1)
        share = shares[(size - 1) * rows :]
        for r in range(size - 2, -1, -1):
            got = lax.ppermute(share.astype(bf16), "tensor", down_chain)
            share = shares[r * rows : (r + 1) * rows] + got.astype(f32)
        grad_rows = share + dot(dq1, wq, 1, 1)
        back, first_gain_grad, first_shift_grad = norm_back(tokens_f, first_gain, grad_rows)
        tokens_grad = grad_hidden_one + back

        wo_g, xq_g, xk_g, xv_g, xo_g = scatter_weights(
            [wo_grad, xq_grad, xk_grad, xv_grad, xo_grad], sizes, low, place
        )
        wq_g, wk_g, wv_g = scatter_weights([wq_grad, wk_grad, wv_grad], sizes, low, place)

        spread = jnp.zeros((size, up_bias.shape[0]), f32)
        spread = lax.dynamic_update_slice(
            spread, up_bias_part.reshape(size, hidden), (0, low * hidden)
        )
        vectors = [
            first_gain_grad,
            first_shift_grad,
            second_gain_grad,
            second_shift_grad,
            third_gain_grad,
            third_shift_grad,
            self_out_bias_grad,
            cross_out_bias_grad,
            down_bias_grad,
            column_sums(dq1),
            column_sums(dv1),
            column_sums(dq2),
            column_sums(dv2),
            spread.reshape(-1),
        ]
        summed = lax.psum(jnp.concatenate(vectors), ("high", "low", "tensor"))
        small = [summed[i * width : (i + 1) * width] for i in range(13)]
        part = width // size
        split = [lax.dynamic_slice_in_dim(s, place * part, part, 0) for s in small[9:]]
        up_bias_grad = lax.dynamic_slice_in_dim(
            summed[13 * width :], place * up_bias.shape[0], up_bias.shape[0], 0
        )
        return (
            block_out.astype(bf16),
            tokens_grad,
            encoded_grad,
            small[0],
            small[1],
            wq_g,
            split[0],
            wk_g,
            wv_g,
            split[1],
            wo_g.T,
            small[6],
            small[2],
            small[3],
            xq_g,
            split[2],
            xk_g,
            xv_g,
            split[3],
            xo_g.T,
            small[7],
            small[4],
            small[5],
            up_weight_grad,
            up_bias_grad,
            down_weight_grad,
            small[8],
        )

    return run


def solution(mesh):
    dp, size = mesh.shape["dp"], mesh.shape["tensor"]
    low = min(8, dp)
    sizes = (dp // low, low, size)
    fine = Mesh(mesh.devices.reshape(sizes), ("high", "low", "tensor"))
    depth = ("high", "low")
    rows = P((*depth, "tensor"), None)
    block, turned = P(depth, "tensor"), P("tensor", depth)
    part, whole = P("tensor"), P()
    placed = (
        rows, rows, P(depth, None), P(depth), rows, whole, whole,
        block, part, block, block, part, turned, whole, whole, whole,
        block, part, block, block, part, turned, whole, whole, whole,
        block, part, turned, whole,
    )
    out = (
        rows, rows, rows, whole, whole,
        block, part, block, block, part, turned, whole, whole, whole,
        block, part, block, block, part, turned, whole, whole, whole,
        block, part, turned, whole,
    )
    return jax.shard_map(
        on_device(sizes, 768), mesh=fine, in_specs=placed, out_specs=out, check_vma=False
    )
```

```python
import functools

import jax
import jax.numpy as jnp
from jax import lax
from jax.experimental import pallas as pl
from jax.experimental.pallas import tpu as pltpu
from jax.sharding import Mesh, PartitionSpec as P

HEAD_DIM = 64
SEG = 128
PAIR = 2 * HEAD_DIM
EPSILON = 1e-05
LOG2E = 1.4426950408889634
SCALE = HEAD_DIM ** -0.5
NEG = -1e30
CHUNK = 512
VMEM_LIMIT = 56 * 1024 * 1024
f32, bf16 = jnp.float32, jnp.bfloat16


def dot(a, b, ca=1, cb=0):
    return lax.dot_general(a, b, (((ca,), (cb,)), ((), ())), preferred_element_type=f32)


def cost(flops, moved):
    return pl.CostEstimate(flops=int(flops), bytes_accessed=int(moved), transcendentals=0)


def params():
    return pltpu.CompilerParams(vmem_limit_bytes=VMEM_LIMIT)


def move(name, scalars, sources, outs, plan):
    count = len(plan([0] * scalars.shape[0]))

    def kernel(scalars_ref, *refs):
        ins, dests, sems = refs[: len(sources)], refs[len(sources) : -1], refs[-1]
        values = [scalars_ref[i] for i in range(scalars.shape[0])]
        copies = [
            pltpu.make_async_copy(ins[a].at[ai], dests[b].at[bi], sems.at[n])
            for n, (a, ai, b, bi) in enumerate(plan(values))
        ]
        for copy in copies:
            copy.start()
        for copy in copies:
            copy.wait()

    anywhere = pl.BlockSpec(memory_space=pl.ANY)
    return pl.pallas_call(
        kernel,
        in_specs=[pl.BlockSpec(memory_space=pltpu.SMEM)]
        + [pl.BlockSpec(memory_space=pltpu.VMEM)] * len(sources),
        out_specs=[anywhere] * len(outs),
        out_shape=[jax.ShapeDtypeStruct(s, bf16) for s in outs],
        scratch_shapes=[pltpu.SemaphoreType.DMA((count,))],
        compiler_params=params(),
        cost_estimate=cost(0, 4 * sum(x.size for x in sources)),
        name=name,
    )(scalars, *sources)


def at(start, extent):
    return pl.ds(start if isinstance(start, int) else pl.multiple_of(start, extent), extent)


def stack_heads(x):
    lane = lax.broadcasted_iota(jnp.int32, x.shape, 1)
    zero = jnp.zeros_like(x)
    return jnp.concatenate(
        [jnp.where(lane < HEAD_DIM, x, zero), jnp.where(lane >= HEAD_DIM, x, zero)], axis=0
    )


def unstack_heads(xt):
    n = xt.shape[1] // 2
    return jnp.concatenate([xt[:HEAD_DIM, :n], xt[HEAD_DIM:, n:]], axis=0).T


def segment_bias(bias_ref, block, s, causal):
    keys, wide = s.shape
    segs = keys // SEG
    b = jnp.concatenate(
        [
            jnp.broadcast_to(bias_ref[block * segs + j : block * segs + j + 1, :], (SEG, wide))
            for j in range(segs)
        ],
        0,
    )
    s = s + b
    if causal:
        key = lax.broadcasted_iota(jnp.int32, s.shape, 0)
        query = lax.broadcasted_iota(jnp.int32, s.shape, 1) & (wide // 2 - 1)
        s = jnp.where(key <= query, s, NEG)
    return s


def forward_step(k, v, qT, mask, m_ref, l_ref, acc, first):
    s = mask(dot(k, qT) * (SCALE * LOG2E))
    top = jnp.max(s, axis=0, keepdims=True)
    if first:
        p = jnp.exp2(s - top)
        m_ref[...] = top
        l_ref[...] = jnp.sum(p, axis=0, keepdims=True)
        acc[...] = dot(v, p.astype(bf16), 0, 0)
    else:
        m = jnp.maximum(m_ref[...], top)
        p = jnp.exp2(s - m)
        fade = jnp.exp2(m_ref[...] - m)
        m_ref[...] = m
        l_ref[...] = l_ref[...] * fade + jnp.sum(p, axis=0, keepdims=True)
        acc[...] = acc[...] * fade + dot(v, p.astype(bf16), 0, 0)


def forward_finish(o_ref, lse_ref, m_ref, l_ref, acc):
    o_ref[...] = unstack_heads(acc[...] * (1.0 / l_ref[...])).astype(bf16)
    lse_ref[0] = m_ref[...] + jnp.log2(l_ref[...])


def self_forward(place, q, ks, vs, bias, blocks, state, final):
    rows, count = q.shape[0], len(blocks)
    pairs = q.shape[1] // PAIR
    given = 0 if state is None else 3

    def kernel(place_ref, q_ref, *refs):
        k_refs, v_refs, bias_ref = refs[:count], refs[count : 2 * count], refs[2 * count]
        before = refs[2 * count + 1 : 2 * count + 1 + given]
        outs = refs[2 * count + 1 + given :]
        if final:
            o_ref, lse_ref, m_ref, l_ref, acc = outs
        else:
            m_out, l_out, acc_out, m_ref, l_ref, acc = outs
        if given:
            m_ref[...], l_ref[...], acc[...] = before[0][0], before[1][0], before[2][0]
        qT = stack_heads(q_ref[...]).T
        for n, r in enumerate(blocks):
            def step(n=n, r=r):
                forward_step(
                    k_refs[n][...], v_refs[n][...], qT,
                    lambda s: segment_bias(bias_ref, r, s, r == 0), m_ref, l_ref, acc, r == 0,
                )
            if r == 0:
                step()
            else:
                pl.when(place_ref[0] >= r)(step)
        if final:
            forward_finish(o_ref, lse_ref, m_ref, l_ref, acc)
        else:
            m_out[0], l_out[0], acc_out[0] = m_ref[...], l_ref[...], acc[...]

    col = pl.BlockSpec((rows, PAIR), lambda h, p: (0, h))
    line = pl.BlockSpec((1, 1, 2 * rows), lambda h, p: (h, 0, 0))
    slab = pl.BlockSpec((1, PAIR, 2 * rows), lambda h, p: (h, 0, 0))
    lines = jax.ShapeDtypeStruct((pairs, 1, 2 * rows), f32)
    slabs = jax.ShapeDtypeStruct((pairs, PAIR, 2 * rows), f32)
    stat = pltpu.VMEM((1, 2 * rows), f32)
    return pl.pallas_call(
        kernel,
        grid_spec=pltpu.PrefetchScalarGridSpec(
            num_scalar_prefetch=1,
            grid=(pairs,),
            in_specs=[col] * (1 + 2 * count)
            + [pl.BlockSpec(bias.shape, lambda h, p: (0, 0))]
            + [line, line, slab][:given],
            out_specs=[col, line] if final else [line, line, slab],
            scratch_shapes=[stat, stat, pltpu.VMEM((PAIR, 2 * rows), f32)],
        ),
        out_shape=[jax.ShapeDtypeStruct(q.shape, bf16), lines] if final else [lines, lines, slabs],
        compiler_params=params(),
        cost_estimate=cost(16 * count * rows * q.size, 4 * q.size * (1 + count)),
        name="self_forward",
    )(place, q, *[ks[r] for r in blocks], *[vs[r] for r in blocks], bias, *(state or ()))


def cross_forward(length, q, k, v, sure):
    rows, total = q.shape[0], k.shape[0]
    pairs = q.shape[1] // PAIR

    def kernel(length_ref, q_ref, k_ref, v_ref, o_ref, lse_ref, m_ref, l_ref, acc):
        qT = stack_heads(q_ref[...]).T
        for a in range(0, total, CHUNK):
            sl = slice(a, a + CHUNK)
            forward_step(
                k_ref[sl, :], v_ref[sl, :], qT,
                lambda s: length_mask(length_ref, s, a, sure), m_ref, l_ref, acc, a == 0,
            )
        forward_finish(o_ref, lse_ref, m_ref, l_ref, acc)

    col = pl.BlockSpec((rows, PAIR), lambda h, p: (0, h))
    tall = pl.BlockSpec((total, PAIR), lambda h, p: (0, h))
    stat = pltpu.VMEM((1, 2 * rows), f32)
    return pl.pallas_call(
        kernel,
        grid_spec=pltpu.PrefetchScalarGridSpec(
            num_scalar_prefetch=1,
            grid=(pairs,),
            in_specs=[col, tall, tall],
            out_specs=[col, pl.BlockSpec((1, 1, 2 * rows), lambda h, p: (h, 0, 0))],
            scratch_shapes=[stat, stat, pltpu.VMEM((PAIR, 2 * rows), f32)],
        ),
        out_shape=[
            jax.ShapeDtypeStruct(q.shape, bf16),
            jax.ShapeDtypeStruct((pairs, 1, 2 * rows), f32),
        ],
        compiler_params=params(),
        cost_estimate=cost(16 * total * q.size, 4 * q.size + 4 * k.size),
        name="cross_forward",
    )(length, q, k, v)


def length_mask(length_ref, s, start, sure):
    if start + s.shape[0] <= sure:
        return s
    key = lax.broadcasted_iota(jnp.int32, s.shape, 0) + start
    return jnp.where(key < length_ref[0], s, NEG)


def backward_setup(q_ref, o_ref, do_ref):
    qst = stack_heads(q_ref[...])
    dost = stack_heads(do_ref[...])
    qT, doT = qst.T, dost.T
    oT = o_ref[...].T.astype(f32)
    delta = jnp.sum(doT.astype(f32) * jnp.concatenate([oT, oT], axis=1), axis=0, keepdims=True)
    return qst, qT, dost, doT, delta


def backward_step(k, v, query, lse, mask):
    qst, qT, dost, doT, delta = query
    p = jnp.exp2(mask(dot(k, qT) * (SCALE * LOG2E)) - lse)
    ds = (p * (dot(v, doT) - delta)).astype(bf16)
    dv = dot(p.astype(bf16), dost).astype(bf16)
    dk = (dot(ds, qst) * SCALE).astype(bf16)
    return dk, dv, dot(k, ds, 0, 0)


def self_backward(place, q, ks, vs, o, do, lse, bias, blocks, dq_before):
    rows, count = q.shape[0], len(blocks)
    pairs = q.shape[1] // PAIR
    last = 0 in blocks
    given = dq_before is not None

    def kernel(place_ref, q_ref, *refs):
        k_refs, v_refs = refs[:count], refs[count : 2 * count]
        o_ref, do_ref, lse_ref, bias_ref = refs[2 * count : 2 * count + 4]
        rest = refs[2 * count + 4 :]
        before_ref, rest = (rest[0], rest[1:]) if given else (None, rest)
        dq_ref, dk_refs, dv_refs, dqT = rest[0], rest[1 : 1 + count], rest[1 + count : 1 + 2 * count], rest[-1]

        def work():
            query = backward_setup(q_ref, o_ref, do_ref)
            dqT[...] = jnp.zeros_like(dqT)
            for n, r in enumerate(blocks):
                def step(n=n, r=r):
                    dk, dv, dq = backward_step(
                        k_refs[n][...], v_refs[n][...], query, lse_ref[0],
                        lambda s: segment_bias(bias_ref, r, s, r == 0),
                    )
                    dk_refs[n][...] = dk
                    dv_refs[n][...] = dv
                    dqT[...] += dq
                if r == 0:
                    step()
                else:
                    pl.when(place_ref[0] >= r)(step)
            part = unstack_heads(dqT[...]) * SCALE
            if given:
                part = part + before_ref[...]
            dq_ref[...] = part.astype(dq_ref.dtype)

        for n, r in enumerate(blocks):
            if r > 0:
                @pl.when(place_ref[0] < r)
                def _(n=n):
                    dk_refs[n][...] = jnp.zeros_like(dk_refs[n])
                    dv_refs[n][...] = jnp.zeros_like(dv_refs[n])
        if last:
            work()
        else:
            pl.when(place_ref[0] >= min(blocks))(work)

            @pl.when(place_ref[0] < min(blocks))
            def _():
                dq_ref[...] = before_ref[...] if given else jnp.zeros_like(dq_ref)

    col = pl.BlockSpec((rows, PAIR), lambda h, p: (0, h))
    args = [q, *[ks[r] for r in blocks], *[vs[r] for r in blocks], o, do, lse, bias]
    specs = [col] * (3 + 2 * count) + [
        pl.BlockSpec((1, 1, 2 * rows), lambda h, p: (h, 0, 0)),
        pl.BlockSpec(bias.shape, lambda h, p: (0, 0)),
    ]
    if given:
        args.append(dq_before)
        specs.append(col)
    shape = jax.ShapeDtypeStruct(q.shape, bf16)
    out = pl.pallas_call(
        kernel,
        grid_spec=pltpu.PrefetchScalarGridSpec(
            num_scalar_prefetch=1,
            grid=(pairs,),
            in_specs=specs,
            out_specs=[col] * (1 + 2 * count),
            scratch_shapes=[pltpu.VMEM((PAIR, 2 * rows), f32)],
        ),
        out_shape=[jax.ShapeDtypeStruct(q.shape, bf16 if last else f32)] + [shape] * (2 * count),
        compiler_params=params(),
        cost_estimate=cost(40 * count * rows * q.size, 8 * q.size * (2 + count)),
        name="self_backward",
    )(place, *args)
    return out[0], out[1 : 1 + count], out[1 + count :]


def cross_backward(length, q, k, v, o, do, lse, sure):
    rows, total = q.shape[0], k.shape[0]
    pairs = q.shape[1] // PAIR

    def kernel(length_ref, q_ref, k_ref, v_ref, o_ref, do_ref, lse_ref, dq_ref, dk_ref, dv_ref, dqT):
        query = backward_setup(q_ref, o_ref, do_ref)
        for a in range(0, total, CHUNK):
            sl = slice(a, a + CHUNK)
            dk, dv, dq = backward_step(
                k_ref[sl, :], v_ref[sl, :], query, lse_ref[0],
                lambda s: length_mask(length_ref, s, a, sure),
            )
            dk_ref[sl, :] = dk
            dv_ref[sl, :] = dv
            if a == 0:
                dqT[...] = dq
            else:
                dqT[...] += dq
        dq_ref[...] = (unstack_heads(dqT[...]) * SCALE).astype(bf16)

    col = pl.BlockSpec((rows, PAIR), lambda h, p: (0, h))
    tall = pl.BlockSpec((total, PAIR), lambda h, p: (0, h))
    return pl.pallas_call(
        kernel,
        grid_spec=pltpu.PrefetchScalarGridSpec(
            num_scalar_prefetch=1,
            grid=(pairs,),
            in_specs=[col, tall, tall, col, col, pl.BlockSpec((1, 1, 2 * rows), lambda h, p: (h, 0, 0))],
            out_specs=[col, tall, tall],
            scratch_shapes=[pltpu.VMEM((PAIR, 2 * rows), f32)],
        ),
        out_shape=[
            jax.ShapeDtypeStruct(q.shape, bf16),
            jax.ShapeDtypeStruct(k.shape, bf16),
            jax.ShapeDtypeStruct(k.shape, bf16),
        ],
        compiler_params=params(),
        cost_estimate=cost(40 * total * q.size, 8 * q.size + 8 * k.size),
        name="cross_backward",
    )(length, q, k, v, o, do, lse)


ERFC = (0.254829592, -0.284496736, 1.421413741, -1.453152027, 1.061405429)


def gelu_pair(v):
    e = jnp.exp2(v * v * (-0.5 * LOG2E))
    t = 1.0 / (1.0 + jnp.abs(v) * (0.3275911 * 0.7071067811865476))
    a1, a2, a3, a4, a5 = (0.5 * a for a in ERFC)
    tail = ((((a5 * t + a4) * t + a3) * t + a2) * t + a1) * t * e
    cdf = jnp.where(v >= 0.0, 1.0 - tail, tail)
    return v * cdf, cdf + v * e * 0.3989422804014327


def feed_forward(low, pair, r0, r1, cots, lifts, ub, outs):
    rows, width = r0.shape
    part, count = lifts[0].shape[3], len(lifts)
    hidden = part * count
    given = 0 if outs is None else 1

    def kernel(low_ref, r0_ref, r1_ref, g_ref, *refs):
        w_refs, ub_ref = refs[:count], refs[count]
        out_ref, back0, back1, inner_ref, grad_ref, sums_ref, r_ref, back_s = refs[count + 1 + given :]
        i = pl.program_id(0)

        @pl.when(i == 0)
        def _():
            r_ref[...] = r0_ref[...]
            sums_ref[...] = jnp.zeros_like(sums_ref)

        @pl.when(i == 1)
        def _():
            r_ref[...] = r1_ref[...]

        ups = [w[:, 0].reshape(width, part) for w in w_refs]
        downs = [w[:, 1].reshape(width, part) for w in w_refs]
        out = back = None
        for n in range(count):
            cols = slice(n * part, (n + 1) * part)
            lifted = dot(r_ref[...], ups[n]) + ub_ref[:, cols]
            grad_inner = dot(g_ref[...], downs[n])
            value, slope = gelu_pair(lifted)
            inner_ref[:, cols] = value.astype(bf16)
            grad = (grad_inner * slope).astype(bf16)
            grad_ref[:, cols] = grad
            sums_ref[:, cols] += jnp.sum(grad.astype(f32), axis=0, keepdims=True)
        for n in range(count):
            cols = slice(n * part, (n + 1) * part)
            o = dot(inner_ref[:, cols], downs[n], 1, 1)
            b = dot(grad_ref[:, cols], ups[n], 1, 1)
            out, back = (o, b) if n == 0 else (out + o, back + b)
        out_ref[...] = out.astype(bf16)
        back_s[...] = back.astype(bf16)

        @pl.when(i == 0)
        def _():
            back0[...] = back_s[...]

        @pl.when(i == 1)
        def _():
            back1[...] = back_s[...]

    whole = lambda x: pl.BlockSpec(x.shape, lambda i, s: (0,) * x.ndim)
    row = jax.ShapeDtypeStruct((rows, width), bf16)
    tall = jax.ShapeDtypeStruct((2 * rows, hidden), bf16)
    tall_spec = pl.BlockSpec((rows, hidden), lambda i, s: (i, 0))
    by_device = pl.BlockSpec((rows, width), lambda i, s: (s[0] ^ (pair + i), 0))
    return pl.pallas_call(
        kernel,
        grid_spec=pltpu.PrefetchScalarGridSpec(
            num_scalar_prefetch=1,
            grid=(2,),
            in_specs=[whole(r0), whole(r1), by_device]
            + [whole(x) for x in lifts] + [whole(ub)]
            + [pl.BlockSpec(memory_space=pl.ANY)] * given,
            out_specs=[by_device] + [whole(r0)] * 2 + [tall_spec] * 2 + [whole(ub)],
            scratch_shapes=[pltpu.VMEM((rows, width), bf16)] * 2,
        ),
        out_shape=[jax.ShapeDtypeStruct(cots.shape, bf16)] + [row] * 2 + [tall] * 2
        + [jax.ShapeDtypeStruct(ub.shape, f32)],
        input_output_aliases={5 + count: 0} if given else {},
        compiler_params=params(),
        cost_estimate=cost(16 * rows * width * hidden, 24 * rows * width + 4 * hidden * width),
        name="feed_forward",
    )(low, r0, r1, cots, *lifts, ub, *([outs] if given else []))


def lift_grad(low, lefts, rights, place, before):
    ordered = not isinstance(rights, list)
    ins = [rights] if ordered else rights
    hidden, wide = lefts[0].shape[1], ins[0].shape[1]
    count = len(lefts)
    piece = lefts[0].shape[0] // 2
    tiles, given = 4, 0 if before is None else 4
    tile = hidden // tiles

    def kernel(low_ref, *refs):
        l_refs, r_refs = refs[:count], refs[count : count + len(ins)]
        out_refs = refs[count + len(ins) + given :]
        total = None
        for k in range(2 * count):
            if ordered:
                right = r_refs[0][pl.ds(pl.multiple_of((low_ref[0] ^ k) * piece, piece), piece), :]
            else:
                right = r_refs[k][...]
            start = (k % 2) * piece
            part = dot(l_refs[k // 2][start : start + piece, :], right, 0, 0)
            total = part if total is None else total + part
        total = total.astype(bf16)
        for n in range(tiles):
            @pl.when(pl.program_id(0) == n)
            def _(n=n):
                out_refs[n][0] = total

    depth = 2 * count * piece
    return pl.pallas_call(
        kernel,
        grid_spec=pltpu.PrefetchScalarGridSpec(
            num_scalar_prefetch=1,
            grid=(tiles,),
            in_specs=[pl.BlockSpec((2 * piece, tile), lambda i, s: (0, i))] * count
            + [pl.BlockSpec(x.shape, lambda i, s: (0, 0)) for x in ins]
            + [pl.BlockSpec(memory_space=pl.ANY)] * given,
            out_specs=[pl.BlockSpec((1, tile, wide), lambda i, s: (place, 0, 0))] * tiles,
        ),
        out_shape=[jax.ShapeDtypeStruct((2, tile, wide), bf16)] * tiles,
        input_output_aliases={1 + count + len(ins) + n: n for n in range(given)},
        compiler_params=params(),
        cost_estimate=cost(2 * depth * hidden * wide, 2 * depth * (hidden + wide) + 2 * hidden * wide),
        name="lift_grad",
    )(low, *lefts, *ins, *(before or ()))


def shard_grad(low, lefts, rights, column, columns, before):
    high, wide = lefts[0].shape[1], rights[0].shape[1]
    count = len(lefts)
    rows = high // 8
    given = 0 if before is None else 2

    def kernel(low_ref, *refs):
        even_ref, odd_ref = refs[2 * count + given :]
        total = None
        for l_ref, r_ref in zip(refs[:count], refs[count : 2 * count]):
            part = dot(l_ref[...], r_ref[...], 0, 0)
            total = part if total is None else total + part
        total = total.astype(bf16)

        @pl.when((low_ref[0] & 1) == 0)
        def _():
            even_ref[0] = total[:rows]
            odd_ref[0] = total[rows:]

        @pl.when((low_ref[0] & 1) == 1)
        def _():
            even_ref[0] = total[rows:]
            odd_ref[0] = total[:rows]

    depth = sum(x.shape[0] for x in lefts)
    shape = jax.ShapeDtypeStruct((4, rows, columns * wide), bf16)
    return pl.pallas_call(
        kernel,
        grid_spec=pltpu.PrefetchScalarGridSpec(
            num_scalar_prefetch=1,
            grid=(4,),
            in_specs=[pl.BlockSpec((x.shape[0], 2 * rows), lambda i, s: (0, i)) for x in lefts]
            + [pl.BlockSpec(x.shape, lambda i, s: (0, 0)) for x in rights]
            + [pl.BlockSpec(memory_space=pl.ANY)] * given,
            out_specs=[pl.BlockSpec((1, rows, wide), lambda i, s: ((s[0] >> 1) ^ i, 0, column))] * 2,
        ),
        out_shape=[shape] * 2,
        input_output_aliases={1 + 2 * count: 0, 2 + 2 * count: 1} if given else {},
        compiler_params=params(),
        cost_estimate=cost(2 * depth * high * wide, 2 * depth * (high + wide) + 2 * high * wide),
        name="shard_grad",
    )(low, *lefts, *rights, *(before or ()))


def pack_shards(shards, turned, up, down):
    rows, cols = shards[0].shape
    flat = [*shards, up, down]
    part = up.shape[1] // 8

    def kernel(*refs):
        up_ref, down_ref, out_ref, lift_ref = refs[len(shards) :]
        for i, ref in enumerate(refs[: len(shards)]):
            out_ref[:, i * cols : (i + 1) * cols] = ref[...].T if i in turned else ref[...]
        for d in range(8):
            span = slice(d * part, (d + 1) * part)
            lift_ref[d, 0] = up_ref[:, span]
            lift_ref[d, 1] = down_ref[span, :].T

    return pl.pallas_call(
        kernel,
        out_shape=[
            jax.ShapeDtypeStruct((rows, len(shards) * cols), bf16),
            jax.ShapeDtypeStruct((8, 2, rows, part), bf16),
        ],
        compiler_params=params(),
        cost_estimate=cost(0, 4 * sum(x.size for x in flat)),
        name="pack_shards",
    )(*flat)


def sum_columns(place, pieces, count, size):
    rows, wide = pieces[0].shape
    cols = wide // count
    part = cols // size

    def kernel(place_ref, *refs):
        ins, outs, total = refs[: len(pieces)], refs[len(pieces) : -1], refs[-1]
        acc = ins[0][...].astype(f32)
        for ref in ins[1:]:
            acc = acc + ref[...].astype(f32)
        total[...] = acc
        for r in range(size):
            start = lax.rem(place_ref[0] + size - r, size) * part
            for w in range(count):
                span = pl.ds(pl.multiple_of(w * cols + start, part), part)
                outs[r][:, w * part : (w + 1) * part] = total[:, span].astype(outs[r].dtype)

    return pl.pallas_call(
        kernel,
        grid_spec=pltpu.PrefetchScalarGridSpec(
            num_scalar_prefetch=1,
            grid=(1,),
            in_specs=[pl.BlockSpec(x.shape, lambda i, s: (0, 0)) for x in pieces],
            out_specs=[pl.BlockSpec((rows, count * part), lambda i, s: (0, 0))] * size,
            scratch_shapes=[pltpu.VMEM((rows, wide), f32)],
        ),
        out_shape=[jax.ShapeDtypeStruct((rows, count * part), f32 if r == 0 else bf16) for r in range(size)],
        compiler_params=params(),
        cost_estimate=cost(0, 4 * sum(x.size for x in pieces)),
        name="sum_columns",
    )(place, *pieces)


def normed(rows, gain, shift):
    average = jnp.mean(rows, axis=-1, keepdims=True)
    centered = rows - average
    variance = jnp.mean(centered * centered, axis=-1, keepdims=True)
    return (centered * lax.rsqrt(variance + EPSILON) * gain + shift).astype(bf16)


def centered_rows(rows):
    average = jnp.mean(rows, axis=-1, keepdims=True)
    centered = rows - average
    scale = lax.rsqrt(jnp.mean(centered * centered, axis=-1, keepdims=True) + EPSILON)
    return centered * scale, scale


def norm_back(rows, gain, grad):
    xhat, scale = centered_rows(rows)
    scaled = grad * gain
    return scale * (
        scaled
        - jnp.mean(scaled, axis=-1, keepdims=True)
        - xhat * jnp.mean(scaled * xhat, axis=-1, keepdims=True)
    )


def norm_sums(rows, grad):
    return jnp.sum(grad * centered_rows(rows)[0], axis=0), jnp.sum(grad, axis=0)


def column_sums(matrix):
    return jnp.sum(matrix.astype(f32), axis=0)


def together(*values):
    return lax.optimization_barrier(values)


def flip(x, k):
    return lax.ppermute(x, "low", [(i, i ^ k) for i in range(8)])


def wrap(value, size):
    return value % size if isinstance(value, int) else lax.rem(value, size)


def turn(x, r, size):
    return lax.ppermute(x, "tensor", [(i, (i + r) % size) for i in range(size)])


def gather_chips(x):
    return [x] + [flip(x, k) for k in (2, 4, 6)]


def gather_cores(even):
    return [p for e in even for p in (e, flip(e, 1))]


def by_place(pieces, place):
    size = len(pieces)
    return jnp.stack(
        [
            sum(jnp.where(lax.rem(place + size - r, size) == z, pieces[r], 0.0) for r in range(size))
            for z in range(size)
        ]
    )


def stack_shards(scalars, pieces, first, count):
    rows, wide = pieces[0].shape
    cut = wide // count * first
    every = slice(None)
    return move(
        "stack_shards", scalars, pieces, [(len(pieces), rows, cut), (len(pieces), rows, wide - cut)],
        lambda s: [
            (r, (every, pl.ds(start, extent)), part, (r, every, every))
            for r in range(len(pieces))
            for part, (start, extent) in enumerate([(0, cut), (cut, wide - cut)])
        ],
    )


def unpack_weights(scalars, pieces, count, sizes):
    size, rows, cols = pieces[0].shape
    cols //= count
    every = slice(None)

    def plan(s):
        return [
            (
                k, (r, every, pl.ds(w * cols, cols)),
                w, (at((s[0] ^ k) * rows, rows), at(wrap(s[1] + size - r, size) * cols, cols)),
            )
            for w in range(count) for k in range(8) for r in range(size)
        ]

    matrices = move("unpack_weights", scalars, pieces, [(8 * rows, size * cols)] * count, plan)
    if sizes[0] > 1:
        matrices = [lax.all_gather(m, "high", axis=0, tiled=True) for m in matrices]
    return matrices


def add_pair(a, b):
    return (a.astype(f32) + b.astype(f32)).astype(bf16)


def scatter_low(pieces):
    even = [add_pair(pieces[k], flip(pieces[k + 1], 1)) for k in (6, 4, 2)]
    back = [flip(e, k).astype(f32) for e, k in zip(even, (6, 4, 2))]
    own = pieces[0].astype(f32) + flip(pieces[1], 1).astype(f32)
    return own + back[0] + back[1] + back[2]


def shard_grads(low, grads):
    before = None
    for i, (lefts, rights) in enumerate(grads):
        before = shard_grad(low, lefts, rights, i, len(grads), before)
    return before


def whole_shards(parts, turned, count):
    shard = parts[0] + sum(x.astype(f32) for x in turned)
    return jnp.split(shard, count, axis=1)


def sum_vector(vector, sizes):
    size = sizes[2]
    if sizes[0] > 1:
        vector = lax.psum(vector, "high")
    slices = lax.all_to_all(vector.reshape(8, -1), "low", split_axis=0, concat_axis=0, tiled=True)
    mine = jnp.sum(slices, axis=0)
    mine = mine + sum(turn(mine, r, size) for r in range(1, size))
    spread = jnp.broadcast_to(mine, (8, *mine.shape))
    return lax.all_to_all(spread, "low", split_axis=0, concat_axis=0, tiled=True).reshape(-1)


def path_bias(parents, place, own, blocks):
    count = parents.shape[0]
    labels = jnp.arange(count)
    table = (
        (labels[:, None] == labels[None, :])
        | ((parents[:, None] == labels[None, :]) & (labels[:, None] > 0))
    ).astype(f32)
    reach = 1
    while reach < count:
        table = jnp.minimum(jnp.dot(table, table), 1.0)
        reach *= 2
    slots = jnp.arange(blocks * own)
    segment = (place - slots // own) * own + slots % own
    pick = (labels[:, None] == segment[None, :]).astype(f32)
    lanes = jnp.arange(2 * own * SEG)
    query = place * own + (lanes // SEG) % own
    mine = (labels[:, None] == query[None, :]).astype(f32)
    seen = jnp.dot(pick.T, jnp.dot(table.T, mine))
    return jnp.where(seen > 0.5, 0.0, NEG)


def on_device(sizes, sure):
    size = sizes[2]

    def run(
        tokens,
        encoded,
        parents,
        source_lengths,
        cotangent,
        first_gain,
        first_shift,
        self_query,
        self_query_bias,
        self_key,
        self_value,
        self_value_bias,
        self_out,
        self_out_bias,
        second_gain,
        second_shift,
        cross_query,
        cross_query_bias,
        cross_key,
        cross_value,
        cross_value_bias,
        cross_out,
        cross_out_bias,
        third_gain,
        third_shift,
        up_weight,
        up_bias,
        down_weight,
        down_bias,
    ):
        low = lax.axis_index("low")
        place = lax.axis_index("tensor")
        scalars = jnp.stack([low, place]).astype(jnp.int32)
        low_1, place_1 = scalars[:1], scalars[1:]
        rows, width = tokens.shape
        up_chain = [(i, i + 1) for i in range(size - 1)]
        down_chain = [(i + 1, i) for i in range(size - 1)]

        a, lift = pack_shards(
            [
                self_query, self_key, self_value,
                self_out, cross_query, cross_key, cross_value, cross_out,
            ],
            (3, 7), up_weight, down_weight,
        )
        z = [turn(a, r, size) for r in range(1, size)]
        blocks = [tokens, lax.ppermute(tokens, "tensor", up_chain)]
        ones = [normed(tokens.astype(f32), first_gain, first_shift)]
        bias = path_bias(parents[0], place, rows // SEG, size)
        part = width // size
        hidden = up_weight.shape[1] // 8
        biases = jnp.concatenate(
            [
                self_query_bias, self_value_bias, cross_query_bias, cross_value_bias,
                lax.dynamic_slice_in_dim(up_bias, low * hidden, hidden, 0),
            ]
        )
        biases = [biases] + [turn(biases, r, size) for r in range(1, size)]
        ub = jnp.concatenate([x[4 * part :] for x in biases])[None]
        placed = by_place([x[: 4 * part] for x in biases], place).reshape(size, 4, part)
        q_bias, v_bias, xq_bias, xv_bias = [placed[:, i].reshape(width) for i in range(4)]
        lift = lax.all_to_all(lift, "low", split_axis=0, concat_axis=0, tiled=True)
        if sizes[0] > 1:
            lift = lax.all_gather(lift, "high", axis=0, tiled=True)
        cots = lax.all_gather(cotangent, "low", axis=0, tiled=True)
        a, lift, z, blocks, ones, bias, ub, q_bias, v_bias, xq_bias, xv_bias = together(
            a, lift, z, blocks, ones, bias, ub, q_bias, v_bias, xq_bias, xv_bias
        )

        packed_a, packed_b = stack_shards(scalars, [a, *z], 3, 8)
        even_a = gather_chips(packed_a)
        blocks = blocks + [lax.ppermute(blocks[-1], "tensor", up_chain)]
        ones = ones + [normed(blocks[1].astype(f32), first_gain, first_shift)]
        even_a, packed_b, blocks, ones, encoded = together(even_a, packed_b, blocks, ones, encoded)

        all_a = gather_cores(even_a)
        even_b = gather_chips(packed_b)
        blocks = blocks + [lax.ppermute(blocks[-1], "tensor", up_chain)]
        source = lax.all_gather(encoded, "tensor", axis=0, tiled=True)
        wq, wk, wv = unpack_weights(scalars, all_a, 3, sizes)
        ones = ones + [normed(blocks[2].astype(f32), first_gain, first_shift)]
        q1 = (dot(ones[0], wq) + q_bias).astype(bf16)
        ks = [dot(n, wk).astype(bf16) for n in ones]
        vs = [(dot(n, wv) + v_bias).astype(bf16) for n in ones]
        state = self_forward(place_1, q1, ks, vs, bias, range(size - 1), None, False)
        even_b, blocks, state, lift = together(even_b, blocks, state, lift)

        lifts = [lift, turn(lift, 1, size)]
        all_b = gather_cores(even_b)
        ones = ones + [normed(blocks[size - 1].astype(f32), first_gain, first_shift)]
        ks = ks + [dot(ones[-1], wk).astype(bf16)]
        vs = vs + [(dot(ones[-1], wv) + v_bias).astype(bf16)]
        mixed_one, lse_one = self_forward(
            place_1, q1, ks, vs, bias, (size - 1,), state, True
        )
        mixed_one, all_b, lifts, source = together(mixed_one, all_b, lifts, source)

        lifts = lifts + [turn(lifts[-1], 1, size)]
        wo, xq, xk, xv, xo = unpack_weights(scalars, all_b, 5, sizes)
        hidden_one = tokens.astype(f32) + dot(mixed_one, wo, 1, 1) + self_out_bias
        two = normed(hidden_one, second_gain, second_shift)
        q2 = (dot(two, xq) + xq_bias).astype(bf16)
        k2 = dot(source, xk).astype(bf16)
        v2 = (dot(source, xv) + xv_bias).astype(bf16)
        q2, k2, v2, lifts = together(q2, k2, v2, lifts)

        lifts = lifts + [turn(lifts[-1], 1, size)]
        mixed_two, lse_two = cross_forward(source_lengths, q2, k2, v2, sure)
        hidden_two = hidden_one + dot(mixed_two, xo, 1, 1) + cross_out_bias
        three = normed(hidden_two, third_gain, third_shift)
        three, lifts = together(three, lifts)

        x2, x4 = flip(three, 2), flip(three, 4)
        c0 = flip(three, 1)
        outs, firsts, lasts, inners, grads, up_sums, threes = None, [], [], [], [], [], []
        evens = [three, x2, x4, None]
        for n, k in enumerate(range(0, 8, 2)):
            if n == 0:
                pair = (three, c0)
            elif n == 1:
                three_sent, x2, x4, firsts[0] = together(three, x2, x4, firsts[0])
                evens = [three, x2, x4, flip(three_sent, 6)]
                pair = (x2, flip(x2, 1))
            else:
                pair = (evens[n], flip(evens[n], 1))
                pair, firsts[n - 2], lasts[n - 2] = together(pair, firsts[n - 2], lasts[n - 2])
            threes += pair
            outs, back0, back1, inner, grad, sums = feed_forward(
                low_1, k, *pair, cots, lifts, ub, outs
            )
            firsts.append(back0)
            lasts.append(flip(back1, 1))
            inners.append(inner)
            grads.append(grad)
            up_sums.append(sums)
        own = firsts[0].astype(f32) + lasts[0].astype(f32)
        back = [add_pair(firsts[n], lasts[n]) for n in (1, 2)]
        grads, back = together(grads, back)
        back = [flip(back[0], 2), flip(back[1], 4)]
        lift_shares = lift_grad(low_1, grads, threes, 0, None)
        inners, lift_shares, firsts[3], lasts[3], back = together(
            inners, lift_shares, firsts[3], lasts[3], back
        )
        back.append(flip(add_pair(firsts[3], lasts[3]), 6))
        lift_shares = lift_grad(low_1, inners, cots, 1, lift_shares)
        lift_shares, back, own = together(lift_shares, back, own)
        grad_three = own + sum(x.astype(f32) for x in back)

        grad_hidden_two = cotangent.astype(f32) + norm_back(hidden_two, third_gain, grad_three)
        grad_two = grad_hidden_two.astype(bf16)
        do2 = dot(grad_two, xo).astype(bf16)
        do2, outs, lift_shares = together(do2, outs, lift_shares)

        out_sum = lax.psum_scatter(outs, "low", scatter_dimension=0, tiled=True)
        lift_got = turn(lift_shares[size - 1], size - 1, size)
        dq2, dk2, dv2 = cross_backward(source_lengths, q2, k2, v2, mixed_two, do2, lse_two, sure)
        dq2, dk2, dv2, lift_got = together(dq2, dk2, dv2, lift_got)

        lift_got = turn(add_pair(lift_shares[size - 2], lift_got), size - 1, size)
        grad_two_normed = dot(dq2, xq, 1, 1)
        grad_hidden_one = grad_hidden_two + norm_back(hidden_one, second_gain, grad_two_normed)
        grad_one = grad_hidden_one.astype(bf16)
        do1 = dot(grad_one, wo).astype(bf16)
        b_even, b_odd = shard_grads(
            low_1,
            [
                ([grad_one], [mixed_one]),
                ([two], [dq2]),
                ([source], [dk2]),
                ([source], [dv2]),
                ([grad_two], [mixed_two]),
            ],
        )
        encoded_part = (dot(dk2, xk, 1, 1) + dot(dv2, xv, 1, 1)).astype(bf16)
        spread = by_place([sum(up_sums)[0, r * hidden : (r + 1) * hidden] for r in range(size)], place)
        spread = lax.dynamic_update_slice(
            jnp.zeros((size, up_bias.shape[0]), f32), spread, (0, low * hidden)
        )
        early = jnp.concatenate(
            [
                *norm_sums(hidden_one, grad_two_normed),
                *norm_sums(hidden_two, grad_three),
                column_sums(grad_one),
                column_sums(grad_two),
                column_sums(cotangent),
                column_sums(dq2),
                column_sums(dv2),
                spread.reshape(-1),
            ]
        )
        do1, b_even, b_odd, lift_got, encoded_part, early = together(
            do1, b_even, b_odd, lift_got, encoded_part, early
        )

        lift_got = turn(add_pair(lift_shares[size - 3], lift_got), size - 1, size)
        if sizes[0] > 1:
            b_even, b_odd = [
                lax.psum_scatter(x, "high", scatter_dimension=1, tiled=True) for x in (b_even, b_odd)
            ]
        b_got = flip(b_odd, 1)
        early = sum_vector(early, sizes)
        dq, dks, dvs, shares = None, [None] * size, [None] * size, [None] * size
        share = None
        for group in [(r,) for r in range(size - 1, 1, -1)] + [(1, 0)]:
            dq, dk, dv = self_backward(
                place_1, q1, ks, vs, mixed_one, do1, lse_one, bias, group, dq
            )
            for n, r in enumerate(group):
                dks[r], dvs[r] = dk[n], dv[n]
                shares[r] = dot(dk[n], wk, 1, 1) + dot(dv[n], wv, 1, 1)
            r = group[0]
            if share is None:
                share, b_even, b_got, lift_got, do1 = together(shares[r], b_even, b_got, lift_got, do1)
                b_sums = [add_pair(b_even[p], b_got[p]) for p in range(4)]
                b_back = [flip(b_sums[p], 2 * p) for p in (1, 2, 3)]
                share = lax.ppermute(share.astype(bf16), "tensor", down_chain)
            elif r > 1:
                share, shares[r], do1 = together(share, shares[r], do1)
                share = lax.ppermute(add_pair(shares[r], share), "tensor", down_chain)
            else:
                share, shares, dq, dks, dvs, b_back, early = together(
                    share, shares, dq, dks, dvs, b_back, early
                )
                share = lax.ppermute(add_pair(shares[r], share), "tensor", down_chain)
        shares[0] = shares[0] + dot(dq, wq, 1, 1)
        b_parts = sum_columns(place_1, [b_sums[0], *b_back], 5, size)
        b_turned = [turn(b_parts[r], size - r, size) for r in range(1, size)]
        lift_sums = add_pair(lift_shares[0], lift_got)
        if sizes[0] > 1:
            lift_sums = lax.psum_scatter(lift_sums, "high", scatter_dimension=2, tiled=True)
        lift_sums = lax.all_to_all(lift_sums, "low", split_axis=2, concat_axis=1, tiled=True)
        a_even, a_odd = shard_grads(low_1, [([ones[0]], [dq]), (ones, dks), (ones, dvs)])
        own_sums = [norm_sums(x.astype(f32), s) for x, s in zip(blocks, shares)]
        late = jnp.concatenate(
            [
                sum(f[0] for f in own_sums),
                sum(f[1] for f in own_sums),
                column_sums(dq),
                sum(column_sums(v) for v in dvs),
            ]
        )
        a_even, a_odd, b_turned, share, shares, late, encoded_part = together(
            a_even, a_odd, b_turned, share, shares, late, encoded_part
        )

        if sizes[0] > 1:
            a_even, a_odd = [
                lax.psum_scatter(x, "high", scatter_dimension=1, tiled=True) for x in (a_even, a_odd)
            ]
        a_got = flip(a_odd, 1)
        a_sums = [add_pair(a_even[p], a_got[p]) for p in range(4)]
        a_back = [flip(a_sums[p], 2 * p) for p in (1, 2, 3)]
        encoded_grad = lax.psum_scatter(
            encoded_part, "tensor", scatter_dimension=0, tiled=True
        ).astype(f32)
        share = shares[0] + share.astype(f32)
        tokens_grad = grad_hidden_one + norm_back(tokens.astype(f32), first_gain, share)
        a_parts = sum_columns(place_1, [a_sums[0], *a_back], 3, size)
        a_turned = [turn(a_parts[r], size - r, size) for r in range(1, size)]
        wo_g, xq_g, xk_g, xv_g, xo_g = whole_shards(b_parts, b_turned, 5)
        wq_g, wk_g, wv_g = whole_shards(a_parts, a_turned, 3)
        block_out = hidden_two + out_sum.astype(f32) + down_bias
        up_weight_grad = lift_sums[0].T.astype(f32)
        down_weight_grad = lift_sums[1].astype(f32)

        late = sum_vector(late, sizes)
        small = [early[i * width : (i + 1) * width] for i in range(9)]
        small = [late[:width], late[width : 2 * width]] + small + [late[2 * width : 3 * width], late[3 * width :]]
        split = [lax.dynamic_slice_in_dim(s, place * part, part, 0) for s in (small[11], small[12], small[9], small[10])]
        up_bias_grad = lax.dynamic_slice_in_dim(
            early[9 * width :], place * up_bias.shape[0], up_bias.shape[0], 0
        )
        return (
            block_out.astype(bf16),
            tokens_grad,
            encoded_grad,
            small[0],
            small[1],
            wq_g,
            split[0],
            wk_g,
            wv_g,
            split[1],
            wo_g.T,
            small[6],
            small[2],
            small[3],
            xq_g,
            split[2],
            xk_g,
            xv_g,
            split[3],
            xo_g.T,
            small[7],
            small[4],
            small[5],
            up_weight_grad,
            up_bias_grad,
            down_weight_grad,
            small[8],
        )

    return run


def solution(mesh):
    dp, size = mesh.shape["dp"], mesh.shape["tensor"]
    sizes = (dp // 8, 8, size)
    fine = Mesh(mesh.devices.reshape(sizes), ("high", "low", "tensor"))
    depth = ("high", "low")
    rows = P((*depth, "tensor"), None)
    block, turned = P(depth, "tensor"), P("tensor", depth)
    part, whole = P("tensor"), P()
    placed = (
        rows, rows, P(depth, None), P(depth), rows, whole, whole,
        block, part, block, block, part, turned, whole, whole, whole,
        block, part, block, block, part, turned, whole, whole, whole,
        block, part, turned, whole,
    )
    out = (
        rows, rows, rows, whole, whole,
        block, part, block, block, part, turned, whole, whole, whole,
        block, part, block, block, part, turned, whole, whole, whole,
        block, part, turned, whole,
    )
    return jax.shard_map(
        on_device(sizes, 768), mesh=fine, in_specs=placed, out_specs=out, check_vma=False
    )
```

```python
import functools

import jax
import jax.numpy as jnp
from jax import lax
from jax.experimental import pallas as pl
from jax.experimental.pallas import tpu as pltpu
from jax.sharding import Mesh, PartitionSpec as P

HEAD_DIM = 64
SEG = 128
PAIR = 2 * HEAD_DIM
EPSILON = 1e-05
LOG2E = 1.4426950408889634
SCALE = HEAD_DIM ** -0.5
NEG = -1e30
CHUNK = 512
f32, bf16 = jnp.float32, jnp.bfloat16


def dot(a, b, ca=1, cb=0):
    return lax.dot_general(a, b, (((ca,), (cb,)), ((), ())), preferred_element_type=f32)


def cost(flops, moved):
    return pl.CostEstimate(flops=int(flops), bytes_accessed=int(moved), transcendentals=0)


def params(mib):
    return pltpu.CompilerParams(vmem_limit_bytes=mib * 1024 * 1024)


def move(name, scalars, sources, outs, plan):
    count = len(plan([0] * scalars.shape[0]))

    def kernel(scalars_ref, *refs):
        ins, dests, sems = refs[: len(sources)], refs[len(sources) : -1], refs[-1]
        values = [scalars_ref[i] for i in range(scalars.shape[0])]
        copies = [
            pltpu.make_async_copy(ins[a].at[ai], dests[b].at[bi], sems.at[n])
            for n, (a, ai, b, bi) in enumerate(plan(values))
        ]
        for copy in copies:
            copy.start()
        for copy in copies:
            copy.wait()

    anywhere = pl.BlockSpec(memory_space=pl.ANY)
    return pl.pallas_call(
        kernel,
        in_specs=[pl.BlockSpec(memory_space=pltpu.SMEM)]
        + [pl.BlockSpec(memory_space=pltpu.VMEM)] * len(sources),
        out_specs=[anywhere] * len(outs),
        out_shape=[jax.ShapeDtypeStruct(s, bf16) for s in outs],
        scratch_shapes=[pltpu.SemaphoreType.DMA((count,))],
        compiler_params=params(56),
        cost_estimate=cost(0, 4 * sum(x.size for x in sources)),
        name=name,
    )(scalars, *sources)


def at(start, extent):
    return pl.ds(start if isinstance(start, int) else pl.multiple_of(start, extent), extent)


def stack_heads(x):
    lane = lax.broadcasted_iota(jnp.int32, x.shape, 1)
    zero = jnp.zeros_like(x)
    return jnp.concatenate(
        [jnp.where(lane < HEAD_DIM, x, zero), jnp.where(lane >= HEAD_DIM, x, zero)], axis=0
    )


def unstack_heads(xt):
    n = xt.shape[1] // 2
    return jnp.concatenate([xt[:HEAD_DIM, :n], xt[HEAD_DIM:, n:]], axis=0).T


def segment_bias(bias_ref, block, s, causal):
    keys, wide = s.shape
    segs = keys // SEG
    b = jnp.concatenate(
        [
            jnp.broadcast_to(bias_ref[block * segs + j : block * segs + j + 1, :], (SEG, wide))
            for j in range(segs)
        ],
        0,
    )
    s = s + b
    if causal:
        key = lax.broadcasted_iota(jnp.int32, s.shape, 0)
        query = lax.broadcasted_iota(jnp.int32, s.shape, 1) & (wide // 2 - 1)
        s = jnp.where(key <= query, s, NEG)
    return s


def forward_step(k, v, qT, mask, m_ref, l_ref, acc, first):
    s = mask(dot(k, qT) * (SCALE * LOG2E))
    top = jnp.max(s, axis=0, keepdims=True)
    if first:
        p = jnp.exp2(s - top)
        m_ref[...] = top
        l_ref[...] = jnp.sum(p, axis=0, keepdims=True)
        acc[...] = dot(v, p.astype(bf16), 0, 0)
    else:
        m = jnp.maximum(m_ref[...], top)
        p = jnp.exp2(s - m)
        fade = jnp.exp2(m_ref[...] - m)
        m_ref[...] = m
        l_ref[...] = l_ref[...] * fade + jnp.sum(p, axis=0, keepdims=True)
        acc[...] = acc[...] * fade + dot(v, p.astype(bf16), 0, 0)


def forward_finish(o_ref, lse_ref, m_ref, l_ref, acc):
    o_ref[...] = unstack_heads(acc[...] * (1.0 / l_ref[...])).astype(bf16)
    lse_ref[0] = m_ref[...] + jnp.log2(l_ref[...])


def self_forward(place, q, ks, vs, bias, blocks, state, final):
    rows, count = q.shape[0], len(blocks)
    pairs = q.shape[1] // PAIR
    given = 0 if state is None else 3

    def kernel(place_ref, q_ref, *refs):
        k_refs, v_refs, bias_ref = refs[:count], refs[count : 2 * count], refs[2 * count]
        before = refs[2 * count + 1 : 2 * count + 1 + given]
        outs = refs[2 * count + 1 + given :]
        if final:
            o_ref, lse_ref, m_ref, l_ref, acc = outs
        else:
            m_out, l_out, acc_out, m_ref, l_ref, acc = outs
        if given:
            m_ref[...], l_ref[...], acc[...] = before[0][0], before[1][0], before[2][0]
        qT = stack_heads(q_ref[...]).T
        for n, r in enumerate(blocks):
            def step(n=n, r=r):
                forward_step(
                    k_refs[n][...], v_refs[n][...], qT,
                    lambda s: segment_bias(bias_ref, r, s, r == 0), m_ref, l_ref, acc, r == 0,
                )
            if r == 0:
                step()
            else:
                pl.when(place_ref[0] >= r)(step)
        if final:
            forward_finish(o_ref, lse_ref, m_ref, l_ref, acc)
        else:
            m_out[0], l_out[0], acc_out[0] = m_ref[...], l_ref[...], acc[...]

    col = pl.BlockSpec((rows, PAIR), lambda h, p: (0, h))
    line = pl.BlockSpec((1, 1, 2 * rows), lambda h, p: (h, 0, 0))
    slab = pl.BlockSpec((1, PAIR, 2 * rows), lambda h, p: (h, 0, 0))
    lines = jax.ShapeDtypeStruct((pairs, 1, 2 * rows), f32)
    slabs = jax.ShapeDtypeStruct((pairs, PAIR, 2 * rows), f32)
    stat = pltpu.VMEM((1, 2 * rows), f32)
    return pl.pallas_call(
        kernel,
        grid_spec=pltpu.PrefetchScalarGridSpec(
            num_scalar_prefetch=1,
            grid=(pairs,),
            in_specs=[col] * (1 + 2 * count)
            + [pl.BlockSpec(bias.shape, lambda h, p: (0, 0))]
            + [line, line, slab][:given],
            out_specs=[col, line] if final else [line, line, slab],
            scratch_shapes=[stat, stat, pltpu.VMEM((PAIR, 2 * rows), f32)],
        ),
        out_shape=[jax.ShapeDtypeStruct(q.shape, bf16), lines] if final else [lines, lines, slabs],
        compiler_params=params(56),
        cost_estimate=cost(16 * count * rows * q.size, 4 * q.size * (1 + count)),
        name="self_forward",
    )(place, q, *[ks[r] for r in blocks], *[vs[r] for r in blocks], bias, *(state or ()))


def cross_forward(length, q, k, v, sure):
    rows, total = q.shape[0], k.shape[0]
    pairs = q.shape[1] // PAIR

    def kernel(length_ref, q_ref, k_ref, v_ref, o_ref, lse_ref, m_ref, l_ref, acc):
        qT = stack_heads(q_ref[...]).T
        for a in range(0, total, CHUNK):
            sl = slice(a, a + CHUNK)
            forward_step(
                k_ref[sl, :], v_ref[sl, :], qT,
                lambda s: length_mask(length_ref, s, a, sure), m_ref, l_ref, acc, a == 0,
            )
        forward_finish(o_ref, lse_ref, m_ref, l_ref, acc)

    col = pl.BlockSpec((rows, PAIR), lambda h, p: (0, h))
    tall = pl.BlockSpec((total, PAIR), lambda h, p: (0, h))
    stat = pltpu.VMEM((1, 2 * rows), f32)
    return pl.pallas_call(
        kernel,
        grid_spec=pltpu.PrefetchScalarGridSpec(
            num_scalar_prefetch=1,
            grid=(pairs,),
            in_specs=[col, tall, tall],
            out_specs=[col, pl.BlockSpec((1, 1, 2 * rows), lambda h, p: (h, 0, 0))],
            scratch_shapes=[stat, stat, pltpu.VMEM((PAIR, 2 * rows), f32)],
        ),
        out_shape=[
            jax.ShapeDtypeStruct(q.shape, bf16),
            jax.ShapeDtypeStruct((pairs, 1, 2 * rows), f32),
        ],
        compiler_params=params(56),
        cost_estimate=cost(16 * total * q.size, 4 * q.size + 4 * k.size),
        name="cross_forward",
    )(length, q, k, v)


def length_mask(length_ref, s, start, sure):
    if start + s.shape[0] <= sure:
        return s
    key = lax.broadcasted_iota(jnp.int32, s.shape, 0) + start
    return jnp.where(key < length_ref[0], s, NEG)


def backward_setup(q_ref, o_ref, do_ref):
    qst = stack_heads(q_ref[...])
    dost = stack_heads(do_ref[...])
    qT, doT = qst.T, dost.T
    oT = o_ref[...].T.astype(f32)
    delta = jnp.sum(doT.astype(f32) * jnp.concatenate([oT, oT], axis=1), axis=0, keepdims=True)
    return qst, qT, dost, doT, delta


def backward_step(k, v, query, lse, mask):
    qst, qT, dost, doT, delta = query
    p = jnp.exp2(mask(dot(k, qT) * (SCALE * LOG2E)) - lse)
    ds = (p * (dot(v, doT) - delta)).astype(bf16)
    dv = dot(p.astype(bf16), dost).astype(bf16)
    dk = (dot(ds, qst) * SCALE).astype(bf16)
    return dk, dv, dot(k, ds, 0, 0)


def self_backward(place, q, ks, vs, o, do, lse, bias, blocks, dq_before):
    rows, count = q.shape[0], len(blocks)
    pairs = q.shape[1] // PAIR
    last = 0 in blocks
    given = dq_before is not None

    def kernel(place_ref, q_ref, *refs):
        k_refs, v_refs = refs[:count], refs[count : 2 * count]
        o_ref, do_ref, lse_ref, bias_ref = refs[2 * count : 2 * count + 4]
        rest = refs[2 * count + 4 :]
        before_ref, rest = (rest[0], rest[1:]) if given else (None, rest)
        dq_ref, dk_refs, dv_refs, dqT = rest[0], rest[1 : 1 + count], rest[1 + count : 1 + 2 * count], rest[-1]

        def work():
            query = backward_setup(q_ref, o_ref, do_ref)
            dqT[...] = jnp.zeros_like(dqT)
            for n, r in enumerate(blocks):
                def step(n=n, r=r):
                    dk, dv, dq = backward_step(
                        k_refs[n][...], v_refs[n][...], query, lse_ref[0],
                        lambda s: segment_bias(bias_ref, r, s, r == 0),
                    )
                    dk_refs[n][...] = dk
                    dv_refs[n][...] = dv
                    dqT[...] += dq
                if r == 0:
                    step()
                else:
                    pl.when(place_ref[0] >= r)(step)
            part = unstack_heads(dqT[...]) * SCALE
            if given:
                part = part + before_ref[...]
            dq_ref[...] = part.astype(dq_ref.dtype)

        for n, r in enumerate(blocks):
            if r > 0:
                @pl.when(place_ref[0] < r)
                def _(n=n):
                    dk_refs[n][...] = jnp.zeros_like(dk_refs[n])
                    dv_refs[n][...] = jnp.zeros_like(dv_refs[n])
        if last:
            work()
        else:
            pl.when(place_ref[0] >= min(blocks))(work)

            @pl.when(place_ref[0] < min(blocks))
            def _():
                dq_ref[...] = before_ref[...] if given else jnp.zeros_like(dq_ref)

    col = pl.BlockSpec((rows, PAIR), lambda h, p: (0, h))
    args = [q, *[ks[r] for r in blocks], *[vs[r] for r in blocks], o, do, lse, bias]
    specs = [col] * (3 + 2 * count) + [
        pl.BlockSpec((1, 1, 2 * rows), lambda h, p: (h, 0, 0)),
        pl.BlockSpec(bias.shape, lambda h, p: (0, 0)),
    ]
    if given:
        args.append(dq_before)
        specs.append(col)
    shape = jax.ShapeDtypeStruct(q.shape, bf16)
    out = pl.pallas_call(
        kernel,
        grid_spec=pltpu.PrefetchScalarGridSpec(
            num_scalar_prefetch=1,
            grid=(pairs,),
            in_specs=specs,
            out_specs=[col] * (1 + 2 * count),
            scratch_shapes=[pltpu.VMEM((PAIR, 2 * rows), f32)],
        ),
        out_shape=[jax.ShapeDtypeStruct(q.shape, bf16 if last else f32)] + [shape] * (2 * count),
        compiler_params=params(56),
        cost_estimate=cost(40 * count * rows * q.size, 8 * q.size * (2 + count)),
        name="self_backward",
    )(place, *args)
    return out[0], out[1 : 1 + count], out[1 + count :]


def cross_backward(length, q, k, v, o, do, lse, sure):
    rows, total = q.shape[0], k.shape[0]
    pairs = q.shape[1] // PAIR

    def kernel(length_ref, q_ref, k_ref, v_ref, o_ref, do_ref, lse_ref, dq_ref, dk_ref, dv_ref, dqT):
        query = backward_setup(q_ref, o_ref, do_ref)
        for a in range(0, total, CHUNK):
            sl = slice(a, a + CHUNK)
            dk, dv, dq = backward_step(
                k_ref[sl, :], v_ref[sl, :], query, lse_ref[0],
                lambda s: length_mask(length_ref, s, a, sure),
            )
            dk_ref[sl, :] = dk
            dv_ref[sl, :] = dv
            if a == 0:
                dqT[...] = dq
            else:
                dqT[...] += dq
        dq_ref[...] = (unstack_heads(dqT[...]) * SCALE).astype(bf16)

    col = pl.BlockSpec((rows, PAIR), lambda h, p: (0, h))
    tall = pl.BlockSpec((total, PAIR), lambda h, p: (0, h))
    return pl.pallas_call(
        kernel,
        grid_spec=pltpu.PrefetchScalarGridSpec(
            num_scalar_prefetch=1,
            grid=(pairs,),
            in_specs=[col, tall, tall, col, col, pl.BlockSpec((1, 1, 2 * rows), lambda h, p: (h, 0, 0))],
            out_specs=[col, tall, tall],
            scratch_shapes=[pltpu.VMEM((PAIR, 2 * rows), f32)],
        ),
        out_shape=[
            jax.ShapeDtypeStruct(q.shape, bf16),
            jax.ShapeDtypeStruct(k.shape, bf16),
            jax.ShapeDtypeStruct(k.shape, bf16),
        ],
        compiler_params=params(56),
        cost_estimate=cost(40 * total * q.size, 8 * q.size + 8 * k.size),
        name="cross_backward",
    )(length, q, k, v, o, do, lse)


ERFC = (0.254829592, -0.284496736, 1.421413741, -1.453152027, 1.061405429)


def gelu_pair(v):
    e = jnp.exp2(v * v * (-0.5 * LOG2E))
    t = 1.0 / (1.0 + jnp.abs(v) * (0.3275911 * 0.7071067811865476))
    a1, a2, a3, a4, a5 = (0.5 * a for a in ERFC)
    tail = ((((a5 * t + a4) * t + a3) * t + a2) * t + a1) * t * e
    cdf = jnp.where(v >= 0.0, 1.0 - tail, tail)
    return v * cdf, cdf + v * e * 0.3989422804014327


def feed_forward(low, pair, r0, r1, cots, lifts, ub, outs):
    rows, width = r0.shape
    part, count = lifts[0].shape[3], len(lifts)
    hidden = part * count
    given = 0 if outs is None else 1

    def kernel(low_ref, r0_ref, r1_ref, g_ref, *refs):
        w_refs, ub_ref = refs[:count], refs[count]
        out_ref, back0, back1, inner_ref, grad_ref, sums_ref, r_ref, back_s, inner_s, grad_s = refs[count + 1 + given :]
        i = pl.program_id(0)

        @pl.when(i == 0)
        def _():
            r_ref[...] = r0_ref[...]
            sums_ref[...] = jnp.zeros_like(sums_ref)

        @pl.when(i == 1)
        def _():
            r_ref[...] = r1_ref[...]

        ups = [w[:, 0].reshape(width, part) for w in w_refs]
        downs = [w[:, 1].reshape(width, part) for w in w_refs]
        out = back = None
        for n in range(count):
            cols = slice(n * part, (n + 1) * part)
            lifted = dot(r_ref[...], ups[n]) + ub_ref[:, cols]
            grad_inner = dot(g_ref[...], downs[n])
            value, slope = gelu_pair(lifted)
            inner = value.astype(bf16)
            grad = (grad_inner * slope).astype(bf16)
            inner_s[:, cols], grad_s[:, cols] = inner, grad
            inner_ref[cols, :], grad_ref[cols, :] = inner.T, grad.T
            sums_ref[:, cols] += jnp.sum(grad.astype(f32), axis=0, keepdims=True)
        for n in range(count):
            cols = slice(n * part, (n + 1) * part)
            o = dot(inner_s[:, cols], downs[n], 1, 1)
            b = dot(grad_s[:, cols], ups[n], 1, 1)
            out, back = (o, b) if n == 0 else (out + o, back + b)
        out_ref[...] = out.astype(bf16)
        back_s[...] = back.astype(bf16)

        @pl.when(i == 0)
        def _():
            back0[...] = back_s[...]

        @pl.when(i == 1)
        def _():
            back1[...] = back_s[...]

    whole = lambda x: pl.BlockSpec(x.shape, lambda i, s: (0,) * x.ndim)
    row = jax.ShapeDtypeStruct((rows, width), bf16)
    tall = jax.ShapeDtypeStruct((hidden, 2 * rows), bf16)
    tall_spec = pl.BlockSpec((hidden, rows), lambda i, s: (0, i))
    by_device = pl.BlockSpec((rows, width), lambda i, s: (s[0] ^ (pair[0] + (pair[1] - pair[0]) * i), 0))
    return pl.pallas_call(
        kernel,
        grid_spec=pltpu.PrefetchScalarGridSpec(
            num_scalar_prefetch=1,
            grid=(2,),
            in_specs=[whole(r0), whole(r1), by_device]
            + [whole(x) for x in lifts] + [whole(ub)]
            + [pl.BlockSpec(memory_space=pl.ANY)] * given,
            out_specs=[by_device] + [whole(r0)] * 2 + [tall_spec] * 2 + [whole(ub)],
            scratch_shapes=[pltpu.VMEM((rows, width), bf16)] * 2
            + [pltpu.VMEM((rows, hidden), bf16)] * 2,
        ),
        out_shape=[jax.ShapeDtypeStruct(cots.shape, bf16)] + [row] * 2 + [tall] * 2
        + [jax.ShapeDtypeStruct(ub.shape, f32)],
        input_output_aliases={5 + count: 0} if given else {},
        compiler_params=params(56),
        cost_estimate=cost(16 * rows * width * hidden, 24 * rows * width + 4 * hidden * width),
        name="feed_forward",
    )(low, r0, r1, cots, *lifts, ub, *([outs] if given else []))


def lift_grad(scalars, lefts, rights, order, half, before):
    ordered = not isinstance(rights, list)
    ins = [rights] if ordered else rights
    hidden, wide = lefts[0].shape[0], ins[0].shape[1]
    count = len(lefts)
    piece = lefts[0].shape[1] // 2
    tiles, given = 4, 0 if before is None else 4
    tile = hidden // tiles

    def kernel(scalars_ref, *refs):
        l_refs, r_refs = refs[: 2 * count], refs[2 * count : 2 * count + len(ins)]
        out_refs = refs[2 * count + len(ins) + given :]
        total = None
        for n in range(count):
            both = jnp.concatenate([l_refs[2 * n][...], l_refs[2 * n + 1][...]], axis=0)
            for h in range(2):
                if ordered:
                    start = (scalars_ref[0] ^ order[2 * n + h]) * piece
                    right = r_refs[0][pl.ds(pl.multiple_of(start, piece), piece), :]
                else:
                    right = r_refs[2 * n + h][...]
                part = dot(both[:, h * piece : (h + 1) * piece], right)
                total = part if total is None else total + part
        total = total.astype(bf16)
        for n in range(tiles):
            @pl.when(pl.program_id(0) == n // 2)
            def _(n=n):
                out_refs[n][0] = total[(n % 2) * tile : (n % 2 + 1) * tile]

    def quarter(h):
        return pl.BlockSpec((tile, 2 * piece), lambda i, s: (2 * i + h, 0))

    depth = 2 * count * piece
    return pl.pallas_call(
        kernel,
        grid_spec=pltpu.PrefetchScalarGridSpec(
            num_scalar_prefetch=1,
            grid=(2,),
            in_specs=[quarter(0), quarter(1)] * count
            + [pl.BlockSpec(x.shape, lambda i, s: (0, 0)) for x in ins]
            + [pl.BlockSpec(memory_space=pl.ANY)] * given,
            out_specs=[pl.BlockSpec((1, tile, wide), lambda i, s: (half, 0, 0))] * tiles,
        ),
        out_shape=[jax.ShapeDtypeStruct((2, tile, wide), bf16)] * tiles,
        input_output_aliases={1 + 2 * count + len(ins) + n: n for n in range(given)},
        compiler_params=params(56),
        cost_estimate=cost(2 * depth * hidden * wide, 2 * depth * (hidden + wide) + 2 * hidden * wide),
        name="lift_grad",
    )(scalars, *[x for left in lefts for x in (left, left)], *ins, *(before or ()))


def shard_grads(low, products):
    lefts = [x for p in products for x in p[0]]
    rights = [x for p in products for x in p[1]]
    spans = []
    for p in products:
        start = spans[-1][1] if spans else 0
        spans.append((start, start + len(p[0])))
    count, wide = len(lefts), rights[0].shape[1]
    rows = lefts[0].shape[1] // 8

    def kernel(low_ref, *refs):
        l_refs, r_refs = refs[:count], refs[count : 2 * count]
        even_ref, odd_ref = refs[2 * count : 2 * count + 2]
        bufs, sems = refs[2 * count + 2 : -1], refs[-1]
        step = pl.program_id(0)
        copies = [pltpu.make_async_copy(r_refs[n], bufs[n], sems.at[n]) for n in range(count)]

        @pl.when(step == 0)
        def _():
            for copy in copies:
                copy.start()

        for p, (start, stop) in enumerate(spans):
            @pl.when(step == 2 * p)
            def _(start=start, stop=stop):
                for n in range(start, stop):
                    copies[n].wait()

            @pl.when(step // 2 == p)
            def _(start=start, stop=stop):
                total = None
                for n in range(start, stop):
                    part = dot(l_refs[n][...], bufs[n][...], 0, 0)
                    total = part if total is None else total + part
                total = total.astype(bf16)
                swap = (low_ref[0] & 1) == 1
                for h in range(2):
                    first = total[2 * h * rows : (2 * h + 1) * rows]
                    second = total[(2 * h + 1) * rows : (2 * h + 2) * rows]
                    spot = ((low_ref[0] >> 1) & 1) ^ h
                    even_ref[spot] = jnp.where(swap, second, first)
                    odd_ref[spot] = jnp.where(swap, first, second)

    def tile(p):
        return lambda i, s: (0, jnp.clip(i - 2 * p, 0, 1))

    specs = [
        pl.BlockSpec((lefts[n].shape[0], 4 * rows), tile(p))
        for p, (start, stop) in enumerate(spans)
        for n in range(start, stop)
    ]
    depth = sum(x.shape[0] for x in lefts)
    shape = jax.ShapeDtypeStruct((4, rows, len(products) * wide), bf16)
    return pl.pallas_call(
        kernel,
        grid_spec=pltpu.PrefetchScalarGridSpec(
            num_scalar_prefetch=1,
            grid=(2 * len(products),),
            in_specs=specs + [pl.BlockSpec(memory_space=pl.ANY)] * count,
            out_specs=[pl.BlockSpec((2, rows, wide), lambda i, s: ((s[0] >> 2) ^ (i % 2), 0, i // 2))] * 2,
            scratch_shapes=[pltpu.VMEM(x.shape, bf16) for x in rights] + [pltpu.SemaphoreType.DMA((count,))],
        ),
        out_shape=[shape] * 2,
        compiler_params=params(56),
        cost_estimate=cost(16 * depth * rows * wide, 2 * depth * (8 * rows + wide)),
        name="shard_grads",
    )(low, *lefts, *rights)


def pack_shards(ones, twos, up, down):
    rows, cols = ones[0].shape
    flat = [*ones, *twos, up, down]
    part = up.shape[1] // 8

    def kernel(*refs):
        one_refs, two_refs = refs[: len(ones)], refs[len(ones) : len(ones) + len(twos)]
        up_ref, down_ref, out_one, out_two, out_lift = refs[len(flat) - 2 :]
        for i, ref in enumerate(one_refs):
            out_one[:, i * cols : (i + 1) * cols] = ref[...]
        for i, ref in enumerate(two_refs):
            x = ref[...].T if i in (0, len(twos) - 1) else ref[...]
            out_two[:, i * cols : (i + 1) * cols] = x
        for d in range(8):
            span = slice(d * part, (d + 1) * part)
            out_lift[d, 0] = up_ref[:, span]
            out_lift[d, 1] = down_ref[span, :].T

    return pl.pallas_call(
        kernel,
        out_shape=[
            jax.ShapeDtypeStruct((rows, len(ones) * cols), bf16),
            jax.ShapeDtypeStruct((rows, len(twos) * cols), bf16),
            jax.ShapeDtypeStruct((8, 2, rows, part), bf16),
        ],
        compiler_params=params(56),
        cost_estimate=cost(0, 4 * sum(x.size for x in flat)),
        name="pack_shards",
    )(*flat)


def sum_columns(place, pieces, count, size):
    rows, wide = pieces[0].shape
    cols = wide // count
    part = cols // size

    def kernel(place_ref, *refs):
        ins, outs, total = refs[: len(pieces)], refs[len(pieces) : -1], refs[-1]
        acc = ins[0][...].astype(f32)
        for ref in ins[1:]:
            acc = acc + ref[...].astype(f32)
        total[...] = acc
        for r in range(size):
            start = lax.rem(place_ref[0] + size - r, size) * part
            for w in range(count):
                span = pl.ds(pl.multiple_of(w * cols + start, part), part)
                outs[r][:, w * part : (w + 1) * part] = total[:, span].astype(outs[r].dtype)

    return pl.pallas_call(
        kernel,
        grid_spec=pltpu.PrefetchScalarGridSpec(
            num_scalar_prefetch=1,
            grid=(1,),
            in_specs=[pl.BlockSpec(x.shape, lambda i, s: (0, 0)) for x in pieces],
            out_specs=[pl.BlockSpec((rows, count * part), lambda i, s: (0, 0))] * size,
            scratch_shapes=[pltpu.VMEM((rows, wide), f32)],
        ),
        out_shape=[jax.ShapeDtypeStruct((rows, count * part), f32 if r == 0 else bf16) for r in range(size)],
        compiler_params=params(56),
        cost_estimate=cost(0, 4 * sum(x.size for x in pieces)),
        name="sum_columns",
    )(place, *pieces)


def row_sums(x):
    return jnp.mean(x, axis=-1, keepdims=True)


def norm_backward(rows, gain, pieces, residual, sums, tile=128):
    count, width = rows.shape

    def kernel(rows_ref, gain_ref, residual_ref, *refs):
        grads, outs = refs[: len(pieces)], refs[len(pieces) :]
        x = rows_ref[...].astype(f32)
        centered = x - row_sums(x)
        scale = lax.rsqrt(row_sums(centered * centered) + EPSILON)
        xhat = centered * scale
        grad = grads[0][...].astype(f32)
        for g in grads[1:]:
            grad = grad + g[...].astype(f32)
        scaled = grad * gain_ref[...]
        back = scale * (scaled - row_sums(scaled) - xhat * row_sums(scaled * xhat))
        out = residual_ref[...].astype(f32) + back
        outs[0][...] = out
        if sums:
            short = out.astype(bf16)
            outs[1][...] = short

            @pl.when(pl.program_id(0) == 0)
            def _():
                outs[2][...] = jnp.zeros_like(outs[2])

            for n, v in enumerate((grad * xhat, grad, short.astype(f32))):
                outs[2][n : n + 1, :] += jnp.sum(v, axis=0, keepdims=True)

    row = pl.BlockSpec((tile, width), lambda i: (i, 0))
    shape = jax.ShapeDtypeStruct((count, width), f32)
    return pl.pallas_call(
        kernel,
        grid=(count // tile,),
        in_specs=[row, pl.BlockSpec((1, width), lambda i: (0, 0)), row] + [row] * len(pieces),
        out_specs=[row, row, pl.BlockSpec((3, width), lambda i: (0, 0))] if sums else [row],
        out_shape=[
            shape,
            jax.ShapeDtypeStruct((count, width), bf16),
            jax.ShapeDtypeStruct((3, width), f32),
        ]
        if sums
        else [shape],
        compiler_params=params(56),
        cost_estimate=cost(0, 12 * rows.size),
        name="norm_backward",
    )(rows, gain[None], residual, *pieces)


def share_grad(grads, weights, rows, before, final):
    count, width = rows.shape
    tile = count
    given = 0 if before is None else 1

    def kernel(*refs):
        g_refs, w_refs = refs[: len(grads)], refs[len(grads) : 2 * len(grads)]
        rows_ref, rest = refs[2 * len(grads)], refs[2 * len(grads) + 1 :]
        out_ref, sums_ref = rest[given:]
        share = dot(g_refs[0][...], w_refs[0][...], 1, 1)
        for g, w in zip(g_refs[1:], w_refs[1:]):
            share = share + dot(g[...], w[...], 1, 1)
        x = rows_ref[...].astype(f32)
        centered = x - row_sums(x)
        xhat = centered * lax.rsqrt(row_sums(centered * centered) + EPSILON)

        sums_ref[0:1, :] = jnp.sum(share * xhat, axis=0, keepdims=True)
        sums_ref[1:2, :] = jnp.sum(share, axis=0, keepdims=True)
        if given:
            share = share + rest[0][...].astype(f32)
        out_ref[...] = share.astype(out_ref.dtype)

    row = pl.BlockSpec((tile, width), lambda i: (i, 0))
    return pl.pallas_call(
        kernel,
        grid=(1,),
        in_specs=[row] * len(grads)
        + [pl.BlockSpec(w.shape, lambda i: (0, 0)) for w in weights]
        + [row] * (1 + given),
        out_specs=[row, pl.BlockSpec((2, width), lambda i: (0, 0))],
        out_shape=[
            jax.ShapeDtypeStruct((count, width), f32 if final else bf16),
            jax.ShapeDtypeStruct((2, width), f32),
        ],
        compiler_params=params(56),
        cost_estimate=cost(2 * len(grads) * count * width * width, 6 * rows.size),
        name="share_grad",
    )(*grads, *weights, rows, *([before] if given else []))


def normed(rows, gain, shift):
    average = jnp.mean(rows, axis=-1, keepdims=True)
    centered = rows - average
    variance = jnp.mean(centered * centered, axis=-1, keepdims=True)
    return (centered * lax.rsqrt(variance + EPSILON) * gain + shift).astype(bf16)


def centered_rows(rows):
    average = jnp.mean(rows, axis=-1, keepdims=True)
    centered = rows - average
    scale = lax.rsqrt(jnp.mean(centered * centered, axis=-1, keepdims=True) + EPSILON)
    return centered * scale, scale


def norm_back(rows, gain, grad):
    xhat, scale = centered_rows(rows)
    scaled = grad * gain
    return scale * (
        scaled
        - jnp.mean(scaled, axis=-1, keepdims=True)
        - xhat * jnp.mean(scaled * xhat, axis=-1, keepdims=True)
    )


def norm_sums(rows, grad):
    return jnp.sum(grad * centered_rows(rows)[0], axis=0), jnp.sum(grad, axis=0)


def column_sums(matrix):
    return jnp.sum(matrix.astype(f32), axis=0)


def together(*values):
    return lax.optimization_barrier(values)


def flip(x, k):
    return lax.ppermute(x, "low", [(i, i ^ k) for i in range(8)])


def wrap(value, size):
    return value % size if isinstance(value, int) else lax.rem(value, size)


def turn(x, r, size):
    return lax.ppermute(x, "tensor", [(i, (i + r) % size) for i in range(size)])


def gather_chips(x):
    return [x] + [flip(x, k) for k in (2, 4, 6)]


def gather_cores(even):
    return [p for e in even for p in (e, flip(e, 1))]


def by_place(pieces, place):
    size = len(pieces)
    return jnp.stack(
        [
            sum(jnp.where(lax.rem(place + size - r, size) == z, pieces[r], 0.0) for r in range(size))
            for z in range(size)
        ]
    )


def stack_shards(scalars, pieces):
    (stacked,) = move(
        "stack_shards", scalars, pieces, [(len(pieces), *pieces[0].shape)],
        lambda s: [(r, (slice(None), slice(None)), 0, (r,)) for r in range(len(pieces))],
    )
    return stacked


def unpack_weights(scalars, pieces, count, sizes):
    size, rows, cols = pieces[0].shape
    cols //= count
    every = slice(None)

    def plan(s):
        return [
            (
                k, (r, every, pl.ds(w * cols, cols)),
                w, (at((s[0] ^ k) * rows, rows), at(wrap(s[1] + size - r, size) * cols, cols)),
            )
            for w in range(count) for k in range(8) for r in range(size)
        ]

    matrices = move("unpack_weights", scalars, pieces, [(8 * rows, size * cols)] * count, plan)
    if sizes[0] > 1:
        matrices = [lax.all_gather(m, "high", axis=0, tiled=True) for m in matrices]
    return matrices


def add_pair(a, b):
    return (a.astype(f32) + b.astype(f32)).astype(bf16)


def scatter_low(pieces):
    even = [add_pair(pieces[k], flip(pieces[k + 1], 1)) for k in (6, 4, 2)]
    back = [flip(e, k).astype(f32) for e, k in zip(even, (6, 4, 2))]
    own = pieces[0].astype(f32) + flip(pieces[1], 1).astype(f32)
    return own + back[0] + back[1] + back[2]


def whole_shards(parts, turned, count):
    shard = parts[0] + sum(x.astype(f32) for x in turned)
    return jnp.split(shard, count, axis=1)


def sum_tensor(vector, sizes):
    if sizes[0] > 1:
        vector = lax.psum(vector, "high")
    return vector + sum(turn(vector, r, sizes[2]) for r in range(1, sizes[2]))


def sum_low(vector):
    spread = jnp.broadcast_to(vector, (8, *vector.shape))
    return jnp.sum(lax.all_to_all(spread, "low", split_axis=0, concat_axis=0, tiled=True), axis=0)


def path_bias(parents, place, own, blocks):
    count = parents.shape[0]
    labels = jnp.arange(count)
    table = (
        (labels[:, None] == labels[None, :])
        | ((parents[:, None] == labels[None, :]) & (labels[:, None] > 0))
    ).astype(f32)
    reach = 1
    while reach < count:
        table = jnp.minimum(jnp.dot(table, table), 1.0)
        reach *= 2
    slots = jnp.arange(blocks * own)
    segment = (place - slots // own) * own + slots % own
    pick = (labels[:, None] == segment[None, :]).astype(f32)
    lanes = jnp.arange(2 * own * SEG)
    query = place * own + (lanes // SEG) % own
    mine = (labels[:, None] == query[None, :]).astype(f32)
    seen = jnp.dot(pick.T, jnp.dot(table.T, mine))
    return jnp.where(seen > 0.5, 0.0, NEG)


def on_device(sizes, sure):
    size = sizes[2]

    def run(
        tokens,
        encoded,
        parents,
        source_lengths,
        cotangent,
        first_gain,
        first_shift,
        self_query,
        self_query_bias,
        self_key,
        self_value,
        self_value_bias,
        self_out,
        self_out_bias,
        second_gain,
        second_shift,
        cross_query,
        cross_query_bias,
        cross_key,
        cross_value,
        cross_value_bias,
        cross_out,
        cross_out_bias,
        third_gain,
        third_shift,
        up_weight,
        up_bias,
        down_weight,
        down_bias,
    ):
        low = lax.axis_index("low")
        place = lax.axis_index("tensor")
        scalars = jnp.stack([low, place]).astype(jnp.int32)
        low_1, place_1 = scalars[:1], scalars[1:]
        rows, width = tokens.shape
        up_chain = [(i, i + 1) for i in range(size - 1)]
        down_chain = [(i + 1, i) for i in range(size - 1)]

        first, second, lift = pack_shards(
            [self_query, self_key, self_value],
            [self_out, cross_query, cross_key, cross_value, cross_out],
            up_weight, down_weight,
        )
        part = width // size
        hidden = up_weight.shape[1] // 8
        z = [turn(first, r, size) for r in range(1, size)]
        ones = [normed(tokens.astype(f32), first_gain, first_shift)]
        bias = path_bias(parents[0], place, rows // SEG, size)
        lift = lax.all_to_all(lift, "low", split_axis=0, concat_axis=0, tiled=True)
        if sizes[0] > 1:
            lift = lax.all_gather(lift, "high", axis=0, tiled=True)
        first, second, z, ones, bias, tokens_sent = together(first, second, z, ones, bias, tokens)

        even_a = gather_chips(stack_shards(scalars, [first, *z]))
        blocks = [tokens, lax.ppermute(tokens_sent, "tensor", up_chain)]
        z = [turn(second, 1, size)]
        biases = jnp.concatenate(
            [
                self_query_bias, self_value_bias, cross_query_bias, cross_value_bias,
                lax.dynamic_slice_in_dim(up_bias, low * hidden, hidden, 0),
            ]
        )
        biases = [biases] + [turn(biases, r, size) for r in range(1, size)]
        ub = jnp.concatenate([x[4 * part :] for x in biases])[None]
        placed = by_place([x[: 4 * part] for x in biases], place).reshape(size, 4, part)
        q_bias, v_bias, xq_bias, xv_bias = [placed[:, i].reshape(width) for i in range(4)]
        even_a, second, z[0], blocks, ub, q_bias, v_bias, xq_bias, xv_bias, encoded, lift = together(
            even_a, second, z[0], blocks, ub, q_bias, v_bias, xq_bias, xv_bias, encoded, lift
        )

        all_a = gather_cores(even_a)
        blocks.append(lax.ppermute(blocks[-1], "tensor", up_chain))
        source = lax.all_gather(encoded, "tensor", axis=0, tiled=True)
        z = z + [turn(second, r, size) for r in range(2, size)]
        wq, wk, wv = unpack_weights(scalars, all_a, 3, sizes)
        q1 = (dot(ones[0], wq) + q_bias).astype(bf16)
        ks, vs, state, mixed_one = [], [], None, None
        for r in range(size):
            if r:
                ones.append(normed(blocks[r].astype(f32), first_gain, first_shift))
            ks.append(dot(ones[r], wk).astype(bf16))
            vs.append((dot(ones[r], wv) + v_bias).astype(bf16))
            if r == 0:
                continue
            if r == 1:
                q1, ks, vs, second, z = together(q1, ks, vs, second, z)
                packed_b = stack_shards(scalars, [second, *z])
                even_b = [packed_b, flip(packed_b, 2), flip(packed_b, 4)]
            seen = (0, 1) if r == 1 else (r,)
            if r < size - 1:
                state = self_forward(place_1, q1, ks, vs, bias, seen, state, False)
            else:
                mixed_one, lse_one = self_forward(place_1, q1, ks, vs, bias, seen, state, True)
            if r == 1:
                state, blocks, even_b = together(state, blocks, even_b)
                even_b.append(flip(even_b[0], 6))
                blocks.append(lax.ppermute(blocks[-1], "tensor", up_chain))
            elif r < size - 1:
                if r < size - 2:
                    blocks.append(lax.ppermute(blocks[-1], "tensor", up_chain))
                state, blocks, even_b, cots_sent, lift = together(
                    state, blocks, even_b, cotangent, lift
                )
                cots = lax.all_gather(cots_sent, "low", axis=0, tiled=True)
                all_b = gather_cores(even_b)
                lifts = [lift, turn(lift, 1, size)]
        mixed_one, all_b, lifts = together(mixed_one, all_b, lifts)
        lifts = lifts + [turn(lifts[-1], 1, size)]

        wo, xq, xk, xv, xo = unpack_weights(scalars, all_b, 5, sizes)
        hidden_one = tokens.astype(f32) + dot(mixed_one, wo, 1, 1) + self_out_bias
        two = normed(hidden_one, second_gain, second_shift)
        q2 = (dot(two, xq) + xq_bias).astype(bf16)
        k2 = dot(source, xk).astype(bf16)
        v2 = (dot(source, xv) + xv_bias).astype(bf16)
        q2, k2, v2, lifts = together(q2, k2, v2, lifts)

        lifts = lifts + [turn(lifts[-1], 1, size)]
        mixed_two, lse_two = cross_forward(source_lengths, q2, k2, v2, sure)
        hidden_two = hidden_one + dot(mixed_two, xo, 1, 1) + cross_out_bias
        three = normed(hidden_two, third_gain, third_shift)
        three, lifts = together(three, lifts)

        x2, x4, c0 = flip(three, 2), flip(three, 4), flip(three, 1)

        def lift_pair(pair, r0, r1, outs):
            return feed_forward(low_1, pair, r0, r1, cots, lifts, ub, outs)

        outs, own, got, inner_0, grad_0, sums_0 = lift_pair((0, 1), three, c0, None)
        own_got = flip(got, 1)
        three_sent, x2, x4, own = together(three, x2, x4, own)
        c2, c4, x6 = flip(x2, 1), flip(x4, 1), flip(three_sent, 6)
        outs, back_2, back_4, inner_1, grad_1, sums_1 = lift_pair((2, 4), x2, x4, outs)
        c2, c4, back_2, own_got = together(c2, c4, back_2, own_got)
        outs, got_2, got_4, inner_2, grad_2, sums_2 = lift_pair((3, 5), c2, c4, outs)
        x6, got_2 = together(x6, got_2)
        got_2, got_4, c6 = flip(got_2, 1), flip(got_4, 1), flip(x6, 1)
        outs, back_6, got_6, inner_3, grad_3, sums_3 = lift_pair((6, 7), x6, c6, outs)
        back_6, got_2, got_4 = together(back_6, got_2, got_4)
        back_2, back_4 = flip(add_pair(back_2, got_2), 2), flip(add_pair(back_4, got_4), 4)
        got_6 = flip(got_6, 1)
        order = (0, 1, 2, 4, 3, 5, 6, 7)
        lift_shares = lift_grad(
            scalars, [grad_0, grad_1, grad_2, grad_3], [three, c0, x2, x4, c2, c4, x6, c6], order, 0, None
        )
        back_6, got_6, back_2, back_4, lift_shares = together(
            back_6, got_6, back_2, back_4, lift_shares
        )
        back_6 = flip(add_pair(back_6, got_6), 6)
        lift_shares = lift_grad(
            scalars, [inner_0, inner_1, inner_2, inner_3], cots, order, 1, lift_shares
        )
        up_sums = [sums_0, sums_1, sums_2, sums_3]
        lift_shares, back_6 = together(lift_shares, back_6)
        grad_hidden_two, grad_two, sums_three = norm_backward(
            hidden_two, third_gain, [own, own_got, back_2, back_4, back_6], cotangent, True
        )
        do2 = dot(grad_two, xo).astype(bf16)
        do2, outs, lift_shares = together(do2, outs, lift_shares)

        out_sum = lax.psum_scatter(outs, "low", scatter_dimension=0, tiled=True)
        lift_got = turn(lift_shares[size - 1], size - 1, size)
        dq2, dk2, dv2 = cross_backward(source_lengths, q2, k2, v2, mixed_two, do2, lse_two, sure)
        dq2, dk2, dv2, lift_got = together(dq2, dk2, dv2, lift_got)

        lift_got = turn(add_pair(lift_shares[size - 2], lift_got), size - 1, size)
        grad_hidden_one, grad_one, sums_two = norm_backward(
            hidden_one, second_gain, [dot(dq2, xq, 1, 1)], grad_hidden_two, True
        )
        do1 = dot(grad_one, wo).astype(bf16)
        encoded_part = (dot(dk2, xk, 1, 1) + dot(dv2, xv, 1, 1)).astype(bf16)
        early = column_sums(cotangent), column_sums(dq2), column_sums(dv2)
        do1, lift_got, encoded_part, early = together(do1, lift_got, encoded_part, early)

        lift_got = turn(add_pair(lift_shares[size - 3], lift_got), size - 1, size)
        b_laid = shard_grads(
            low_1,
            [
                ([grad_one], [mixed_one]),
                ([two], [dq2]),
                ([source], [dk2]),
                ([source], [dv2]),
                ([grad_two], [mixed_two]),
            ],
        )
        spread = by_place([sum(up_sums)[0, r * hidden : (r + 1) * hidden] for r in range(size)], place)
        spread = lax.dynamic_update_slice(
            jnp.zeros((size, up_bias.shape[0]), f32), spread, (0, low * hidden)
        )
        early = jnp.concatenate(
            [
                sums_two.reshape(-1),
                sums_three.reshape(-1),
                *early,
                spread.reshape(-1),
            ]
        )
        (b_even, b_odd), do1, lift_got, encoded_part, early = together(
            b_laid, do1, lift_got, encoded_part, early
        )

        if sizes[0] > 1:
            b_even, b_odd = [
                lax.psum_scatter(x, "high", scatter_dimension=1, tiled=True) for x in (b_even, b_odd)
            ]
        b_got = flip(b_odd, 1)
        early = sum_tensor(early, sizes)
        lift_sums = add_pair(lift_shares[0], lift_got)
        if sizes[0] > 1:
            lift_sums = lax.psum_scatter(lift_sums, "high", scatter_dimension=2, tiled=True)
        lift_sums = lax.all_to_all(lift_sums, "low", split_axis=2, concat_axis=1, tiled=True)
        encoded_sum = lax.psum_scatter(encoded_part, "tensor", scatter_dimension=0, tiled=True)
        dq, dks, dvs, own_sums, share = None, [None] * size, [None] * size, [], None
        for group in [(r,) for r in range(size - 1, 1, -1)] + [(1, 0)]:
            r = group[0]
            dq, dk, dv = self_backward(
                place_1, q1, ks, vs, mixed_one, do1, lse_one, bias, group, dq
            )
            for n, s in enumerate(group):
                dks[s], dvs[s] = dk[n], dv[n]
            if r > 1:
                share, sums = share_grad([dk[0], dv[0]], [wk, wv], blocks[r], share, False)
                own_sums.append(sums)
            if r == size - 1:
                share, do1, b_even, b_got, early, out_sum, lift_sums = together(
                    share, do1, b_even, b_got, early, out_sum, lift_sums
                )
                share = lax.ppermute(share, "tensor", down_chain)
                b_sums = [add_pair(b_even[p], b_got[p]) for p in range(4)]
                b_back = [flip(b_sums[p], 2 * p) for p in (1, 2, 3)]
            elif r > 1:
                share, do1, encoded_sum = together(share, do1, encoded_sum)
                share = lax.ppermute(share, "tensor", down_chain)
        share, sums = share_grad([dk[0], dv[0]], [wk, wv], blocks[1], share, False)
        own_sums.append(sums)
        share, dq, dks, dvs, b_back, early = together(share, dq, dks, dvs, b_back, early)
        share = lax.ppermute(share, "tensor", down_chain)
        a_even, a_odd = shard_grads(low_1, [([ones[0]], [dq]), (ones, dks), (ones, dvs)])
        if sizes[0] > 1:
            a_even, a_odd = [
                lax.psum_scatter(x, "high", scatter_dimension=1, tiled=True) for x in (a_even, a_odd)
            ]
        a_even, a_odd, share, dq, dks, dvs, b_sums, b_back = together(
            a_even, a_odd, share, dq, dks, dvs, b_sums, b_back
        )

        a_got = flip(a_odd, 1)
        own_share, sums = share_grad([dks[0], dvs[0], dq], [wk, wv, wq], tokens, None, True)
        own_sums.append(sums)
        a_even, a_got, own_share, own_sums, share, b_sums, b_back = together(
            a_even, a_got, own_share, own_sums, share, b_sums, b_back
        )
        a_sums = [add_pair(a_even[p], a_got[p]) for p in range(4)]
        a_sums, own_sums, own_share, share, b_sums, b_back, dq, dvs = together(
            a_sums, own_sums, own_share, share, b_sums, b_back, dq, dvs
        )
        a_back = [flip(a_sums[p], 2 * p) for p in (1, 2, 3)]
        b_parts = sum_columns(place_1, [b_sums[0], *b_back], 5, size)
        b_turned = [turn(b_parts[r], size - r, size) for r in range(1, size)]
        (tokens_grad,) = norm_backward(tokens, first_gain, [own_share, share], grad_hidden_one, False)
        late = jnp.concatenate(
            [sum(own_sums).reshape(-1), column_sums(dq), sum(column_sums(v) for v in dvs)]
        )
        late = sum_tensor(late, sizes)
        a_back, b_turned, late, tokens_grad, out_sum, lift_sums = together(
            a_back, b_turned, late, tokens_grad, out_sum, lift_sums
        )
        a_parts = sum_columns(place_1, [a_sums[0], *a_back], 3, size)
        a_turned = [turn(a_parts[r], size - r, size) for r in range(1, size)]
        vectors = sum_low(jnp.concatenate([early, late]))
        early, late = vectors[: early.shape[0]], vectors[early.shape[0] :]
        encoded_grad = encoded_sum.astype(f32)
        wo_g, xq_g, xk_g, xv_g, xo_g = whole_shards(b_parts, b_turned, 5)
        wq_g, wk_g, wv_g = whole_shards(a_parts, a_turned, 3)
        block_out = hidden_two + out_sum.astype(f32) + down_bias
        up_weight_grad = lift_sums[0].T.astype(f32)
        down_weight_grad = lift_sums[1].astype(f32)

        small = [early[i * width : (i + 1) * width] for i in range(9)]
        small = [late[:width], late[width : 2 * width]] + [small[i] for i in (0, 1, 3, 4, 2, 5, 6, 7, 8)]
        small = small + [late[2 * width : 3 * width], late[3 * width :]]
        split = [lax.dynamic_slice_in_dim(s, place * part, part, 0) for s in (small[11], small[12], small[9], small[10])]
        up_bias_grad = lax.dynamic_slice_in_dim(
            early[9 * width :], place * up_bias.shape[0], up_bias.shape[0], 0
        )
        return (
            block_out.astype(bf16),
            tokens_grad,
            encoded_grad,
            small[0],
            small[1],
            wq_g,
            split[0],
            wk_g,
            wv_g,
            split[1],
            wo_g.T,
            small[6],
            small[2],
            small[3],
            xq_g,
            split[2],
            xk_g,
            xv_g,
            split[3],
            xo_g.T,
            small[7],
            small[4],
            small[5],
            up_weight_grad,
            up_bias_grad,
            down_weight_grad,
            small[8],
        )

    return run


def solution(mesh):
    dp, size = mesh.shape["dp"], mesh.shape["tensor"]
    sizes = (dp // 8, 8, size)
    fine = Mesh(mesh.devices.reshape(sizes), ("high", "low", "tensor"))
    depth = ("high", "low")
    rows = P((*depth, "tensor"), None)
    block, turned = P(depth, "tensor"), P("tensor", depth)
    part, whole = P("tensor"), P()
    placed = (
        rows, rows, P(depth, None), P(depth), rows, whole, whole,
        block, part, block, block, part, turned, whole, whole, whole,
        block, part, block, block, part, turned, whole, whole, whole,
        block, part, turned, whole,
    )
    out = (
        rows, rows, rows, whole, whole,
        block, part, block, block, part, turned, whole, whole, whole,
        block, part, block, block, part, turned, whole, whole, whole,
        block, part, turned, whole,
    )
    return jax.shard_map(
        on_device(sizes, 768), mesh=fine, in_specs=placed, out_specs=out, check_vma=False
    )
```

```python
import functools

import jax
import jax.numpy as jnp
from jax import lax
from jax.experimental import pallas as pl
from jax.experimental.pallas import tpu as pltpu
from jax.sharding import Mesh, PartitionSpec as P

HEAD_DIM = 64
SEG = 128
PAIR = 2 * HEAD_DIM
EPSILON = 1e-05
LOG2E = 1.4426950408889634
SCALE = HEAD_DIM ** -0.5
NEG = -1e30
CHUNK = 512
f32, bf16 = jnp.float32, jnp.bfloat16


def dot(a, b, ca=1, cb=0):
    return lax.dot_general(a, b, (((ca,), (cb,)), ((), ())), preferred_element_type=f32)


def cost(flops, moved):
    return pl.CostEstimate(flops=int(flops), bytes_accessed=int(moved), transcendentals=0)


def params(mib):
    return pltpu.CompilerParams(vmem_limit_bytes=mib * 1024 * 1024)


def move(name, scalars, sources, outs, plan):
    count = len(plan([0] * scalars.shape[0]))

    def kernel(scalars_ref, *refs):
        ins, dests, sems = refs[: len(sources)], refs[len(sources) : -1], refs[-1]
        values = [scalars_ref[i] for i in range(scalars.shape[0])]
        copies = [
            pltpu.make_async_copy(ins[a].at[ai], dests[b].at[bi], sems.at[n])
            for n, (a, ai, b, bi) in enumerate(plan(values))
        ]
        for copy in copies:
            copy.start()
        for copy in copies:
            copy.wait()

    anywhere = pl.BlockSpec(memory_space=pl.ANY)
    return pl.pallas_call(
        kernel,
        in_specs=[pl.BlockSpec(memory_space=pltpu.SMEM)]
        + [pl.BlockSpec(memory_space=pltpu.VMEM)] * len(sources),
        out_specs=[anywhere] * len(outs),
        out_shape=[jax.ShapeDtypeStruct(s, bf16) for s in outs],
        scratch_shapes=[pltpu.SemaphoreType.DMA((count,))],
        compiler_params=params(56),
        cost_estimate=cost(0, 4 * sum(x.size for x in sources)),
        name=name,
    )(scalars, *sources)


def at(start, extent):
    return pl.ds(start if isinstance(start, int) else pl.multiple_of(start, extent), extent)


def stack_heads(x):
    lane = lax.broadcasted_iota(jnp.int32, x.shape, 1)
    zero = jnp.zeros_like(x)
    return jnp.concatenate(
        [jnp.where(lane < HEAD_DIM, x, zero), jnp.where(lane >= HEAD_DIM, x, zero)], axis=0
    )


def unstack_heads(xt):
    n = xt.shape[1] // 2
    return jnp.concatenate([xt[:HEAD_DIM, :n], xt[HEAD_DIM:, n:]], axis=0).T


def segment_bias(bias_ref, block, s, causal):
    keys, wide = s.shape
    segs = keys // SEG
    b = jnp.concatenate(
        [
            jnp.broadcast_to(bias_ref[block * segs + j : block * segs + j + 1, :], (SEG, wide))
            for j in range(segs)
        ],
        0,
    )
    s = s + b
    if causal:
        key = lax.broadcasted_iota(jnp.int32, s.shape, 0)
        query = lax.broadcasted_iota(jnp.int32, s.shape, 1) & (wide // 2 - 1)
        s = jnp.where(key <= query, s, NEG)
    return s


def forward_step(k, v, qT, mask, m_ref, l_ref, acc, first):
    s = mask(dot(k, qT) * (SCALE * LOG2E))
    top = jnp.max(s, axis=0, keepdims=True)
    if first:
        p = jnp.exp2(s - top)
        m_ref[...] = top
        l_ref[...] = jnp.sum(p, axis=0, keepdims=True)
        acc[...] = dot(v, p.astype(bf16), 0, 0)
    else:
        m = jnp.maximum(m_ref[...], top)
        p = jnp.exp2(s - m)
        fade = jnp.exp2(m_ref[...] - m)
        m_ref[...] = m
        l_ref[...] = l_ref[...] * fade + jnp.sum(p, axis=0, keepdims=True)
        acc[...] = acc[...] * fade + dot(v, p.astype(bf16), 0, 0)


def forward_finish(o_ref, lse_ref, m_ref, l_ref, acc):
    o_ref[...] = unstack_heads(acc[...] * (1.0 / l_ref[...])).astype(bf16)
    lse_ref[0] = m_ref[...] + jnp.log2(l_ref[...])


def self_forward(place, q, ks, vs, bias, blocks, state, final):
    rows, count = q.shape[0], len(blocks)
    pairs = q.shape[1] // PAIR
    given = 0 if state is None else 3

    def kernel(place_ref, q_ref, *refs):
        k_refs, v_refs, bias_ref = refs[:count], refs[count : 2 * count], refs[2 * count]
        before = refs[2 * count + 1 : 2 * count + 1 + given]
        outs = refs[2 * count + 1 + given :]
        if final:
            o_ref, lse_ref, m_ref, l_ref, acc = outs
        else:
            m_out, l_out, acc_out, m_ref, l_ref, acc = outs
        if given:
            m_ref[...], l_ref[...], acc[...] = before[0][0], before[1][0], before[2][0]
        qT = stack_heads(q_ref[...]).T
        for n, r in enumerate(blocks):
            def step(n=n, r=r):
                forward_step(
                    k_refs[n][...], v_refs[n][...], qT,
                    lambda s: segment_bias(bias_ref, r, s, r == 0), m_ref, l_ref, acc, r == 0,
                )
            if r == 0:
                step()
            else:
                pl.when(place_ref[0] >= r)(step)
        if final:
            forward_finish(o_ref, lse_ref, m_ref, l_ref, acc)
        else:
            m_out[0], l_out[0], acc_out[0] = m_ref[...], l_ref[...], acc[...]

    col = pl.BlockSpec((rows, PAIR), lambda h, p: (0, h))
    line = pl.BlockSpec((1, 1, 2 * rows), lambda h, p: (h, 0, 0))
    slab = pl.BlockSpec((1, PAIR, 2 * rows), lambda h, p: (h, 0, 0))
    lines = jax.ShapeDtypeStruct((pairs, 1, 2 * rows), f32)
    slabs = jax.ShapeDtypeStruct((pairs, PAIR, 2 * rows), f32)
    stat = pltpu.VMEM((1, 2 * rows), f32)
    return pl.pallas_call(
        kernel,
        grid_spec=pltpu.PrefetchScalarGridSpec(
            num_scalar_prefetch=1,
            grid=(pairs,),
            in_specs=[col] * (1 + 2 * count)
            + [pl.BlockSpec(bias.shape, lambda h, p: (0, 0))]
            + [line, line, slab][:given],
            out_specs=[col, line] if final else [line, line, slab],
            scratch_shapes=[stat, stat, pltpu.VMEM((PAIR, 2 * rows), f32)],
        ),
        out_shape=[jax.ShapeDtypeStruct(q.shape, bf16), lines] if final else [lines, lines, slabs],
        compiler_params=params(56),
        cost_estimate=cost(16 * count * rows * q.size, 4 * q.size * (1 + count)),
        name="self_forward",
    )(place, q, *[ks[r] for r in blocks], *[vs[r] for r in blocks], bias, *(state or ()))


def cross_forward(length, q, k, v, sure):
    rows, total = q.shape[0], k.shape[0]
    pairs = q.shape[1] // PAIR

    def kernel(length_ref, q_ref, k_ref, v_ref, o_ref, lse_ref, m_ref, l_ref, acc):
        qT = stack_heads(q_ref[...]).T
        for a in range(0, total, CHUNK):
            sl = slice(a, a + CHUNK)
            forward_step(
                k_ref[sl, :], v_ref[sl, :], qT,
                lambda s: length_mask(length_ref, s, a, sure), m_ref, l_ref, acc, a == 0,
            )
        forward_finish(o_ref, lse_ref, m_ref, l_ref, acc)

    col = pl.BlockSpec((rows, PAIR), lambda h, p: (0, h))
    tall = pl.BlockSpec((total, PAIR), lambda h, p: (0, h))
    stat = pltpu.VMEM((1, 2 * rows), f32)
    return pl.pallas_call(
        kernel,
        grid_spec=pltpu.PrefetchScalarGridSpec(
            num_scalar_prefetch=1,
            grid=(pairs,),
            in_specs=[col, tall, tall],
            out_specs=[col, pl.BlockSpec((1, 1, 2 * rows), lambda h, p: (h, 0, 0))],
            scratch_shapes=[stat, stat, pltpu.VMEM((PAIR, 2 * rows), f32)],
        ),
        out_shape=[
            jax.ShapeDtypeStruct(q.shape, bf16),
            jax.ShapeDtypeStruct((pairs, 1, 2 * rows), f32),
        ],
        compiler_params=params(56),
        cost_estimate=cost(16 * total * q.size, 4 * q.size + 4 * k.size),
        name="cross_forward",
    )(length, q, k, v)


def length_mask(length_ref, s, start, sure):
    if start + s.shape[0] <= sure:
        return s
    key = lax.broadcasted_iota(jnp.int32, s.shape, 0) + start
    return jnp.where(key < length_ref[0], s, NEG)


def backward_setup(q_ref, o_ref, do_ref):
    qst = stack_heads(q_ref[...])
    dost = stack_heads(do_ref[...])
    qT, doT = qst.T, dost.T
    oT = o_ref[...].T.astype(f32)
    delta = jnp.sum(doT.astype(f32) * jnp.concatenate([oT, oT], axis=1), axis=0, keepdims=True)
    return qst, qT, dost, doT, delta


def backward_step(k, v, query, lse, mask):
    qst, qT, dost, doT, delta = query
    p = jnp.exp2(mask(dot(k, qT) * (SCALE * LOG2E)) - lse)
    ds = (p * (dot(v, doT) - delta)).astype(bf16)
    dv = dot(p.astype(bf16), dost).astype(bf16)
    dk = (dot(ds, qst) * SCALE).astype(bf16)
    return dk, dv, dot(k, ds, 0, 0)


def self_backward(place, q, ks, vs, o, do, lse, bias, blocks, dq_before):
    rows, count = q.shape[0], len(blocks)
    pairs = q.shape[1] // PAIR
    last = 0 in blocks
    given = dq_before is not None

    def kernel(place_ref, q_ref, *refs):
        k_refs, v_refs = refs[:count], refs[count : 2 * count]
        o_ref, do_ref, lse_ref, bias_ref = refs[2 * count : 2 * count + 4]
        rest = refs[2 * count + 4 :]
        before_ref, rest = (rest[0], rest[1:]) if given else (None, rest)
        dq_ref, dk_refs, dv_refs, dqT = rest[0], rest[1 : 1 + count], rest[1 + count : 1 + 2 * count], rest[-1]

        def work():
            query = backward_setup(q_ref, o_ref, do_ref)
            dqT[...] = jnp.zeros_like(dqT)
            for n, r in enumerate(blocks):
                def step(n=n, r=r):
                    dk, dv, dq = backward_step(
                        k_refs[n][...], v_refs[n][...], query, lse_ref[0],
                        lambda s: segment_bias(bias_ref, r, s, r == 0),
                    )
                    dk_refs[n][...] = dk
                    dv_refs[n][...] = dv
                    dqT[...] += dq
                if r == 0:
                    step()
                else:
                    pl.when(place_ref[0] >= r)(step)
            part = unstack_heads(dqT[...]) * SCALE
            if given:
                part = part + before_ref[...]
            dq_ref[...] = part.astype(dq_ref.dtype)

        for n, r in enumerate(blocks):
            if r > 0:
                @pl.when(place_ref[0] < r)
                def _(n=n):
                    dk_refs[n][...] = jnp.zeros_like(dk_refs[n])
                    dv_refs[n][...] = jnp.zeros_like(dv_refs[n])
        if last:
            work()
        else:
            pl.when(place_ref[0] >= min(blocks))(work)

            @pl.when(place_ref[0] < min(blocks))
            def _():
                dq_ref[...] = before_ref[...] if given else jnp.zeros_like(dq_ref)

    col = pl.BlockSpec((rows, PAIR), lambda h, p: (0, h))
    args = [q, *[ks[r] for r in blocks], *[vs[r] for r in blocks], o, do, lse, bias]
    specs = [col] * (3 + 2 * count) + [
        pl.BlockSpec((1, 1, 2 * rows), lambda h, p: (h, 0, 0)),
        pl.BlockSpec(bias.shape, lambda h, p: (0, 0)),
    ]
    if given:
        args.append(dq_before)
        specs.append(col)
    shape = jax.ShapeDtypeStruct(q.shape, bf16)
    out = pl.pallas_call(
        kernel,
        grid_spec=pltpu.PrefetchScalarGridSpec(
            num_scalar_prefetch=1,
            grid=(pairs,),
            in_specs=specs,
            out_specs=[col] * (1 + 2 * count),
            scratch_shapes=[pltpu.VMEM((PAIR, 2 * rows), f32)],
        ),
        out_shape=[jax.ShapeDtypeStruct(q.shape, bf16 if last else f32)] + [shape] * (2 * count),
        compiler_params=params(56),
        cost_estimate=cost(40 * count * rows * q.size, 8 * q.size * (2 + count)),
        name="self_backward",
    )(place, *args)
    return out[0], out[1 : 1 + count], out[1 + count :]


def cross_backward(length, q, k, v, o, do, lse, sure):
    rows, total = q.shape[0], k.shape[0]
    pairs = q.shape[1] // PAIR

    def kernel(length_ref, q_ref, k_ref, v_ref, o_ref, do_ref, lse_ref, dq_ref, dk_ref, dv_ref, dqT):
        query = backward_setup(q_ref, o_ref, do_ref)
        for a in range(0, total, CHUNK):
            sl = slice(a, a + CHUNK)
            dk, dv, dq = backward_step(
                k_ref[sl, :], v_ref[sl, :], query, lse_ref[0],
                lambda s: length_mask(length_ref, s, a, sure),
            )
            dk_ref[sl, :] = dk
            dv_ref[sl, :] = dv
            if a == 0:
                dqT[...] = dq
            else:
                dqT[...] += dq
        dq_ref[...] = (unstack_heads(dqT[...]) * SCALE).astype(bf16)

    col = pl.BlockSpec((rows, PAIR), lambda h, p: (0, h))
    tall = pl.BlockSpec((total, PAIR), lambda h, p: (0, h))
    return pl.pallas_call(
        kernel,
        grid_spec=pltpu.PrefetchScalarGridSpec(
            num_scalar_prefetch=1,
            grid=(pairs,),
            in_specs=[col, tall, tall, col, col, pl.BlockSpec((1, 1, 2 * rows), lambda h, p: (h, 0, 0))],
            out_specs=[col, tall, tall],
            scratch_shapes=[pltpu.VMEM((PAIR, 2 * rows), f32)],
        ),
        out_shape=[
            jax.ShapeDtypeStruct(q.shape, bf16),
            jax.ShapeDtypeStruct(k.shape, bf16),
            jax.ShapeDtypeStruct(k.shape, bf16),
        ],
        compiler_params=params(56),
        cost_estimate=cost(40 * total * q.size, 8 * q.size + 8 * k.size),
        name="cross_backward",
    )(length, q, k, v, o, do, lse)


ERFC = (0.254829592, -0.284496736, 1.421413741, -1.453152027, 1.061405429)


def gelu_pair(v):
    e = jnp.exp2(v * v * (-0.5 * LOG2E))
    t = 1.0 / (1.0 + jnp.abs(v) * (0.3275911 * 0.7071067811865476))
    a1, a2, a3, a4, a5 = (0.5 * a for a in ERFC)
    tail = ((((a5 * t + a4) * t + a3) * t + a2) * t + a1) * t * e
    cdf = jnp.where(v >= 0.0, 1.0 - tail, tail)
    return v * cdf, cdf + v * e * 0.3989422804014327


def feed_forward(low, pair, r0, r1, cots, lifts, ub, outs):
    rows, width = r0.shape
    part, count = lifts[0].shape[3], len(lifts)
    hidden = part * count
    given = 0 if outs is None else 1

    def kernel(low_ref, r0_ref, r1_ref, g_ref, *refs):
        w_refs, ub_ref = refs[:count], refs[count]
        out_ref, back0, back1, inner_ref, grad_ref, sums_ref, r_ref, back_s, inner_s, grad_s = refs[count + 1 + given :]
        i = pl.program_id(0)

        @pl.when(i == 0)
        def _():
            r_ref[...] = r0_ref[...]
            sums_ref[...] = jnp.zeros_like(sums_ref)

        @pl.when(i == 1)
        def _():
            r_ref[...] = r1_ref[...]

        ups = [w[:, 0].reshape(width, part) for w in w_refs]
        downs = [w[:, 1].reshape(width, part) for w in w_refs]
        out = back = None
        for n in range(count):
            cols = slice(n * part, (n + 1) * part)
            lifted = dot(r_ref[...], ups[n]) + ub_ref[:, cols]
            grad_inner = dot(g_ref[...], downs[n])
            value, slope = gelu_pair(lifted)
            inner = value.astype(bf16)
            grad = (grad_inner * slope).astype(bf16)
            inner_s[:, cols], grad_s[:, cols] = inner, grad
            inner_ref[cols, :], grad_ref[cols, :] = inner.T, grad.T
            sums_ref[:, cols] += jnp.sum(grad.astype(f32), axis=0, keepdims=True)
        for n in range(count):
            cols = slice(n * part, (n + 1) * part)
            o = dot(inner_s[:, cols], downs[n], 1, 1)
            b = dot(grad_s[:, cols], ups[n], 1, 1)
            out, back = (o, b) if n == 0 else (out + o, back + b)
        out_ref[...] = out.astype(bf16)
        back_s[...] = back.astype(bf16)

        @pl.when(i == 0)
        def _():
            back0[...] = back_s[...]

        @pl.when(i == 1)
        def _():
            back1[...] = back_s[...]

    whole = lambda x: pl.BlockSpec(x.shape, lambda i, s: (0,) * x.ndim)
    row = jax.ShapeDtypeStruct((rows, width), bf16)
    tall = jax.ShapeDtypeStruct((hidden, 2 * rows), bf16)
    tall_spec = pl.BlockSpec((hidden, rows), lambda i, s: (0, i))
    by_device = pl.BlockSpec((rows, width), lambda i, s: (s[0] ^ (pair[0] + (pair[1] - pair[0]) * i), 0))
    return pl.pallas_call(
        kernel,
        grid_spec=pltpu.PrefetchScalarGridSpec(
            num_scalar_prefetch=1,
            grid=(2,),
            in_specs=[whole(r0), whole(r1), by_device]
            + [whole(x) for x in lifts] + [whole(ub)]
            + [pl.BlockSpec(memory_space=pl.ANY)] * given,
            out_specs=[by_device] + [whole(r0)] * 2 + [tall_spec] * 2 + [whole(ub)],
            scratch_shapes=[pltpu.VMEM((rows, width), bf16)] * 2
            + [pltpu.VMEM((rows, hidden), bf16)] * 2,
        ),
        out_shape=[jax.ShapeDtypeStruct(cots.shape, bf16)] + [row] * 2 + [tall] * 2
        + [jax.ShapeDtypeStruct(ub.shape, f32)],
        input_output_aliases={5 + count: 0} if given else {},
        compiler_params=params(56),
        cost_estimate=cost(16 * rows * width * hidden, 24 * rows * width + 4 * hidden * width),
        name="feed_forward",
    )(low, r0, r1, cots, *lifts, ub, *([outs] if given else []))


def lift_grad(low, lefts, rights, order, place, before):
    ordered = not isinstance(rights, list)
    ins = [rights] if ordered else rights
    hidden, wide = lefts[0].shape[0], ins[0].shape[1]
    count = len(lefts)
    piece = lefts[0].shape[1] // 2
    tiles, given = 4, 0 if before is None else 4
    tile = hidden // tiles

    def kernel(low_ref, *refs):
        l_refs, r_refs = refs[:count], refs[count : count + len(ins)]
        out_refs = refs[count + len(ins) + given :]
        total = None
        for k in range(2 * count):
            if ordered:
                right = r_refs[0][pl.ds(pl.multiple_of((low_ref[0] ^ order[k]) * piece, piece), piece), :]
            else:
                right = r_refs[k][...]
            start = (k % 2) * piece
            part = dot(l_refs[k // 2][:, start : start + piece], right)
            total = part if total is None else total + part
        total = total.astype(bf16)
        for n in range(tiles):
            @pl.when(pl.program_id(0) == n)
            def _(n=n):
                out_refs[n][0] = total

    depth = 2 * count * piece
    return pl.pallas_call(
        kernel,
        grid_spec=pltpu.PrefetchScalarGridSpec(
            num_scalar_prefetch=1,
            grid=(tiles,),
            in_specs=[pl.BlockSpec((tile, 2 * piece), lambda i, s: (i, 0))] * count
            + [pl.BlockSpec(x.shape, lambda i, s: (0, 0)) for x in ins]
            + [pl.BlockSpec(memory_space=pl.ANY)] * given,
            out_specs=[pl.BlockSpec((1, tile, wide), lambda i, s: (place, 0, 0))] * tiles,
        ),
        out_shape=[jax.ShapeDtypeStruct((2, tile, wide), bf16)] * tiles,
        input_output_aliases={1 + count + len(ins) + n: n for n in range(given)},
        compiler_params=params(56),
        cost_estimate=cost(2 * depth * hidden * wide, 2 * depth * (hidden + wide) + 2 * hidden * wide),
        name="lift_grad",
    )(low, *lefts, *ins, *(before or ()))


def shard_grads(low, products):
    lefts = [x for p in products for x in p[0]]
    rights = [x for p in products for x in p[1]]
    spans = []
    for p in products:
        start = spans[-1][1] if spans else 0
        spans.append((start, start + len(p[0])))
    count, wide = len(lefts), rights[0].shape[1]
    rows = lefts[0].shape[1] // 8

    def kernel(low_ref, *refs):
        l_refs, r_refs = refs[:count], refs[count : 2 * count]
        even_ref, odd_ref = refs[2 * count : 2 * count + 2]
        bufs, sems = refs[2 * count + 2 : -1], refs[-1]
        step = pl.program_id(0)
        copies = [pltpu.make_async_copy(r_refs[n], bufs[n], sems.at[n]) for n in range(count)]

        @pl.when(step == 0)
        def _():
            for copy in copies:
                copy.start()

        for p, (start, stop) in enumerate(spans):
            @pl.when(step == 2 * p)
            def _(start=start, stop=stop):
                for n in range(start, stop):
                    copies[n].wait()

            @pl.when(step // 2 == p)
            def _(start=start, stop=stop):
                total = None
                for n in range(start, stop):
                    part = dot(l_refs[n][...], bufs[n][...], 0, 0)
                    total = part if total is None else total + part
                total = total.astype(bf16)
                swap = (low_ref[0] & 1) == 1
                for h in range(2):
                    first = total[2 * h * rows : (2 * h + 1) * rows]
                    second = total[(2 * h + 1) * rows : (2 * h + 2) * rows]
                    spot = ((low_ref[0] >> 1) & 1) ^ h
                    even_ref[spot] = jnp.where(swap, second, first)
                    odd_ref[spot] = jnp.where(swap, first, second)

    def tile(p):
        return lambda i, s: (0, jnp.clip(i - 2 * p, 0, 1))

    specs = [
        pl.BlockSpec((lefts[n].shape[0], 4 * rows), tile(p))
        for p, (start, stop) in enumerate(spans)
        for n in range(start, stop)
    ]
    depth = sum(x.shape[0] for x in lefts)
    shape = jax.ShapeDtypeStruct((4, rows, len(products) * wide), bf16)
    return pl.pallas_call(
        kernel,
        grid_spec=pltpu.PrefetchScalarGridSpec(
            num_scalar_prefetch=1,
            grid=(2 * len(products),),
            in_specs=specs + [pl.BlockSpec(memory_space=pl.ANY)] * count,
            out_specs=[pl.BlockSpec((2, rows, wide), lambda i, s: ((s[0] >> 2) ^ (i % 2), 0, i // 2))] * 2,
            scratch_shapes=[pltpu.VMEM(x.shape, bf16) for x in rights] + [pltpu.SemaphoreType.DMA((count,))],
        ),
        out_shape=[shape] * 2,
        compiler_params=params(56),
        cost_estimate=cost(16 * depth * rows * wide, 2 * depth * (8 * rows + wide)),
        name="shard_grads",
    )(low, *lefts, *rights)


def pack_shards(ones, twos, up, down):
    rows, cols = ones[0].shape
    flat = [*ones, *twos, up, down]
    part = up.shape[1] // 8

    def kernel(*refs):
        one_refs, two_refs = refs[: len(ones)], refs[len(ones) : len(ones) + len(twos)]
        up_ref, down_ref, out_one, out_two, out_lift = refs[len(flat) - 2 :]
        for i, ref in enumerate(one_refs):
            out_one[:, i * cols : (i + 1) * cols] = ref[...]
        for i, ref in enumerate(two_refs):
            x = ref[...].T if i in (0, len(twos) - 1) else ref[...]
            out_two[:, i * cols : (i + 1) * cols] = x
        for d in range(8):
            span = slice(d * part, (d + 1) * part)
            out_lift[d, 0] = up_ref[:, span]
            out_lift[d, 1] = down_ref[span, :].T

    return pl.pallas_call(
        kernel,
        out_shape=[
            jax.ShapeDtypeStruct((rows, len(ones) * cols), bf16),
            jax.ShapeDtypeStruct((rows, len(twos) * cols), bf16),
            jax.ShapeDtypeStruct((8, 2, rows, part), bf16),
        ],
        compiler_params=params(56),
        cost_estimate=cost(0, 4 * sum(x.size for x in flat)),
        name="pack_shards",
    )(*flat)


def sum_columns(place, pieces, count, size):
    rows, wide = pieces[0].shape
    cols = wide // count
    part = cols // size

    def kernel(place_ref, *refs):
        ins, outs, total = refs[: len(pieces)], refs[len(pieces) : -1], refs[-1]
        acc = ins[0][...].astype(f32)
        for ref in ins[1:]:
            acc = acc + ref[...].astype(f32)
        total[...] = acc
        for r in range(size):
            start = lax.rem(place_ref[0] + size - r, size) * part
            for w in range(count):
                span = pl.ds(pl.multiple_of(w * cols + start, part), part)
                outs[r][:, w * part : (w + 1) * part] = total[:, span].astype(outs[r].dtype)

    return pl.pallas_call(
        kernel,
        grid_spec=pltpu.PrefetchScalarGridSpec(
            num_scalar_prefetch=1,
            grid=(1,),
            in_specs=[pl.BlockSpec(x.shape, lambda i, s: (0, 0)) for x in pieces],
            out_specs=[pl.BlockSpec((rows, count * part), lambda i, s: (0, 0))] * size,
            scratch_shapes=[pltpu.VMEM((rows, wide), f32)],
        ),
        out_shape=[jax.ShapeDtypeStruct((rows, count * part), f32 if r == 0 else bf16) for r in range(size)],
        compiler_params=params(56),
        cost_estimate=cost(0, 4 * sum(x.size for x in pieces)),
        name="sum_columns",
    )(place, *pieces)


def row_sums(x):
    return jnp.mean(x, axis=-1, keepdims=True)


def norm_backward(rows, gain, pieces, residual, sums, tile=256):
    count, width = rows.shape

    def kernel(rows_ref, gain_ref, residual_ref, *refs):
        grads, outs = refs[: len(pieces)], refs[len(pieces) :]
        x = rows_ref[...].astype(f32)
        centered = x - row_sums(x)
        scale = lax.rsqrt(row_sums(centered * centered) + EPSILON)
        xhat = centered * scale
        grad = grads[0][...].astype(f32)
        for g in grads[1:]:
            grad = grad + g[...].astype(f32)
        scaled = grad * gain_ref[...]
        back = scale * (scaled - row_sums(scaled) - xhat * row_sums(scaled * xhat))
        out = residual_ref[...].astype(f32) + back
        outs[0][...] = out
        if sums:
            short = out.astype(bf16)
            outs[1][...] = short

            @pl.when(pl.program_id(0) == 0)
            def _():
                outs[2][...] = jnp.zeros_like(outs[2])

            for n, v in enumerate((grad * xhat, grad, short.astype(f32))):
                outs[2][n : n + 1, :] += jnp.sum(v, axis=0, keepdims=True)

    row = pl.BlockSpec((tile, width), lambda i: (i, 0))
    shape = jax.ShapeDtypeStruct((count, width), f32)
    return pl.pallas_call(
        kernel,
        grid=(count // tile,),
        in_specs=[row, pl.BlockSpec((1, width), lambda i: (0, 0)), row] + [row] * len(pieces),
        out_specs=[row, row, pl.BlockSpec((3, width), lambda i: (0, 0))] if sums else [row],
        out_shape=[
            shape,
            jax.ShapeDtypeStruct((count, width), bf16),
            jax.ShapeDtypeStruct((3, width), f32),
        ]
        if sums
        else [shape],
        compiler_params=params(56),
        cost_estimate=cost(0, 12 * rows.size),
        name="norm_backward",
    )(rows, gain[None], residual, *pieces)


def share_grad(grads, weights, rows, before, final):
    count, width = rows.shape
    tile = count
    given = 0 if before is None else 1

    def kernel(*refs):
        g_refs, w_refs = refs[: len(grads)], refs[len(grads) : 2 * len(grads)]
        rows_ref, rest = refs[2 * len(grads)], refs[2 * len(grads) + 1 :]
        out_ref, sums_ref = rest[given:]
        share = dot(g_refs[0][...], w_refs[0][...], 1, 1)
        for g, w in zip(g_refs[1:], w_refs[1:]):
            share = share + dot(g[...], w[...], 1, 1)
        x = rows_ref[...].astype(f32)
        centered = x - row_sums(x)
        xhat = centered * lax.rsqrt(row_sums(centered * centered) + EPSILON)

        sums_ref[0:1, :] = jnp.sum(share * xhat, axis=0, keepdims=True)
        sums_ref[1:2, :] = jnp.sum(share, axis=0, keepdims=True)
        if given:
            share = share + rest[0][...].astype(f32)
        out_ref[...] = share.astype(out_ref.dtype)

    row = pl.BlockSpec((tile, width), lambda i: (i, 0))
    return pl.pallas_call(
        kernel,
        grid=(1,),
        in_specs=[row] * len(grads)
        + [pl.BlockSpec(w.shape, lambda i: (0, 0)) for w in weights]
        + [row] * (1 + given),
        out_specs=[row, pl.BlockSpec((2, width), lambda i: (0, 0))],
        out_shape=[
            jax.ShapeDtypeStruct((count, width), f32 if final else bf16),
            jax.ShapeDtypeStruct((2, width), f32),
        ],
        compiler_params=params(56),
        cost_estimate=cost(2 * len(grads) * count * width * width, 6 * rows.size),
        name="share_grad",
    )(*grads, *weights, rows, *([before] if given else []))


def normed(rows, gain, shift):
    average = jnp.mean(rows, axis=-1, keepdims=True)
    centered = rows - average
    variance = jnp.mean(centered * centered, axis=-1, keepdims=True)
    return (centered * lax.rsqrt(variance + EPSILON) * gain + shift).astype(bf16)


def centered_rows(rows):
    average = jnp.mean(rows, axis=-1, keepdims=True)
    centered = rows - average
    scale = lax.rsqrt(jnp.mean(centered * centered, axis=-1, keepdims=True) + EPSILON)
    return centered * scale, scale


def norm_back(rows, gain, grad):
    xhat, scale = centered_rows(rows)
    scaled = grad * gain
    return scale * (
        scaled
        - jnp.mean(scaled, axis=-1, keepdims=True)
        - xhat * jnp.mean(scaled * xhat, axis=-1, keepdims=True)
    )


def norm_sums(rows, grad):
    return jnp.sum(grad * centered_rows(rows)[0], axis=0), jnp.sum(grad, axis=0)


def column_sums(matrix):
    return jnp.sum(matrix.astype(f32), axis=0)


def together(*values):
    return lax.optimization_barrier(values)


def flip(x, k):
    return lax.ppermute(x, "low", [(i, i ^ k) for i in range(8)])


def wrap(value, size):
    return value % size if isinstance(value, int) else lax.rem(value, size)


def turn(x, r, size):
    return lax.ppermute(x, "tensor", [(i, (i + r) % size) for i in range(size)])


def gather_chips(x):
    return [x] + [flip(x, k) for k in (2, 4, 6)]


def gather_cores(even):
    return [p for e in even for p in (e, flip(e, 1))]


def by_place(pieces, place):
    size = len(pieces)
    return jnp.stack(
        [
            sum(jnp.where(lax.rem(place + size - r, size) == z, pieces[r], 0.0) for r in range(size))
            for z in range(size)
        ]
    )


def stack_shards(scalars, pieces):
    (stacked,) = move(
        "stack_shards", scalars, pieces, [(len(pieces), *pieces[0].shape)],
        lambda s: [(r, (slice(None), slice(None)), 0, (r,)) for r in range(len(pieces))],
    )
    return stacked


def unpack_weights(scalars, pieces, count, sizes):
    size, rows, cols = pieces[0].shape
    cols //= count
    every = slice(None)

    def plan(s):
        return [
            (
                k, (r, every, pl.ds(w * cols, cols)),
                w, (at((s[0] ^ k) * rows, rows), at(wrap(s[1] + size - r, size) * cols, cols)),
            )
            for w in range(count) for k in range(8) for r in range(size)
        ]

    matrices = move("unpack_weights", scalars, pieces, [(8 * rows, size * cols)] * count, plan)
    if sizes[0] > 1:
        matrices = [lax.all_gather(m, "high", axis=0, tiled=True) for m in matrices]
    return matrices


def add_pair(a, b):
    return (a.astype(f32) + b.astype(f32)).astype(bf16)


def scatter_low(pieces):
    even = [add_pair(pieces[k], flip(pieces[k + 1], 1)) for k in (6, 4, 2)]
    back = [flip(e, k).astype(f32) for e, k in zip(even, (6, 4, 2))]
    own = pieces[0].astype(f32) + flip(pieces[1], 1).astype(f32)
    return own + back[0] + back[1] + back[2]


def whole_shards(parts, turned, count):
    shard = parts[0] + sum(x.astype(f32) for x in turned)
    return jnp.split(shard, count, axis=1)


def sum_tensor(vector, sizes):
    if sizes[0] > 1:
        vector = lax.psum(vector, "high")
    return vector + sum(turn(vector, r, sizes[2]) for r in range(1, sizes[2]))


def sum_low(vector):
    spread = jnp.broadcast_to(vector, (8, *vector.shape))
    return jnp.sum(lax.all_to_all(spread, "low", split_axis=0, concat_axis=0, tiled=True), axis=0)


def path_bias(parents, place, own, blocks):
    count = parents.shape[0]
    labels = jnp.arange(count)
    table = (
        (labels[:, None] == labels[None, :])
        | ((parents[:, None] == labels[None, :]) & (labels[:, None] > 0))
    ).astype(f32)
    reach = 1
    while reach < count:
        table = jnp.minimum(jnp.dot(table, table), 1.0)
        reach *= 2
    slots = jnp.arange(blocks * own)
    segment = (place - slots // own) * own + slots % own
    pick = (labels[:, None] == segment[None, :]).astype(f32)
    lanes = jnp.arange(2 * own * SEG)
    query = place * own + (lanes // SEG) % own
    mine = (labels[:, None] == query[None, :]).astype(f32)
    seen = jnp.dot(pick.T, jnp.dot(table.T, mine))
    return jnp.where(seen > 0.5, 0.0, NEG)


def on_device(sizes, sure):
    size = sizes[2]

    def run(
        tokens,
        encoded,
        parents,
        source_lengths,
        cotangent,
        first_gain,
        first_shift,
        self_query,
        self_query_bias,
        self_key,
        self_value,
        self_value_bias,
        self_out,
        self_out_bias,
        second_gain,
        second_shift,
        cross_query,
        cross_query_bias,
        cross_key,
        cross_value,
        cross_value_bias,
        cross_out,
        cross_out_bias,
        third_gain,
        third_shift,
        up_weight,
        up_bias,
        down_weight,
        down_bias,
    ):
        low = lax.axis_index("low")
        place = lax.axis_index("tensor")
        scalars = jnp.stack([low, place]).astype(jnp.int32)
        low_1, place_1 = scalars[:1], scalars[1:]
        rows, width = tokens.shape
        up_chain = [(i, i + 1) for i in range(size - 1)]
        down_chain = [(i + 1, i) for i in range(size - 1)]

        first, second, lift = pack_shards(
            [self_query, self_key, self_value],
            [self_out, cross_query, cross_key, cross_value, cross_out],
            up_weight, down_weight,
        )
        part = width // size
        hidden = up_weight.shape[1] // 8
        z = [turn(first, r, size) for r in range(1, size)]
        ones = [normed(tokens.astype(f32), first_gain, first_shift)]
        bias = path_bias(parents[0], place, rows // SEG, size)
        lift = lax.all_to_all(lift, "low", split_axis=0, concat_axis=0, tiled=True)
        if sizes[0] > 1:
            lift = lax.all_gather(lift, "high", axis=0, tiled=True)
        first, second, z, ones, bias, tokens_sent = together(first, second, z, ones, bias, tokens)

        even_a = gather_chips(stack_shards(scalars, [first, *z]))
        blocks = [tokens, lax.ppermute(tokens_sent, "tensor", up_chain)]
        z = [turn(second, 1, size)]
        biases = jnp.concatenate(
            [
                self_query_bias, self_value_bias, cross_query_bias, cross_value_bias,
                lax.dynamic_slice_in_dim(up_bias, low * hidden, hidden, 0),
            ]
        )
        biases = [biases] + [turn(biases, r, size) for r in range(1, size)]
        ub = jnp.concatenate([x[4 * part :] for x in biases])[None]
        placed = by_place([x[: 4 * part] for x in biases], place).reshape(size, 4, part)
        q_bias, v_bias, xq_bias, xv_bias = [placed[:, i].reshape(width) for i in range(4)]
        even_a, second, z[0], blocks, ub, q_bias, v_bias, xq_bias, xv_bias, encoded, lift = together(
            even_a, second, z[0], blocks, ub, q_bias, v_bias, xq_bias, xv_bias, encoded, lift
        )

        all_a = gather_cores(even_a)
        blocks.append(lax.ppermute(blocks[-1], "tensor", up_chain))
        source = lax.all_gather(encoded, "tensor", axis=0, tiled=True)
        z = z + [turn(second, r, size) for r in range(2, size)]
        wq, wk, wv = unpack_weights(scalars, all_a, 3, sizes)
        q1 = (dot(ones[0], wq) + q_bias).astype(bf16)
        ks, vs, state, mixed_one = [], [], None, None
        for r in range(size):
            if r:
                ones.append(normed(blocks[r].astype(f32), first_gain, first_shift))
            ks.append(dot(ones[r], wk).astype(bf16))
            vs.append((dot(ones[r], wv) + v_bias).astype(bf16))
            if r == 0:
                continue
            if r == 1:
                q1, ks, vs, second, z = together(q1, ks, vs, second, z)
                packed_b = stack_shards(scalars, [second, *z])
                even_b = [packed_b, flip(packed_b, 2), flip(packed_b, 4)]
            seen = (0, 1) if r == 1 else (r,)
            if r < size - 1:
                state = self_forward(place_1, q1, ks, vs, bias, seen, state, False)
            else:
                mixed_one, lse_one = self_forward(place_1, q1, ks, vs, bias, seen, state, True)
            if r == 1:
                state, blocks, even_b = together(state, blocks, even_b)
                even_b.append(flip(even_b[0], 6))
                blocks.append(lax.ppermute(blocks[-1], "tensor", up_chain))
            elif r < size - 1:
                if r < size - 2:
                    blocks.append(lax.ppermute(blocks[-1], "tensor", up_chain))
                state, blocks, even_b, cots_sent, lift = together(
                    state, blocks, even_b, cotangent, lift
                )
                cots = lax.all_gather(cots_sent, "low", axis=0, tiled=True)
                all_b = gather_cores(even_b)
                lifts = [lift, turn(lift, 1, size)]
        mixed_one, all_b, lifts = together(mixed_one, all_b, lifts)
        lifts = lifts + [turn(lifts[-1], 1, size)]

        wo, xq, xk, xv, xo = unpack_weights(scalars, all_b, 5, sizes)
        hidden_one = tokens.astype(f32) + dot(mixed_one, wo, 1, 1) + self_out_bias
        two = normed(hidden_one, second_gain, second_shift)
        q2 = (dot(two, xq) + xq_bias).astype(bf16)
        k2 = dot(source, xk).astype(bf16)
        v2 = (dot(source, xv) + xv_bias).astype(bf16)
        q2, k2, v2, lifts = together(q2, k2, v2, lifts)

        lifts = lifts + [turn(lifts[-1], 1, size)]
        mixed_two, lse_two = cross_forward(source_lengths, q2, k2, v2, sure)
        hidden_two = hidden_one + dot(mixed_two, xo, 1, 1) + cross_out_bias
        three = normed(hidden_two, third_gain, third_shift)
        three, lifts = together(three, lifts)

        x2, x4, c0 = flip(three, 2), flip(three, 4), flip(three, 1)

        def lift_pair(pair, r0, r1, outs):
            return feed_forward(low_1, pair, r0, r1, cots, lifts, ub, outs)

        outs, own, got, inner_0, grad_0, sums_0 = lift_pair((0, 1), three, c0, None)
        own_got = flip(got, 1)
        three_sent, x2, x4, own = together(three, x2, x4, own)
        c2, c4, x6 = flip(x2, 1), flip(x4, 1), flip(three_sent, 6)
        outs, back_2, back_4, inner_1, grad_1, sums_1 = lift_pair((2, 4), x2, x4, outs)
        c2, c4, back_2, own_got = together(c2, c4, back_2, own_got)
        outs, got_2, got_4, inner_2, grad_2, sums_2 = lift_pair((3, 5), c2, c4, outs)
        x6, got_2 = together(x6, got_2)
        got_2, got_4, c6 = flip(got_2, 1), flip(got_4, 1), flip(x6, 1)
        outs, back_6, got_6, inner_3, grad_3, sums_3 = lift_pair((6, 7), x6, c6, outs)
        back_6, got_2, got_4 = together(back_6, got_2, got_4)
        back_2, back_4 = flip(add_pair(back_2, got_2), 2), flip(add_pair(back_4, got_4), 4)
        got_6 = flip(got_6, 1)
        order = (0, 1, 2, 4, 3, 5, 6, 7)
        lift_shares = lift_grad(
            low_1, [grad_0, grad_1, grad_2, grad_3], [three, c0, x2, x4, c2, c4, x6, c6], order, 0, None
        )
        back_6, got_6, back_2, back_4, lift_shares = together(
            back_6, got_6, back_2, back_4, lift_shares
        )
        back_6 = flip(add_pair(back_6, got_6), 6)
        lift_shares = lift_grad(
            low_1, [inner_0, inner_1, inner_2, inner_3], cots, order, 1, lift_shares
        )
        up_sums = [sums_0, sums_1, sums_2, sums_3]
        lift_shares, back_6 = together(lift_shares, back_6)
        grad_hidden_two, grad_two, sums_three = norm_backward(
            hidden_two, third_gain, [own, own_got, back_2, back_4, back_6], cotangent, True
        )
        do2 = dot(grad_two, xo).astype(bf16)
        do2, outs, lift_shares = together(do2, outs, lift_shares)

        out_sum = lax.psum_scatter(outs, "low", scatter_dimension=0, tiled=True)
        lift_got = turn(lift_shares[size - 1], size - 1, size)
        dq2, dk2, dv2 = cross_backward(source_lengths, q2, k2, v2, mixed_two, do2, lse_two, sure)
        dq2, dk2, dv2, lift_got = together(dq2, dk2, dv2, lift_got)

        lift_got = turn(add_pair(lift_shares[size - 2], lift_got), size - 1, size)
        grad_hidden_one, grad_one, sums_two = norm_backward(
            hidden_one, second_gain, [dot(dq2, xq, 1, 1)], grad_hidden_two, True
        )
        do1 = dot(grad_one, wo).astype(bf16)
        encoded_part = (dot(dk2, xk, 1, 1) + dot(dv2, xv, 1, 1)).astype(bf16)
        early = column_sums(cotangent), column_sums(dq2), column_sums(dv2)
        do1, lift_got, encoded_part, early = together(do1, lift_got, encoded_part, early)

        lift_got = turn(add_pair(lift_shares[size - 3], lift_got), size - 1, size)
        b_laid = shard_grads(
            low_1,
            [
                ([grad_one], [mixed_one]),
                ([two], [dq2]),
                ([source], [dk2]),
                ([source], [dv2]),
                ([grad_two], [mixed_two]),
            ],
        )
        spread = by_place([sum(up_sums)[0, r * hidden : (r + 1) * hidden] for r in range(size)], place)
        spread = lax.dynamic_update_slice(
            jnp.zeros((size, up_bias.shape[0]), f32), spread, (0, low * hidden)
        )
        whole_sums = [sums_two.reshape(-1), sums_three.reshape(-1), early[0]]
        place_sums = [spread, early[1].reshape(size, part), early[2].reshape(size, part)]
        (b_even, b_odd), do1, lift_got, encoded_part, whole_sums, place_sums = together(
            b_laid, do1, lift_got, encoded_part, whole_sums, place_sums
        )

        if sizes[0] > 1:
            b_even, b_odd = [
                lax.psum_scatter(x, "high", scatter_dimension=1, tiled=True) for x in (b_even, b_odd)
            ]
        b_got = flip(b_odd, 1)
        lift_sums = add_pair(lift_shares[0], lift_got)
        if sizes[0] > 1:
            lift_sums = lax.psum_scatter(lift_sums, "high", scatter_dimension=2, tiled=True)
        lift_sums = lax.all_to_all(lift_sums, "low", split_axis=2, concat_axis=1, tiled=True)
        encoded_sum = lax.psum_scatter(encoded_part, "tensor", scatter_dimension=0, tiled=True)
        dq, dks, dvs, own_sums, share = None, [None] * size, [None] * size, [], None
        for group in [(r,) for r in range(size - 1, 1, -1)] + [(1, 0)]:
            r = group[0]
            dq, dk, dv = self_backward(
                place_1, q1, ks, vs, mixed_one, do1, lse_one, bias, group, dq
            )
            for n, s in enumerate(group):
                dks[s], dvs[s] = dk[n], dv[n]
            if r > 1:
                share, sums = share_grad([dk[0], dv[0]], [wk, wv], blocks[r], share, False)
                own_sums.append(sums)
            if r == size - 1:
                share, do1, b_even, b_got, out_sum, lift_sums = together(
                    share, do1, b_even, b_got, out_sum, lift_sums
                )
                share = lax.ppermute(share, "tensor", down_chain)
                b_sums = [add_pair(b_even[p], b_got[p]) for p in range(4)]
                b_back = [flip(b_sums[p], 2 * p) for p in (1, 2, 3)]
            elif r > 1:
                share, do1, encoded_sum = together(share, do1, encoded_sum)
                share = lax.ppermute(share, "tensor", down_chain)
        share, sums = share_grad([dk[0], dv[0]], [wk, wv], blocks[1], share, False)
        own_sums.append(sums)
        share, dq, dks, dvs, b_back = together(share, dq, dks, dvs, b_back)
        share = lax.ppermute(share, "tensor", down_chain)
        a_even, a_odd = shard_grads(low_1, [([ones[0]], [dq]), (ones, dks), (ones, dvs)])
        if sizes[0] > 1:
            a_even, a_odd = [
                lax.psum_scatter(x, "high", scatter_dimension=1, tiled=True) for x in (a_even, a_odd)
            ]
        a_even, a_odd, share, dq, dks, dvs, b_sums, b_back = together(
            a_even, a_odd, share, dq, dks, dvs, b_sums, b_back
        )

        a_got = flip(a_odd, 1)
        b_parts = sum_columns(place_1, [b_sums[0], *b_back], 5, size)
        a_even, a_got, b_parts = together(a_even, a_got, b_parts)
        a_sums = [add_pair(a_even[p], a_got[p]) for p in range(4)]
        a_sums, b_parts, dq, dks, dvs, share = together(a_sums, b_parts, dq, dks, dvs, share)
        a_back = [flip(a_sums[p], 2 * p) for p in (1, 2, 3)]
        b_turned = [turn(b_parts[r], size - r, size) for r in range(1, size)]
        own_share, sums = share_grad([dks[0], dvs[0], dq], [wk, wv, wq], tokens, None, True)
        own_sums.append(sums)
        (tokens_grad,) = norm_backward(tokens, first_gain, [own_share, share], grad_hidden_one, False)
        whole_sums = jnp.concatenate([*whole_sums, sum(own_sums).reshape(-1)])
        place_sums += [
            column_sums(dq).reshape(size, part),
            sum(column_sums(v) for v in dvs).reshape(size, part),
        ]
        vectors = jnp.concatenate([whole_sums, jnp.concatenate(place_sums, axis=1).reshape(-1)])
        a_back, b_turned, vectors, tokens_grad, out_sum, lift_sums = together(
            a_back, b_turned, vectors, tokens_grad, out_sum, lift_sums
        )
        a_parts = sum_columns(place_1, [a_sums[0], *a_back], 3, size)
        a_turned = [turn(a_parts[r], size - r, size) for r in range(1, size)]
        vectors, a_parts = together(vectors, a_parts)
        vectors = sum_low(sum_tensor(vectors, sizes))
        small = [vectors[i * width : (i + 1) * width] for i in range(9)]
        small = [small[i] for i in (7, 8, 0, 1, 3, 4, 2, 5, 6)]
        mine = lax.dynamic_index_in_dim(vectors[9 * width :].reshape(size, -1), place, 0, keepdims=False)
        up_bias_grad, mine = mine[: up_bias.shape[0]], mine[up_bias.shape[0] :]
        split = [mine[i * part : (i + 1) * part] for i in (2, 3, 0, 1)]
        encoded_grad = encoded_sum.astype(f32)
        wo_g, xq_g, xk_g, xv_g, xo_g = whole_shards(b_parts, b_turned, 5)
        wq_g, wk_g, wv_g = whole_shards(a_parts, a_turned, 3)
        block_out = hidden_two + out_sum.astype(f32) + down_bias
        up_weight_grad = lift_sums[0].T.astype(f32)
        down_weight_grad = lift_sums[1].astype(f32)

        return (
            block_out.astype(bf16),
            tokens_grad,
            encoded_grad,
            small[0],
            small[1],
            wq_g,
            split[0],
            wk_g,
            wv_g,
            split[1],
            wo_g.T,
            small[6],
            small[2],
            small[3],
            xq_g,
            split[2],
            xk_g,
            xv_g,
            split[3],
            xo_g.T,
            small[7],
            small[4],
            small[5],
            up_weight_grad,
            up_bias_grad,
            down_weight_grad,
            small[8],
        )

    return run


def solution(mesh):
    dp, size = mesh.shape["dp"], mesh.shape["tensor"]
    sizes = (dp // 8, 8, size)
    fine = Mesh(mesh.devices.reshape(sizes), ("high", "low", "tensor"))
    depth = ("high", "low")
    rows = P((*depth, "tensor"), None)
    block, turned = P(depth, "tensor"), P("tensor", depth)
    part, whole = P("tensor"), P()
    placed = (
        rows, rows, P(depth, None), P(depth), rows, whole, whole,
        block, part, block, block, part, turned, whole, whole, whole,
        block, part, block, block, part, turned, whole, whole, whole,
        block, part, turned, whole,
    )
    out = (
        rows, rows, rows, whole, whole,
        block, part, block, block, part, turned, whole, whole, whole,
        block, part, block, block, part, turned, whole, whole, whole,
        block, part, turned, whole,
    )
    return jax.shard_map(
        on_device(sizes, 768), mesh=fine, in_specs=placed, out_specs=out, check_vma=False
    )
```

```python
import functools

import jax
import jax.numpy as jnp
from jax import lax
from jax.experimental import pallas as pl
from jax.experimental.pallas import tpu as pltpu
from jax.sharding import Mesh, PartitionSpec as P

HEAD_DIM = 64
SEG = 128
PAIR = 2 * HEAD_DIM
EPSILON = 1e-05
LOG2E = 1.4426950408889634
SCALE = HEAD_DIM ** -0.5
NEG = -1e30
CHUNK = 512
f32, bf16 = jnp.float32, jnp.bfloat16


def dot(a, b, ca=1, cb=0):
    return lax.dot_general(a, b, (((ca,), (cb,)), ((), ())), preferred_element_type=f32)


def cost(flops, moved):
    return pl.CostEstimate(flops=int(flops), bytes_accessed=int(moved), transcendentals=0)


def params(mib):
    return pltpu.CompilerParams(vmem_limit_bytes=mib * 1024 * 1024)


def move(name, scalars, sources, outs, plan):
    count = len(plan([0] * scalars.shape[0]))

    def kernel(scalars_ref, *refs):
        ins, dests, sems = refs[: len(sources)], refs[len(sources) : -1], refs[-1]
        values = [scalars_ref[i] for i in range(scalars.shape[0])]
        copies = [
            pltpu.make_async_copy(ins[a].at[ai], dests[b].at[bi], sems.at[n])
            for n, (a, ai, b, bi) in enumerate(plan(values))
        ]
        for copy in copies:
            copy.start()
        for copy in copies:
            copy.wait()

    anywhere = pl.BlockSpec(memory_space=pl.ANY)
    return pl.pallas_call(
        kernel,
        in_specs=[pl.BlockSpec(memory_space=pltpu.SMEM)]
        + [pl.BlockSpec(memory_space=pltpu.VMEM)] * len(sources),
        out_specs=[anywhere] * len(outs),
        out_shape=[jax.ShapeDtypeStruct(s, bf16) for s in outs],
        scratch_shapes=[pltpu.SemaphoreType.DMA((count,))],
        compiler_params=params(56),
        cost_estimate=cost(0, 4 * sum(x.size for x in sources)),
        name=name,
    )(scalars, *sources)


def at(start, extent):
    return pl.ds(start if isinstance(start, int) else pl.multiple_of(start, extent), extent)


def stack_heads(x):
    lane = lax.broadcasted_iota(jnp.int32, x.shape, 1)
    zero = jnp.zeros_like(x)
    return jnp.concatenate(
        [jnp.where(lane < HEAD_DIM, x, zero), jnp.where(lane >= HEAD_DIM, x, zero)], axis=0
    )


def unstack_heads(xt):
    n = xt.shape[1] // 2
    return jnp.concatenate([xt[:HEAD_DIM, :n], xt[HEAD_DIM:, n:]], axis=0).T


def segment_bias(bias_ref, block, s, causal):
    keys, wide = s.shape
    segs = keys // SEG
    b = jnp.concatenate(
        [
            jnp.broadcast_to(bias_ref[block * segs + j : block * segs + j + 1, :], (SEG, wide))
            for j in range(segs)
        ],
        0,
    )
    s = s + b
    if causal:
        key = lax.broadcasted_iota(jnp.int32, s.shape, 0)
        query = lax.broadcasted_iota(jnp.int32, s.shape, 1) & (wide // 2 - 1)
        s = jnp.where(key <= query, s, NEG)
    return s


def forward_step(k, v, qT, mask, m_ref, l_ref, acc, first):
    s = mask(dot(k, qT) * (SCALE * LOG2E))
    top = jnp.max(s, axis=0, keepdims=True)
    if first:
        p = jnp.exp2(s - top)
        m_ref[...] = top
        l_ref[...] = jnp.sum(p, axis=0, keepdims=True)
        acc[...] = dot(v, p.astype(bf16), 0, 0)
    else:
        m = jnp.maximum(m_ref[...], top)
        p = jnp.exp2(s - m)
        fade = jnp.exp2(m_ref[...] - m)
        m_ref[...] = m
        l_ref[...] = l_ref[...] * fade + jnp.sum(p, axis=0, keepdims=True)
        acc[...] = acc[...] * fade + dot(v, p.astype(bf16), 0, 0)


def forward_finish(o_ref, lse_ref, m_ref, l_ref, acc):
    o_ref[...] = unstack_heads(acc[...] * (1.0 / l_ref[...])).astype(bf16)
    lse_ref[0] = m_ref[...] + jnp.log2(l_ref[...])


def self_forward(place, q, ks, vs, bias, blocks, state, final):
    rows, count = q.shape[0], len(blocks)
    pairs = q.shape[1] // PAIR
    given = 0 if state is None else 3

    def kernel(place_ref, q_ref, *refs):
        k_refs, v_refs, bias_ref = refs[:count], refs[count : 2 * count], refs[2 * count]
        before = refs[2 * count + 1 : 2 * count + 1 + given]
        outs = refs[2 * count + 1 + given :]
        if final:
            o_ref, lse_ref, m_ref, l_ref, acc = outs
        else:
            m_out, l_out, acc_out, m_ref, l_ref, acc = outs
        if given:
            m_ref[...], l_ref[...], acc[...] = before[0][0], before[1][0], before[2][0]
        qT = stack_heads(q_ref[...]).T
        for n, r in enumerate(blocks):
            def step(n=n, r=r):
                forward_step(
                    k_refs[n][...], v_refs[n][...], qT,
                    lambda s: segment_bias(bias_ref, r, s, r == 0), m_ref, l_ref, acc, r == 0,
                )
            if r == 0:
                step()
            else:
                pl.when(place_ref[0] >= r)(step)
        if final:
            forward_finish(o_ref, lse_ref, m_ref, l_ref, acc)
        else:
            m_out[0], l_out[0], acc_out[0] = m_ref[...], l_ref[...], acc[...]

    col = pl.BlockSpec((rows, PAIR), lambda h, p: (0, h))
    line = pl.BlockSpec((1, 1, 2 * rows), lambda h, p: (h, 0, 0))
    slab = pl.BlockSpec((1, PAIR, 2 * rows), lambda h, p: (h, 0, 0))
    lines = jax.ShapeDtypeStruct((pairs, 1, 2 * rows), f32)
    slabs = jax.ShapeDtypeStruct((pairs, PAIR, 2 * rows), f32)
    stat = pltpu.VMEM((1, 2 * rows), f32)
    return pl.pallas_call(
        kernel,
        grid_spec=pltpu.PrefetchScalarGridSpec(
            num_scalar_prefetch=1,
            grid=(pairs,),
            in_specs=[col] * (1 + 2 * count)
            + [pl.BlockSpec(bias.shape, lambda h, p: (0, 0))]
            + [line, line, slab][:given],
            out_specs=[col, line] if final else [line, line, slab],
            scratch_shapes=[stat, stat, pltpu.VMEM((PAIR, 2 * rows), f32)],
        ),
        out_shape=[jax.ShapeDtypeStruct(q.shape, bf16), lines] if final else [lines, lines, slabs],
        compiler_params=params(56),
        cost_estimate=cost(16 * count * rows * q.size, 4 * q.size * (1 + count)),
        name="self_forward",
    )(place, q, *[ks[r] for r in blocks], *[vs[r] for r in blocks], bias, *(state or ()))


def cross_forward(length, q, k, v, sure):
    rows, total = q.shape[0], k.shape[0]
    pairs = q.shape[1] // PAIR

    def kernel(length_ref, q_ref, k_ref, v_ref, o_ref, lse_ref, m_ref, l_ref, acc):
        qT = stack_heads(q_ref[...]).T
        for a in range(0, total, CHUNK):
            sl = slice(a, a + CHUNK)
            forward_step(
                k_ref[sl, :], v_ref[sl, :], qT,
                lambda s: length_mask(length_ref, s, a, sure), m_ref, l_ref, acc, a == 0,
            )
        forward_finish(o_ref, lse_ref, m_ref, l_ref, acc)

    col = pl.BlockSpec((rows, PAIR), lambda h, p: (0, h))
    tall = pl.BlockSpec((total, PAIR), lambda h, p: (0, h))
    stat = pltpu.VMEM((1, 2 * rows), f32)
    return pl.pallas_call(
        kernel,
        grid_spec=pltpu.PrefetchScalarGridSpec(
            num_scalar_prefetch=1,
            grid=(pairs,),
            in_specs=[col, tall, tall],
            out_specs=[col, pl.BlockSpec((1, 1, 2 * rows), lambda h, p: (h, 0, 0))],
            scratch_shapes=[stat, stat, pltpu.VMEM((PAIR, 2 * rows), f32)],
        ),
        out_shape=[
            jax.ShapeDtypeStruct(q.shape, bf16),
            jax.ShapeDtypeStruct((pairs, 1, 2 * rows), f32),
        ],
        compiler_params=params(56),
        cost_estimate=cost(16 * total * q.size, 4 * q.size + 4 * k.size),
        name="cross_forward",
    )(length, q, k, v)


def length_mask(length_ref, s, start, sure):
    if start + s.shape[0] <= sure:
        return s
    key = lax.broadcasted_iota(jnp.int32, s.shape, 0) + start
    return jnp.where(key < length_ref[0], s, NEG)


def backward_setup(q_ref, o_ref, do_ref):
    qst = stack_heads(q_ref[...])
    dost = stack_heads(do_ref[...])
    qT, doT = qst.T, dost.T
    oT = o_ref[...].T.astype(f32)
    delta = jnp.sum(doT.astype(f32) * jnp.concatenate([oT, oT], axis=1), axis=0, keepdims=True)
    return qst, qT, dost, doT, delta


def backward_step(k, v, query, lse, mask):
    qst, qT, dost, doT, delta = query
    p = jnp.exp2(mask(dot(k, qT) * (SCALE * LOG2E)) - lse)
    ds = (p * (dot(v, doT) - delta)).astype(bf16)
    dv = dot(p.astype(bf16), dost).astype(bf16)
    dk = (dot(ds, qst) * SCALE).astype(bf16)
    return dk, dv, dot(k, ds, 0, 0)


def self_backward(place, q, ks, vs, o, do, lse, bias, blocks, dq_before):
    rows, count = q.shape[0], len(blocks)
    pairs = q.shape[1] // PAIR
    last = 0 in blocks
    given = dq_before is not None

    def kernel(place_ref, q_ref, *refs):
        k_refs, v_refs = refs[:count], refs[count : 2 * count]
        o_ref, do_ref, lse_ref, bias_ref = refs[2 * count : 2 * count + 4]
        rest = refs[2 * count + 4 :]
        before_ref, rest = (rest[0], rest[1:]) if given else (None, rest)
        dq_ref, dk_refs, dv_refs, dqT = rest[0], rest[1 : 1 + count], rest[1 + count : 1 + 2 * count], rest[-1]

        def work():
            query = backward_setup(q_ref, o_ref, do_ref)
            dqT[...] = jnp.zeros_like(dqT)
            for n, r in enumerate(blocks):
                def step(n=n, r=r):
                    dk, dv, dq = backward_step(
                        k_refs[n][...], v_refs[n][...], query, lse_ref[0],
                        lambda s: segment_bias(bias_ref, r, s, r == 0),
                    )
                    dk_refs[n][...] = dk
                    dv_refs[n][...] = dv
                    dqT[...] += dq
                if r == 0:
                    step()
                else:
                    pl.when(place_ref[0] >= r)(step)
            part = unstack_heads(dqT[...]) * SCALE
            if given:
                part = part + before_ref[...]
            dq_ref[...] = part.astype(dq_ref.dtype)

        for n, r in enumerate(blocks):
            if r > 0:
                @pl.when(place_ref[0] < r)
                def _(n=n):
                    dk_refs[n][...] = jnp.zeros_like(dk_refs[n])
                    dv_refs[n][...] = jnp.zeros_like(dv_refs[n])
        if last:
            work()
        else:
            pl.when(place_ref[0] >= min(blocks))(work)

            @pl.when(place_ref[0] < min(blocks))
            def _():
                dq_ref[...] = before_ref[...] if given else jnp.zeros_like(dq_ref)

    col = pl.BlockSpec((rows, PAIR), lambda h, p: (0, h))
    args = [q, *[ks[r] for r in blocks], *[vs[r] for r in blocks], o, do, lse, bias]
    specs = [col] * (3 + 2 * count) + [
        pl.BlockSpec((1, 1, 2 * rows), lambda h, p: (h, 0, 0)),
        pl.BlockSpec(bias.shape, lambda h, p: (0, 0)),
    ]
    if given:
        args.append(dq_before)
        specs.append(col)
    shape = jax.ShapeDtypeStruct(q.shape, bf16)
    out = pl.pallas_call(
        kernel,
        grid_spec=pltpu.PrefetchScalarGridSpec(
            num_scalar_prefetch=1,
            grid=(pairs,),
            in_specs=specs,
            out_specs=[col] * (1 + 2 * count),
            scratch_shapes=[pltpu.VMEM((PAIR, 2 * rows), f32)],
        ),
        out_shape=[jax.ShapeDtypeStruct(q.shape, bf16 if last else f32)] + [shape] * (2 * count),
        compiler_params=params(56),
        cost_estimate=cost(40 * count * rows * q.size, 8 * q.size * (2 + count)),
        name="self_backward",
    )(place, *args)
    return out[0], out[1 : 1 + count], out[1 + count :]


def cross_backward(length, q, k, v, o, do, lse, sure):
    rows, total = q.shape[0], k.shape[0]
    pairs = q.shape[1] // PAIR

    def kernel(length_ref, q_ref, k_ref, v_ref, o_ref, do_ref, lse_ref, dq_ref, dk_ref, dv_ref, dqT):
        query = backward_setup(q_ref, o_ref, do_ref)
        for a in range(0, total, CHUNK):
            sl = slice(a, a + CHUNK)
            dk, dv, dq = backward_step(
                k_ref[sl, :], v_ref[sl, :], query, lse_ref[0],
                lambda s: length_mask(length_ref, s, a, sure),
            )
            dk_ref[sl, :] = dk
            dv_ref[sl, :] = dv
            if a == 0:
                dqT[...] = dq
            else:
                dqT[...] += dq
        dq_ref[...] = (unstack_heads(dqT[...]) * SCALE).astype(bf16)

    col = pl.BlockSpec((rows, PAIR), lambda h, p: (0, h))
    tall = pl.BlockSpec((total, PAIR), lambda h, p: (0, h))
    return pl.pallas_call(
        kernel,
        grid_spec=pltpu.PrefetchScalarGridSpec(
            num_scalar_prefetch=1,
            grid=(pairs,),
            in_specs=[col, tall, tall, col, col, pl.BlockSpec((1, 1, 2 * rows), lambda h, p: (h, 0, 0))],
            out_specs=[col, tall, tall],
            scratch_shapes=[pltpu.VMEM((PAIR, 2 * rows), f32)],
        ),
        out_shape=[
            jax.ShapeDtypeStruct(q.shape, bf16),
            jax.ShapeDtypeStruct(k.shape, bf16),
            jax.ShapeDtypeStruct(k.shape, bf16),
        ],
        compiler_params=params(56),
        cost_estimate=cost(40 * total * q.size, 8 * q.size + 8 * k.size),
        name="cross_backward",
    )(length, q, k, v, o, do, lse)


ERFC = (0.254829592, -0.284496736, 1.421413741, -1.453152027, 1.061405429)


def gelu_pair(v):
    e = jnp.exp2(v * v * (-0.5 * LOG2E))
    t = 1.0 / (1.0 + jnp.abs(v) * (0.3275911 * 0.7071067811865476))
    a1, a2, a3, a4, a5 = (0.5 * a for a in ERFC)
    tail = ((((a5 * t + a4) * t + a3) * t + a2) * t + a1) * t * e
    cdf = jnp.where(v >= 0.0, 1.0 - tail, tail)
    return v * cdf, cdf + v * e * 0.3989422804014327


def feed_forward(low, pair, r0, r1, cots, lifts, ub, outs):
    rows, width = r0.shape
    part, count = lifts[0].shape[3], len(lifts)
    hidden = part * count
    given = 0 if outs is None else 1

    def kernel(low_ref, r0_ref, r1_ref, g_ref, *refs):
        w_refs, ub_ref = refs[:count], refs[count]
        out_ref, back0, back1, inner_ref, grad_ref, sums_ref, r_ref, back_s, inner_s, grad_s = refs[count + 1 + given :]
        i = pl.program_id(0)

        @pl.when(i == 0)
        def _():
            r_ref[...] = r0_ref[...]
            sums_ref[...] = jnp.zeros_like(sums_ref)

        @pl.when(i == 1)
        def _():
            r_ref[...] = r1_ref[...]

        ups = [w[:, 0].reshape(width, part) for w in w_refs]
        downs = [w[:, 1].reshape(width, part) for w in w_refs]
        out = back = None
        for n in range(count):
            cols = slice(n * part, (n + 1) * part)
            lifted = dot(r_ref[...], ups[n]) + ub_ref[:, cols]
            grad_inner = dot(g_ref[...], downs[n])
            value, slope = gelu_pair(lifted)
            inner = value.astype(bf16)
            grad = (grad_inner * slope).astype(bf16)
            inner_s[:, cols], grad_s[:, cols] = inner, grad
            inner_ref[cols, :], grad_ref[cols, :] = inner.T, grad.T
            sums_ref[:, cols] += jnp.sum(grad.astype(f32), axis=0, keepdims=True)
        for n in range(count):
            cols = slice(n * part, (n + 1) * part)
            o = dot(inner_s[:, cols], downs[n], 1, 1)
            b = dot(grad_s[:, cols], ups[n], 1, 1)
            out, back = (o, b) if n == 0 else (out + o, back + b)
        out_ref[...] = out.astype(bf16)
        back_s[...] = back.astype(bf16)

        @pl.when(i == 0)
        def _():
            back0[...] = back_s[...]

        @pl.when(i == 1)
        def _():
            back1[...] = back_s[...]

    whole = lambda x: pl.BlockSpec(x.shape, lambda i, s: (0,) * x.ndim)
    row = jax.ShapeDtypeStruct((rows, width), bf16)
    tall = jax.ShapeDtypeStruct((hidden, 2 * rows), bf16)
    tall_spec = pl.BlockSpec((hidden, rows), lambda i, s: (0, i))
    by_device = pl.BlockSpec((rows, width), lambda i, s: (s[0] ^ (pair[0] + (pair[1] - pair[0]) * i), 0))
    return pl.pallas_call(
        kernel,
        grid_spec=pltpu.PrefetchScalarGridSpec(
            num_scalar_prefetch=1,
            grid=(2,),
            in_specs=[whole(r0), whole(r1), by_device]
            + [whole(x) for x in lifts] + [whole(ub)]
            + [pl.BlockSpec(memory_space=pl.ANY)] * given,
            out_specs=[by_device] + [whole(r0)] * 2 + [tall_spec] * 2 + [whole(ub)],
            scratch_shapes=[pltpu.VMEM((rows, width), bf16)] * 2
            + [pltpu.VMEM((rows, hidden), bf16)] * 2,
        ),
        out_shape=[jax.ShapeDtypeStruct(cots.shape, bf16)] + [row] * 2 + [tall] * 2
        + [jax.ShapeDtypeStruct(ub.shape, f32)],
        input_output_aliases={5 + count: 0} if given else {},
        compiler_params=params(56),
        cost_estimate=cost(16 * rows * width * hidden, 24 * rows * width + 4 * hidden * width),
        name="feed_forward",
    )(low, r0, r1, cots, *lifts, ub, *([outs] if given else []))


def lift_grad(low, lefts, rights, order, place, before):
    ordered = not isinstance(rights, list)
    ins = [rights] if ordered else rights
    hidden, wide = lefts[0].shape[0], ins[0].shape[1]
    count = len(lefts)
    piece = lefts[0].shape[1] // 2
    tiles, given = 4, 0 if before is None else 4
    tile = hidden // tiles

    def kernel(low_ref, *refs):
        l_refs, r_refs = refs[:count], refs[count : count + len(ins)]
        out_refs = refs[count + len(ins) + given :]
        total = None
        for k in range(2 * count):
            if ordered:
                right = r_refs[0][pl.ds(pl.multiple_of((low_ref[0] ^ order[k]) * piece, piece), piece), :]
            else:
                right = r_refs[k][...]
            start = (k % 2) * piece
            part = dot(l_refs[k // 2][:, start : start + piece], right)
            total = part if total is None else total + part
        total = total.astype(bf16)
        for n in range(tiles):
            @pl.when(pl.program_id(0) == n)
            def _(n=n):
                out_refs[n][0] = total

    depth = 2 * count * piece
    return pl.pallas_call(
        kernel,
        grid_spec=pltpu.PrefetchScalarGridSpec(
            num_scalar_prefetch=1,
            grid=(tiles,),
            in_specs=[pl.BlockSpec((tile, 2 * piece), lambda i, s: (i, 0))] * count
            + [pl.BlockSpec(x.shape, lambda i, s: (0, 0)) for x in ins]
            + [pl.BlockSpec(memory_space=pl.ANY)] * given,
            out_specs=[pl.BlockSpec((1, tile, wide), lambda i, s: (place, 0, 0))] * tiles,
        ),
        out_shape=[jax.ShapeDtypeStruct((2, tile, wide), bf16)] * tiles,
        input_output_aliases={1 + count + len(ins) + n: n for n in range(given)},
        compiler_params=params(56),
        cost_estimate=cost(2 * depth * hidden * wide, 2 * depth * (hidden + wide) + 2 * hidden * wide),
        name="lift_grad",
    )(low, *lefts, *ins, *(before or ()))


def shard_grads(low, products):
    lefts = [x for p in products for x in p[0]]
    rights = [x for p in products for x in p[1]]
    spans = []
    for p in products:
        start = spans[-1][1] if spans else 0
        spans.append((start, start + len(p[0])))
    count, wide = len(lefts), rights[0].shape[1]
    rows = lefts[0].shape[1] // 8

    def kernel(low_ref, *refs):
        l_refs, r_refs = refs[:count], refs[count : 2 * count]
        even_ref, odd_ref = refs[2 * count : 2 * count + 2]
        bufs, sems = refs[2 * count + 2 : -1], refs[-1]
        step = pl.program_id(0)
        copies = [pltpu.make_async_copy(r_refs[n], bufs[n], sems.at[n]) for n in range(count)]

        @pl.when(step == 0)
        def _():
            for copy in copies:
                copy.start()

        for p, (start, stop) in enumerate(spans):
            @pl.when(step == 2 * p)
            def _(start=start, stop=stop):
                for n in range(start, stop):
                    copies[n].wait()

            @pl.when(step // 2 == p)
            def _(start=start, stop=stop):
                total = None
                for n in range(start, stop):
                    part = dot(l_refs[n][...], bufs[n][...], 0, 0)
                    total = part if total is None else total + part
                total = total.astype(bf16)
                swap = (low_ref[0] & 1) == 1
                for h in range(2):
                    first = total[2 * h * rows : (2 * h + 1) * rows]
                    second = total[(2 * h + 1) * rows : (2 * h + 2) * rows]
                    spot = ((low_ref[0] >> 1) & 1) ^ h
                    even_ref[spot] = jnp.where(swap, second, first)
                    odd_ref[spot] = jnp.where(swap, first, second)

    def tile(p):
        return lambda i, s: (0, jnp.clip(i - 2 * p, 0, 1))

    specs = [
        pl.BlockSpec((lefts[n].shape[0], 4 * rows), tile(p))
        for p, (start, stop) in enumerate(spans)
        for n in range(start, stop)
    ]
    depth = sum(x.shape[0] for x in lefts)
    shape = jax.ShapeDtypeStruct((4, rows, len(products) * wide), bf16)
    return pl.pallas_call(
        kernel,
        grid_spec=pltpu.PrefetchScalarGridSpec(
            num_scalar_prefetch=1,
            grid=(2 * len(products),),
            in_specs=specs + [pl.BlockSpec(memory_space=pl.ANY)] * count,
            out_specs=[pl.BlockSpec((2, rows, wide), lambda i, s: ((s[0] >> 2) ^ (i % 2), 0, i // 2))] * 2,
            scratch_shapes=[pltpu.VMEM(x.shape, bf16) for x in rights] + [pltpu.SemaphoreType.DMA((count,))],
        ),
        out_shape=[shape] * 2,
        compiler_params=params(56),
        cost_estimate=cost(16 * depth * rows * wide, 2 * depth * (8 * rows + wide)),
        name="shard_grads",
    )(low, *lefts, *rights)


def pack_shards(ones, twos, up, down):
    rows, cols = ones[0].shape
    flat = [*ones, *twos, up, down]
    part = up.shape[1] // 8

    def kernel(*refs):
        one_refs, two_refs = refs[: len(ones)], refs[len(ones) : len(ones) + len(twos)]
        up_ref, down_ref, out_one, out_two, out_lift = refs[len(flat) - 2 :]
        for i, ref in enumerate(one_refs):
            out_one[:, i * cols : (i + 1) * cols] = ref[...]
        for i, ref in enumerate(two_refs):
            x = ref[...].T if i in (0, len(twos) - 1) else ref[...]
            out_two[:, i * cols : (i + 1) * cols] = x
        for d in range(8):
            span = slice(d * part, (d + 1) * part)
            out_lift[d, 0] = up_ref[:, span]
            out_lift[d, 1] = down_ref[span, :].T

    return pl.pallas_call(
        kernel,
        out_shape=[
            jax.ShapeDtypeStruct((rows, len(ones) * cols), bf16),
            jax.ShapeDtypeStruct((rows, len(twos) * cols), bf16),
            jax.ShapeDtypeStruct((8, 2, rows, part), bf16),
        ],
        compiler_params=params(56),
        cost_estimate=cost(0, 4 * sum(x.size for x in flat)),
        name="pack_shards",
    )(*flat)


def sum_columns(place, pieces, count, size):
    rows, wide = pieces[0].shape
    cols = wide // count
    part = cols // size

    def kernel(place_ref, *refs):
        ins, outs, total = refs[: len(pieces)], refs[len(pieces) : -1], refs[-1]
        acc = ins[0][...].astype(f32)
        for ref in ins[1:]:
            acc = acc + ref[...].astype(f32)
        total[...] = acc
        for r in range(size):
            start = lax.rem(place_ref[0] + size - r, size) * part
            for w in range(count):
                span = pl.ds(pl.multiple_of(w * cols + start, part), part)
                outs[r][:, w * part : (w + 1) * part] = total[:, span].astype(outs[r].dtype)

    return pl.pallas_call(
        kernel,
        grid_spec=pltpu.PrefetchScalarGridSpec(
            num_scalar_prefetch=1,
            grid=(1,),
            in_specs=[pl.BlockSpec(x.shape, lambda i, s: (0, 0)) for x in pieces],
            out_specs=[pl.BlockSpec((rows, count * part), lambda i, s: (0, 0))] * size,
            scratch_shapes=[pltpu.VMEM((rows, wide), f32)],
        ),
        out_shape=[jax.ShapeDtypeStruct((rows, count * part), f32 if r == 0 else bf16) for r in range(size)],
        compiler_params=params(56),
        cost_estimate=cost(0, 4 * sum(x.size for x in pieces)),
        name="sum_columns",
    )(place, *pieces)


def row_sums(x):
    return jnp.mean(x, axis=-1, keepdims=True)


def norm_backward(rows, gain, pieces, residual, sums, tile=256):
    count, width = rows.shape

    def kernel(rows_ref, gain_ref, residual_ref, *refs):
        grads, outs = refs[: len(pieces)], refs[len(pieces) :]
        x = rows_ref[...].astype(f32)
        centered = x - row_sums(x)
        scale = lax.rsqrt(row_sums(centered * centered) + EPSILON)
        xhat = centered * scale
        grad = grads[0][...].astype(f32)
        for g in grads[1:]:
            grad = grad + g[...].astype(f32)
        scaled = grad * gain_ref[...]
        back = scale * (scaled - row_sums(scaled) - xhat * row_sums(scaled * xhat))
        out = residual_ref[...].astype(f32) + back
        outs[0][...] = out
        if sums:
            short = out.astype(bf16)
            outs[1][...] = short

            @pl.when(pl.program_id(0) == 0)
            def _():
                outs[2][...] = jnp.zeros_like(outs[2])

            for n, v in enumerate((grad * xhat, grad, short.astype(f32))):
                outs[2][n : n + 1, :] += jnp.sum(v, axis=0, keepdims=True)

    row = pl.BlockSpec((tile, width), lambda i: (i, 0))
    shape = jax.ShapeDtypeStruct((count, width), f32)
    return pl.pallas_call(
        kernel,
        grid=(count // tile,),
        in_specs=[row, pl.BlockSpec((1, width), lambda i: (0, 0)), row] + [row] * len(pieces),
        out_specs=[row, row, pl.BlockSpec((3, width), lambda i: (0, 0))] if sums else [row],
        out_shape=[
            shape,
            jax.ShapeDtypeStruct((count, width), bf16),
            jax.ShapeDtypeStruct((3, width), f32),
        ]
        if sums
        else [shape],
        compiler_params=params(56),
        cost_estimate=cost(0, 12 * rows.size),
        name="norm_backward",
    )(rows, gain[None], residual, *pieces)


def share_grad(grads, weights, rows, before, final):
    count, width = rows.shape
    tile = count
    given = 0 if before is None else 1

    def kernel(*refs):
        g_refs, w_refs = refs[: len(grads)], refs[len(grads) : 2 * len(grads)]
        rows_ref, rest = refs[2 * len(grads)], refs[2 * len(grads) + 1 :]
        out_ref, sums_ref = rest[given:]
        share = dot(g_refs[0][...], w_refs[0][...], 1, 1)
        for g, w in zip(g_refs[1:], w_refs[1:]):
            share = share + dot(g[...], w[...], 1, 1)
        x = rows_ref[...].astype(f32)
        centered = x - row_sums(x)
        xhat = centered * lax.rsqrt(row_sums(centered * centered) + EPSILON)

        sums_ref[0:1, :] = jnp.sum(share * xhat, axis=0, keepdims=True)
        sums_ref[1:2, :] = jnp.sum(share, axis=0, keepdims=True)
        if given:
            share = share + rest[0][...].astype(f32)
        out_ref[...] = share.astype(out_ref.dtype)

    row = pl.BlockSpec((tile, width), lambda i: (i, 0))
    return pl.pallas_call(
        kernel,
        grid=(1,),
        in_specs=[row] * len(grads)
        + [pl.BlockSpec(w.shape, lambda i: (0, 0)) for w in weights]
        + [row] * (1 + given),
        out_specs=[row, pl.BlockSpec((2, width), lambda i: (0, 0))],
        out_shape=[
            jax.ShapeDtypeStruct((count, width), f32 if final else bf16),
            jax.ShapeDtypeStruct((2, width), f32),
        ],
        compiler_params=params(56),
        cost_estimate=cost(2 * len(grads) * count * width * width, 6 * rows.size),
        name="share_grad",
    )(*grads, *weights, rows, *([before] if given else []))


def normed(rows, gain, shift):
    average = jnp.mean(rows, axis=-1, keepdims=True)
    centered = rows - average
    variance = jnp.mean(centered * centered, axis=-1, keepdims=True)
    return (centered * lax.rsqrt(variance + EPSILON) * gain + shift).astype(bf16)


def centered_rows(rows):
    average = jnp.mean(rows, axis=-1, keepdims=True)
    centered = rows - average
    scale = lax.rsqrt(jnp.mean(centered * centered, axis=-1, keepdims=True) + EPSILON)
    return centered * scale, scale


def norm_back(rows, gain, grad):
    xhat, scale = centered_rows(rows)
    scaled = grad * gain
    return scale * (
        scaled
        - jnp.mean(scaled, axis=-1, keepdims=True)
        - xhat * jnp.mean(scaled * xhat, axis=-1, keepdims=True)
    )


def norm_sums(rows, grad):
    return jnp.sum(grad * centered_rows(rows)[0], axis=0), jnp.sum(grad, axis=0)


def column_sums(matrix):
    return jnp.sum(matrix.astype(f32), axis=0)


def together(*values):
    return lax.optimization_barrier(values)


def flip(x, k):
    return lax.ppermute(x, "low", [(i, i ^ k) for i in range(8)])


def wrap(value, size):
    return value % size if isinstance(value, int) else lax.rem(value, size)


def turn(x, r, size):
    return lax.ppermute(x, "tensor", [(i, (i + r) % size) for i in range(size)])


def gather_chips(x):
    return [x] + [flip(x, k) for k in (2, 4, 6)]


def gather_cores(even):
    return [p for e in even for p in (e, flip(e, 1))]


def by_place(pieces, place):
    size = len(pieces)
    return jnp.stack(
        [
            sum(jnp.where(lax.rem(place + size - r, size) == z, pieces[r], 0.0) for r in range(size))
            for z in range(size)
        ]
    )


def stack_shards(scalars, pieces):
    (stacked,) = move(
        "stack_shards", scalars, pieces, [(len(pieces), *pieces[0].shape)],
        lambda s: [(r, (slice(None), slice(None)), 0, (r,)) for r in range(len(pieces))],
    )
    return stacked


def unpack_weights(scalars, pieces, count, sizes):
    size, rows, cols = pieces[0].shape
    cols //= count
    every = slice(None)

    def plan(s):
        return [
            (
                k, (r, every, pl.ds(w * cols, cols)),
                w, (at((s[0] ^ k) * rows, rows), at(wrap(s[1] + size - r, size) * cols, cols)),
            )
            for w in range(count) for k in range(8) for r in range(size)
        ]

    matrices = move("unpack_weights", scalars, pieces, [(8 * rows, size * cols)] * count, plan)
    if sizes[0] > 1:
        matrices = [lax.all_gather(m, "high", axis=0, tiled=True) for m in matrices]
    return matrices


def add_pair(a, b):
    return (a.astype(f32) + b.astype(f32)).astype(bf16)


def scatter_low(pieces):
    even = [add_pair(pieces[k], flip(pieces[k + 1], 1)) for k in (6, 4, 2)]
    back = [flip(e, k).astype(f32) for e, k in zip(even, (6, 4, 2))]
    own = pieces[0].astype(f32) + flip(pieces[1], 1).astype(f32)
    return own + back[0] + back[1] + back[2]


def whole_shards(parts, turned, count):
    shard = parts[0] + sum(x.astype(f32) for x in turned)
    return jnp.split(shard, count, axis=1)


def sum_tensor(vector, sizes):
    if sizes[0] > 1:
        vector = lax.psum(vector, "high")
    return vector + sum(turn(vector, r, sizes[2]) for r in range(1, sizes[2]))


def sum_low(vector):
    spread = jnp.broadcast_to(vector, (8, *vector.shape))
    return jnp.sum(lax.all_to_all(spread, "low", split_axis=0, concat_axis=0, tiled=True), axis=0)


def path_bias(parents, place, own, blocks):
    count = parents.shape[0]
    labels = jnp.arange(count)
    table = (
        (labels[:, None] == labels[None, :])
        | ((parents[:, None] == labels[None, :]) & (labels[:, None] > 0))
    ).astype(f32)
    reach = 1
    while reach < count:
        table = jnp.minimum(jnp.dot(table, table), 1.0)
        reach *= 2
    slots = jnp.arange(blocks * own)
    segment = (place - slots // own) * own + slots % own
    pick = (labels[:, None] == segment[None, :]).astype(f32)
    lanes = jnp.arange(2 * own * SEG)
    query = place * own + (lanes // SEG) % own
    mine = (labels[:, None] == query[None, :]).astype(f32)
    seen = jnp.dot(pick.T, jnp.dot(table.T, mine))
    return jnp.where(seen > 0.5, 0.0, NEG)


def on_device(sizes, sure):
    size = sizes[2]

    def run(
        tokens,
        encoded,
        parents,
        source_lengths,
        cotangent,
        first_gain,
        first_shift,
        self_query,
        self_query_bias,
        self_key,
        self_value,
        self_value_bias,
        self_out,
        self_out_bias,
        second_gain,
        second_shift,
        cross_query,
        cross_query_bias,
        cross_key,
        cross_value,
        cross_value_bias,
        cross_out,
        cross_out_bias,
        third_gain,
        third_shift,
        up_weight,
        up_bias,
        down_weight,
        down_bias,
    ):
        low = lax.axis_index("low")
        place = lax.axis_index("tensor")
        scalars = jnp.stack([low, place]).astype(jnp.int32)
        low_1, place_1 = scalars[:1], scalars[1:]
        rows, width = tokens.shape
        up_chain = [(i, i + 1) for i in range(size - 1)]
        down_chain = [(i + 1, i) for i in range(size - 1)]

        first, second, lift = pack_shards(
            [self_query, self_key, self_value],
            [self_out, cross_query, cross_key, cross_value, cross_out],
            up_weight, down_weight,
        )
        part = width // size
        hidden = up_weight.shape[1] // 8
        z = [turn(first, r, size) for r in range(1, size)]
        ones = [normed(tokens.astype(f32), first_gain, first_shift)]
        bias = path_bias(parents[0], place, rows // SEG, size)
        lift = lax.all_to_all(lift, "low", split_axis=0, concat_axis=0, tiled=True)
        if sizes[0] > 1:
            lift = lax.all_gather(lift, "high", axis=0, tiled=True)
        first, second, z, ones, bias, tokens_sent = together(first, second, z, ones, bias, tokens)

        even_a = gather_chips(stack_shards(scalars, [first, *z]))
        blocks = [tokens, lax.ppermute(tokens_sent, "tensor", up_chain)]
        z = [turn(second, 1, size)]
        biases = jnp.concatenate(
            [
                self_query_bias, self_value_bias, cross_query_bias, cross_value_bias,
                lax.dynamic_slice_in_dim(up_bias, low * hidden, hidden, 0),
            ]
        )
        biases = [biases] + [turn(biases, r, size) for r in range(1, size)]
        ub = jnp.concatenate([x[4 * part :] for x in biases])[None]
        placed = by_place([x[: 4 * part] for x in biases], place).reshape(size, 4, part)
        q_bias, v_bias, xq_bias, xv_bias = [placed[:, i].reshape(width) for i in range(4)]
        even_a, second, z[0], blocks, ub, q_bias, v_bias, xq_bias, xv_bias, encoded, lift = together(
            even_a, second, z[0], blocks, ub, q_bias, v_bias, xq_bias, xv_bias, encoded, lift
        )

        all_a = gather_cores(even_a)
        blocks.append(lax.ppermute(blocks[-1], "tensor", up_chain))
        source = lax.all_gather(encoded, "tensor", axis=0, tiled=True)
        z = z + [turn(second, r, size) for r in range(2, size)]
        wq, wk, wv = unpack_weights(scalars, all_a, 3, sizes)
        q1 = (dot(ones[0], wq) + q_bias).astype(bf16)
        ks, vs, state, mixed_one = [], [], None, None
        for r in range(size):
            if r:
                ones.append(normed(blocks[r].astype(f32), first_gain, first_shift))
            ks.append(dot(ones[r], wk).astype(bf16))
            vs.append((dot(ones[r], wv) + v_bias).astype(bf16))
            if r == 0:
                continue
            if r == 1:
                q1, ks, vs, second, z = together(q1, ks, vs, second, z)
                packed_b = stack_shards(scalars, [second, *z])
                even_b = [packed_b, flip(packed_b, 2), flip(packed_b, 4)]
            seen = (0, 1) if r == 1 else (r,)
            if r < size - 1:
                state = self_forward(place_1, q1, ks, vs, bias, seen, state, False)
            else:
                mixed_one, lse_one = self_forward(place_1, q1, ks, vs, bias, seen, state, True)
            if r == 1:
                state, blocks, even_b = together(state, blocks, even_b)
                even_b.append(flip(even_b[0], 6))
                blocks.append(lax.ppermute(blocks[-1], "tensor", up_chain))
            elif r < size - 1:
                if r < size - 2:
                    blocks.append(lax.ppermute(blocks[-1], "tensor", up_chain))
                state, blocks, even_b, cots_sent, lift = together(
                    state, blocks, even_b, cotangent, lift
                )
                cots = lax.all_gather(cots_sent, "low", axis=0, tiled=True)
                all_b = gather_cores(even_b)
                lifts = [lift, turn(lift, 1, size)]
        mixed_one, all_b, lifts = together(mixed_one, all_b, lifts)
        lifts = lifts + [turn(lifts[-1], 1, size)]

        wo, xq, xk, xv, xo = unpack_weights(scalars, all_b, 5, sizes)
        hidden_one = tokens.astype(f32) + dot(mixed_one, wo, 1, 1) + self_out_bias
        two = normed(hidden_one, second_gain, second_shift)
        q2 = (dot(two, xq) + xq_bias).astype(bf16)
        k2 = dot(source, xk).astype(bf16)
        v2 = (dot(source, xv) + xv_bias).astype(bf16)
        q2, k2, v2, lifts = together(q2, k2, v2, lifts)

        lifts = lifts + [turn(lifts[-1], 1, size)]
        mixed_two, lse_two = cross_forward(source_lengths, q2, k2, v2, sure)
        hidden_two = hidden_one + dot(mixed_two, xo, 1, 1) + cross_out_bias
        three = normed(hidden_two, third_gain, third_shift)
        three, lifts = together(three, lifts)

        x2, x4, c0 = flip(three, 2), flip(three, 4), flip(three, 1)

        def lift_pair(pair, r0, r1, outs):
            return feed_forward(low_1, pair, r0, r1, cots, lifts, ub, outs)

        outs, own, got, inner_0, grad_0, sums_0 = lift_pair((0, 1), three, c0, None)
        own_got = flip(got, 1)
        three_sent, x2, x4, own = together(three, x2, x4, own)
        c2, c4, x6 = flip(x2, 1), flip(x4, 1), flip(three_sent, 6)
        outs, back_2, back_4, inner_1, grad_1, sums_1 = lift_pair((2, 4), x2, x4, outs)
        c2, c4, back_2, own_got = together(c2, c4, back_2, own_got)
        outs, got_2, got_4, inner_2, grad_2, sums_2 = lift_pair((3, 5), c2, c4, outs)
        x6, got_2 = together(x6, got_2)
        got_2, got_4, c6 = flip(got_2, 1), flip(got_4, 1), flip(x6, 1)
        outs, back_6, got_6, inner_3, grad_3, sums_3 = lift_pair((6, 7), x6, c6, outs)
        back_6, got_2, got_4 = together(back_6, got_2, got_4)
        back_2, back_4 = flip(add_pair(back_2, got_2), 2), flip(add_pair(back_4, got_4), 4)
        got_6 = flip(got_6, 1)
        order = (0, 1, 2, 4, 3, 5, 6, 7)
        lift_shares = lift_grad(
            low_1, [grad_0, grad_1, grad_2, grad_3], [three, c0, x2, x4, c2, c4, x6, c6], order, 0, None
        )
        back_6, got_6, back_2, back_4, lift_shares = together(
            back_6, got_6, back_2, back_4, lift_shares
        )
        back_6 = flip(add_pair(back_6, got_6), 6)
        lift_shares = lift_grad(
            low_1, [inner_0, inner_1, inner_2, inner_3], cots, order, 1, lift_shares
        )
        up_sums = [sums_0, sums_1, sums_2, sums_3]
        lift_shares, back_6 = together(lift_shares, back_6)
        grad_hidden_two, grad_two, sums_three = norm_backward(
            hidden_two, third_gain, [own, own_got, back_2, back_4, back_6], cotangent, True
        )
        do2 = dot(grad_two, xo).astype(bf16)
        do2, outs, lift_shares = together(do2, outs, lift_shares)

        out_sum = lax.psum_scatter(outs, "low", scatter_dimension=0, tiled=True)
        lift_got = turn(lift_shares[size - 1], size - 1, size)
        dq2, dk2, dv2 = cross_backward(source_lengths, q2, k2, v2, mixed_two, do2, lse_two, sure)
        dq2, dk2, dv2, lift_got = together(dq2, dk2, dv2, lift_got)

        lift_got = turn(add_pair(lift_shares[size - 2], lift_got), size - 1, size)
        grad_hidden_one, grad_one, sums_two = norm_backward(
            hidden_one, second_gain, [dot(dq2, xq, 1, 1)], grad_hidden_two, True
        )
        do1 = dot(grad_one, wo).astype(bf16)
        encoded_part = (dot(dk2, xk, 1, 1) + dot(dv2, xv, 1, 1)).astype(bf16)
        early = column_sums(cotangent), column_sums(dq2), column_sums(dv2)
        do1, lift_got, encoded_part, early = together(do1, lift_got, encoded_part, early)

        lift_got = turn(add_pair(lift_shares[size - 3], lift_got), size - 1, size)
        b_laid = shard_grads(
            low_1,
            [
                ([grad_one], [mixed_one]),
                ([two], [dq2]),
                ([source], [dk2]),
                ([source], [dv2]),
                ([grad_two], [mixed_two]),
            ],
        )
        spread = by_place([sum(up_sums)[0, r * hidden : (r + 1) * hidden] for r in range(size)], place)
        spread = lax.dynamic_update_slice(
            jnp.zeros((size, up_bias.shape[0]), f32), spread, (0, low * hidden)
        )
        whole_sums = [sums_two.reshape(-1), sums_three.reshape(-1), early[0]]
        place_sums = [spread, early[1].reshape(size, part), early[2].reshape(size, part)]
        (b_even, b_odd), do1, lift_got, encoded_part, whole_sums, place_sums = together(
            b_laid, do1, lift_got, encoded_part, whole_sums, place_sums
        )

        if sizes[0] > 1:
            b_even, b_odd = [
                lax.psum_scatter(x, "high", scatter_dimension=1, tiled=True) for x in (b_even, b_odd)
            ]
        b_got = flip(b_odd, 1)
        lift_sums = add_pair(lift_shares[0], lift_got)
        if sizes[0] > 1:
            lift_sums = lax.psum_scatter(lift_sums, "high", scatter_dimension=2, tiled=True)
        lift_sums = lax.all_to_all(lift_sums, "low", split_axis=2, concat_axis=1, tiled=True)
        encoded_sum = lax.psum_scatter(encoded_part, "tensor", scatter_dimension=0, tiled=True)
        dks, dvs, own_sums = [None] * size, [None] * size, []
        far = tuple(range(size - 1, 1, -1))
        dq, dk, dv = self_backward(place_1, q1, ks, vs, mixed_one, do1, lse_one, bias, far, None)
        for n, r in enumerate(far):
            dks[r], dvs[r] = dk[n], dv[n]
        share, sums = share_grad([dks[far[0]], dvs[far[0]]], [wk, wv], blocks[far[0]], None, False)
        own_sums.append(sums)
        share, dq, b_even, b_got, out_sum, lift_sums = together(
            share, dq, b_even, b_got, out_sum, lift_sums
        )
        share = lax.ppermute(share, "tensor", down_chain)
        b_sums = [add_pair(b_even[p], b_got[p]) for p in range(4)]
        b_sums, dq = together(b_sums, dq)
        b_back = [flip(b_sums[p], 2 * p) for p in (1, 2, 3)]
        dq, dk, dv = self_backward(place_1, q1, ks, vs, mixed_one, do1, lse_one, bias, (1, 0), dq)
        dks[1], dvs[1], dks[0], dvs[0] = dk[0], dv[0], dk[1], dv[1]
        for r in far[1:]:
            share, sums = share_grad([dks[r], dvs[r]], [wk, wv], blocks[r], share, False)
            own_sums.append(sums)
            share, dq, dks, dvs, encoded_sum = together(share, dq, dks, dvs, encoded_sum)
            share = lax.ppermute(share, "tensor", down_chain)
        a_even, a_odd = shard_grads(low_1, [([ones[0]], [dq]), (ones, dks), (ones, dvs)])
        if sizes[0] > 1:
            a_even, a_odd = [
                lax.psum_scatter(x, "high", scatter_dimension=1, tiled=True) for x in (a_even, a_odd)
            ]
        a_even, a_odd, share, dq, dks, dvs, b_back = together(
            a_even, a_odd, share, dq, dks, dvs, b_back
        )

        a_got = flip(a_odd, 1)
        share, sums = share_grad([dks[1], dvs[1]], [wk, wv], blocks[1], share, False)
        own_sums.append(sums)
        a_even, a_got, share = together(a_even, a_got, share)
        share = lax.ppermute(share, "tensor", down_chain)
        a_sums = [add_pair(a_even[p], a_got[p]) for p in range(4)]
        a_sums, b_sums, b_back, dq, dks, dvs = together(a_sums, b_sums, b_back, dq, dks, dvs)
        a_back = [flip(a_sums[p], 2 * p) for p in (1, 2, 3)]
        b_parts = sum_columns(place_1, [b_sums[0], *b_back], 5, size)
        b_turned = [turn(b_parts[1], size - 1, size)]
        own_share, sums = share_grad([dks[0], dvs[0], dq], [wk, wv, wq], tokens, None, True)
        own_sums.append(sums)
        share, b_parts = together(share, b_parts)
        b_turned += [turn(b_parts[r], size - r, size) for r in range(2, size)]
        whole_sums = jnp.concatenate([*whole_sums, sum(own_sums).reshape(-1)])
        place_sums += [
            column_sums(dq).reshape(size, part),
            sum(column_sums(v) for v in dvs).reshape(size, part),
        ]
        vectors = jnp.concatenate([whole_sums, jnp.concatenate(place_sums, axis=1).reshape(-1)])
        a_back, vectors, out_sum, lift_sums, share, own_share = together(
            a_back, vectors, out_sum, lift_sums, share, own_share
        )
        vectors = sum_tensor(vectors, sizes)
        a_parts = sum_columns(place_1, [a_sums[0], *a_back], 3, size)
        a_turned = [turn(a_parts[r], size - r, size) for r in range(1, size)]
        vectors, a_parts, share = together(vectors, a_parts, share)
        vectors = sum_low(vectors)
        (tokens_grad,) = norm_backward(tokens, first_gain, [own_share, share], grad_hidden_one, False)
        small = [vectors[i * width : (i + 1) * width] for i in range(9)]
        small = [small[i] for i in (7, 8, 0, 1, 3, 4, 2, 5, 6)]
        mine = lax.dynamic_index_in_dim(vectors[9 * width :].reshape(size, -1), place, 0, keepdims=False)
        up_bias_grad, mine = mine[: up_bias.shape[0]], mine[up_bias.shape[0] :]
        split = [mine[i * part : (i + 1) * part] for i in (2, 3, 0, 1)]
        encoded_grad = encoded_sum.astype(f32)
        wo_g, xq_g, xk_g, xv_g, xo_g = whole_shards(b_parts, b_turned, 5)
        wq_g, wk_g, wv_g = whole_shards(a_parts, a_turned, 3)
        block_out = hidden_two + out_sum.astype(f32) + down_bias
        up_weight_grad = lift_sums[0].T.astype(f32)
        down_weight_grad = lift_sums[1].astype(f32)

        return (
            block_out.astype(bf16),
            tokens_grad,
            encoded_grad,
            small[0],
            small[1],
            wq_g,
            split[0],
            wk_g,
            wv_g,
            split[1],
            wo_g.T,
            small[6],
            small[2],
            small[3],
            xq_g,
            split[2],
            xk_g,
            xv_g,
            split[3],
            xo_g.T,
            small[7],
            small[4],
            small[5],
            up_weight_grad,
            up_bias_grad,
            down_weight_grad,
            small[8],
        )

    return run


def solution(mesh):
    dp, size = mesh.shape["dp"], mesh.shape["tensor"]
    sizes = (dp // 8, 8, size)
    fine = Mesh(mesh.devices.reshape(sizes), ("high", "low", "tensor"))
    depth = ("high", "low")
    rows = P((*depth, "tensor"), None)
    block, turned = P(depth, "tensor"), P("tensor", depth)
    part, whole = P("tensor"), P()
    placed = (
        rows, rows, P(depth, None), P(depth), rows, whole, whole,
        block, part, block, block, part, turned, whole, whole, whole,
        block, part, block, block, part, turned, whole, whole, whole,
        block, part, turned, whole,
    )
    out = (
        rows, rows, rows, whole, whole,
        block, part, block, block, part, turned, whole, whole, whole,
        block, part, block, block, part, turned, whole, whole, whole,
        block, part, turned, whole,
    )
    return jax.shard_map(
        on_device(sizes, 768), mesh=fine, in_specs=placed, out_specs=out, check_vma=False
    )
```
